32 devices in a mesh: tm: 8 (over z, x), rows: 4 (over y, core).
Axes of the slice: x: 2, y: 2, z: 4, core: 2. Of those that a mesh axis runs over, the one named last changes fastest.
Arguments:
- observed: int32 [32], P('tm'), may hold values from 0 to 255
- pattern: int32 [16, 4], replicated, may hold values from 0 to 15, as said below
- trans_blocks: bfloat16 [16, 4, 64, 64], replicated, may hold values from 0.00077819824 to 0.0078125
- leave_rate: float32 [1024], replicated, may hold values from 0.0078125 to 0.03
- symbol_emit: float32 [256, 1024], replicated, may hold values from 0.25 to 4
- cluster_emit: float32 [16, 1024], replicated, may hold values from 0.25 to 4
- symbol_cluster: int32 [256], replicated, may hold values from 0 to 15
Outputs:
- prefix_rows: float32 [8, 1024, 1024], P('tm', 'rows')
- prefix_rate: float32 [8, 1024], P('tm', 'rows')
The draws below stay inside these ranges and needn't reach their ends.
Inputs may be any that keep to these rules, and one draw needn't show every extreme that they name: Each row of pattern names 4 different source blocks.
All inputs are finite; a program needn't handle non-finite values.
Results may differ from the reference program's by a relative error of at most 0.0037.
Values sent between devices are 32-bit elements; how exact they have to be, the bound alone decides.
No kernel may reach another device: no remote copies, remote signals or barrier semaphores. Data moves between devices by JAX's collectives and lax.ppermute only.
A program may use at most 64 MiB of HBM per device.

```python
import math
import jax
import jax.numpy as jnp
import numpy as np
from jax import lax

S = 1024
NB = 16
CL = 64
KB = 4
V = 256
STEPS = 4
LENGTH = 32
N_TM = 8


def draw_pattern(key, part):
    key = jax.random.fold_in(key, 7)
    row_keys = jax.random.split(key, NB)
    chosen = jax.vmap(lambda sub_key: jax.random.permutation(sub_key, NB)[:KB])(row_keys)
    return chosen.astype(jnp.int32)


def set_ends(drawn, rng, least, largest):
    longest = drawn.shape.index(max(drawn.shape))
    spots = []
    for shift in (0, 1):
        where = [jax.random.randint(jax.random.fold_in(rng, axis), (), 0, length) for axis, length in enumerate(drawn.shape)]
        where[longest] = (where[longest] + shift) % drawn.shape[longest]
        spots.append(tuple(where))
    return drawn.at[spots[0]].set(least).at[spots[1]].set(largest)


def cumulative_ranks(amount, skew):
    weights = [(1 << 20) // math.isqrt(standing ** skew) + 1 for standing in range(1, amount + 1)]
    scale = 1 + sum(weights) // (1 << 30)
    return np.cumsum(np.array([max(1, weight // scale) for weight in weights]))


def skewed_ids(own_key, shape, count, skew):
    listing = cumulative_ranks(count, skew)
    ticket = jax.random.randint(jax.random.fold_in(own_key, 1), shape, 0, int(listing[count - 1]))
    grade = jnp.searchsorted(jnp.asarray(listing, jnp.int32), ticket, side="right")
    return jax.random.permutation(jax.random.fold_in(own_key, 2), count)[grade].astype(jnp.int32)


def setup_inputs(seed: int = 0) -> dict:
    key_of = jax.random.split(jax.random.key(seed), 8)
    return {
        "observed": set_ends(skewed_ids(key_of[0], (LENGTH,), V, 2), jax.random.fold_in(key_of[0], 3), 0, V - 1).astype(jnp.int32),
        "pattern": draw_pattern(jax.random.fold_in(key_of[7], 71), 0),
        "trans_blocks": jnp.clip(jnp.exp(jax.random.uniform(key_of[2], (NB, KB, CL, CL), jnp.float32, math.log(0.00077819824), math.log(0.0078125))), 0.00077819824, 0.0078125).astype(jnp.bfloat16),
        "leave_rate": jnp.clip(jnp.exp(jax.random.uniform(key_of[3], (S,), jnp.float32, math.log(0.0078125), math.log(0.03))), 0.0078125, 0.03),
        "symbol_emit": jnp.clip(jnp.exp(jax.random.uniform(key_of[4], (V, S), jnp.float32, math.log(0.25), math.log(4.0))), 0.25, 4.0),
        "cluster_emit": jnp.clip(jnp.exp(jax.random.uniform(key_of[5], (NB, S), jnp.float32, math.log(0.25), math.log(4.0))), 0.25, 4.0),
        "symbol_cluster": set_ends(jax.random.randint(key_of[6], (V,), 0, NB), jax.random.fold_in(key_of[6], 1), 0, NB - 1).astype(jnp.int32),
    }


def normalize(product, base_log):
    row_sum = jnp.sum(product, axis=1)
    n_cols = product.shape[1]
    return product * (n_cols / row_sum)[:, None], base_log + jnp.log(row_sum / n_cols)


def combine(left_r, left_l, right_r, right_l):
    top_log = jnp.max(right_l)
    scaled = left_r * jnp.exp(right_l - top_log)[None, :]
    product = jnp.dot(scaled, right_r, precision=lax.Precision.HIGHEST, preferred_element_type=jnp.float32)
    return normalize(product, left_l + top_log)


def reference(observed, pattern, trans_blocks, leave_rate, symbol_emit, cluster_emit, symbol_cluster):
    emission = symbol_emit[observed] * cluster_emit[symbol_cluster[observed]]
    src_leave = leave_rate.reshape(NB, CL)[pattern]
    moved_blocks = (trans_blocks.astype(jnp.float32) * src_leave[..., None]).astype(jnp.bfloat16)
    moved_flat = moved_blocks.reshape(NB, KB * CL, CL).astype(jnp.float32)
    stay_rate = 1.0 - leave_rate
    eye_bf = jnp.eye(S, dtype=jnp.float32).astype(jnp.bfloat16)

    def advance(carried, emission_row):
        current, log_scale = carried
        kept_part = current.astype(jnp.float32) * stay_rate[None, :]
        kept_part = jnp.roll(kept_part.reshape(S, NB, CL), 1, axis=2)
        picked = current.reshape(S, NB, CL)[:, pattern, :].reshape(S, NB, KB * CL).astype(jnp.float32)
        moved_part = jnp.einsum("rjc,jcd->rjd", picked, moved_flat)
        product = (kept_part + moved_part).reshape(S, S) * emission_row[None, :]
        new_r, new_l = normalize(product, log_scale)
        return (new_r.astype(jnp.bfloat16), new_l), None

    def segment(emission_block):
        start_value = (eye_bf, jnp.zeros((S,), jnp.float32))
        (seg_r, seg_l), _ = lax.scan(advance, start_value, emission_block)
        return seg_r, seg_l

    seg_rows, seg_logs = lax.map(segment, emission.reshape(N_TM, STEPS, S))

    def chain_step(carried, pair):
        prev_r, prev_l = carried
        seg_r, seg_l = pair
        new_r, new_l = combine(prev_r, prev_l, seg_r.astype(jnp.float32), seg_l)
        return (new_r, new_l), (new_r, new_l)

    start_pair = (jnp.eye(S, dtype=jnp.float32), jnp.zeros((S,), jnp.float32))
    _, (prefix_rows, prefix_logs) = lax.scan(chain_step, start_pair, (seg_rows, seg_logs))
    divisor = (STEPS * (jnp.arange(N_TM) + 1)).astype(jnp.float32)
    prefix_rate = prefix_logs / divisor[:, None]
    return prefix_rows, prefix_rate
```

```python
import functools

import jax
import jax.numpy as jnp
from jax import lax
from jax.experimental import pallas as pl
from jax.experimental.pallas import tpu as pltpu
from jax.sharding import PartitionSpec as P

LANES = 128
WIDTH = 256


def build_kernel(pattern_ref, blocks_ref, leave_ref, dense_ref, leave_col_ref):
    n_blocks, n_source, size, _ = blocks_ref.shape
    n_states = leave_ref.shape[1]
    leave_col_ref[...] = jnp.broadcast_to(leave_ref[...], (LANES, n_states)).T
    dense_ref[...] = jnp.zeros_like(dense_ref)
    per_tile = LANES // size
    lane = lax.broadcasted_iota(jnp.int32, (size, LANES), 1)
    sub = lax.broadcasted_iota(jnp.int32, (size, LANES), 0)
    for j in range(n_blocks):
        place = (lane == sub + size * (j % per_tile)).astype(jnp.bfloat16)
        tile = pl.ds(LANES * (j // per_tile), LANES)
        for k in range(n_source):
            rows = pl.ds(pl.multiple_of(pattern_ref[j, k] * size, size), size)
            block = jnp.dot(blocks_ref[j, k], place, preferred_element_type=jnp.float32)
            moved = (block * leave_col_ref[rows, :]).astype(jnp.bfloat16)
            dense_ref[rows, tile] = dense_ref[rows, tile] + moved


def shifted(x, size):
    lane = lax.broadcasted_iota(jnp.int32, x.shape, 1)
    return jnp.where(lane % size == 0, pltpu.roll(x, LANES - size + 1, 1), pltpu.roll(x, 1, 1))


def chain_kernel(
    steps,
    size,
    place_ref,
    observed_ref,
    cluster_ref,
    symbol_ref,
    cluster_emit_ref,
    leave_ref,
    dense_ref,
    rows_ref,
    rate_ref,
    cur_ref,
    low_ref,
    log_ref,
):
    n_rows, n_states = cur_ref.shape
    n_segments = place_ref[0]
    row_start = place_ref[1]
    row = lax.broadcasted_iota(jnp.int32, (n_rows, n_states), 0) + row_start
    col = lax.broadcasted_iota(jnp.int32, (n_rows, n_states), 1)
    start = (row == col).astype(jnp.float32)
    cur_ref[...] = start
    low_ref[0] = start.astype(jnp.bfloat16)
    log_ref[...] = jnp.zeros_like(log_ref)

    def segment(g, _):
        for s in range(steps):
            now, later = s % 2, (s + 1) % 2
            symbol = observed_ref[g * steps + s]
            emission = symbol_ref[pl.ds(symbol, 1), :]
            emission = emission * cluster_emit_ref[pl.ds(cluster_ref[symbol], 1), :]
            low = low_ref[now]
            total = None
            for n in range(n_states // WIDTH):
                cols = pl.ds(n * WIDTH, WIDTH)
                moved = jnp.dot(low, dense_ref[:, cols], preferred_element_type=jnp.float32)
                for h in range(WIDTH // LANES):
                    at = n * WIDTH + h * LANES
                    part = pl.ds(at, LANES)
                    kept = cur_ref[:, part] * (1.0 - leave_ref[:, part])
                    new = shifted(kept, size) + moved[:, h * LANES : (h + 1) * LANES]
                    new = new * emission[:, at : at + LANES]
                    cur_ref[:, part] = new
                    if s < steps - 1:
                        low_ref[later, :, part] = new.astype(jnp.bfloat16)
                    else:
                        total = new if total is None else total + new
        row_sum = jnp.sum(total, axis=1, keepdims=True)
        scale = n_states / row_sum
        log_ref[...] = log_ref[...] + jnp.log(row_sum / n_states)
        for n in range(n_states // LANES):
            part = pl.ds(n * LANES, LANES)
            new = cur_ref[:, part] * scale
            cur_ref[:, part] = new
            low_ref[0, :, part] = new.astype(jnp.bfloat16)
        return 0

    lax.fori_loop(0, n_segments, segment, 0)
    rows_ref[0] = cur_ref[...]
    divisor = (n_segments * steps).astype(jnp.float32)
    rate_ref[...] = (log_ref[...] / divisor).T[0:1, :]


def body(observed, pattern, trans_blocks, leave_rate, symbol_emit, cluster_emit, symbol_cluster):
    size = trans_blocks.shape[-1]
    n_states = leave_rate.shape[0]
    steps = observed.shape[0]
    n_rows = n_states // lax.axis_size("rows")
    all_observed = lax.all_gather(observed, "tm", axis=0, tiled=True)
    leave_row = leave_rate.reshape(1, n_states)
    vmem = pl.BlockSpec(memory_space=pltpu.VMEM)
    smem = pl.BlockSpec(memory_space=pltpu.SMEM)
    dense = pl.pallas_call(
        build_kernel,
        out_shape=jax.ShapeDtypeStruct((n_states, n_states), jnp.bfloat16),
        in_specs=[smem, vmem, vmem],
        out_specs=vmem,
        scratch_shapes=[pltpu.VMEM((n_states, LANES), jnp.float32)],
        compiler_params=pltpu.CompilerParams(vmem_limit_bytes=32 << 20),
        cost_estimate=pl.CostEstimate(flops=1 << 30, bytes_accessed=4 << 20, transcendentals=0),
        name="build",
    )(pattern, trans_blocks, leave_row)
    place = jnp.stack([lax.axis_index("tm") + 1, lax.axis_index("rows") * n_rows]).astype(jnp.int32)
    return pl.pallas_call(
        functools.partial(chain_kernel, steps, size),
        out_shape=[
            jax.ShapeDtypeStruct((1, n_rows, n_states), jnp.float32),
            jax.ShapeDtypeStruct((1, n_rows), jnp.float32),
        ],
        in_specs=[smem, smem, smem, vmem, vmem, vmem, vmem],
        out_specs=[vmem, vmem],
        scratch_shapes=[
            pltpu.VMEM((n_rows, n_states), jnp.float32),
            pltpu.VMEM((2, n_rows, n_states), jnp.bfloat16),
            pltpu.VMEM((n_rows, LANES), jnp.float32),
        ],
        compiler_params=pltpu.CompilerParams(vmem_limit_bytes=32 << 20),
        cost_estimate=pl.CostEstimate(flops=1 << 34, bytes_accessed=4 << 20, transcendentals=0),
        name="chain",
    )(place, all_observed, symbol_cluster, symbol_emit, cluster_emit, leave_row, dense)


def solution(mesh):
    in_specs = (P("tm"), P(), P(), P(), P(), P(), P())
    out_specs = (P("tm", "rows", None), P("tm", "rows"))
    return jax.shard_map(body, mesh=mesh, in_specs=in_specs, out_specs=out_specs, check_vma=False)
```

```python
import functools

import jax
import jax.numpy as jnp
from jax import lax
from jax.experimental import pallas as pl
from jax.experimental.pallas import tpu as pltpu
from jax.sharding import PartitionSpec as P

LANES = 128
SUBLANES = 8


def column(row):
    return jnp.broadcast_to(row, (LANES, row.shape[1])).T


def build_kernel(pattern_ref, blocks_ref, leave_ref, weight_ref, stay_ref, leave_col_ref):
    n_blocks, n_source, size, _ = blocks_ref.shape
    n_states = leave_ref.shape[1]
    leave_col = column(leave_ref[...])
    leave_col_ref[...] = leave_col
    for j in range(n_blocks):
        own = leave_col[j * size : (j + 1) * size]
        stay_ref[j * size : (j + 1) * size, :] = 1.0 - pltpu.roll(own, 1, 0)
    for j in range(n_blocks):
        parts = []
        for k in range(n_source):
            rows = pl.ds(pl.multiple_of(pattern_ref[j, k] * size, size), size)
            parts.append(blocks_ref[j, k].astype(jnp.float32) * leave_col_ref[rows, :size])
        moved = jnp.concatenate(parts, axis=0)
        weight_ref[j] = moved.T.astype(jnp.bfloat16)


def chain_kernel(
    steps,
    size,
    place_ref,
    observed_ref,
    cluster_ref,
    pattern_ref,
    symbol_ref,
    cluster_emit_ref,
    weight_ref,
    stay_ref,
    rows_ref,
    rate_ref,
    cur_ref,
    low_ref,
    emit_ref,
    emit_col_ref,
):
    n_half, n_blocks, padded, _ = cur_ref.shape
    n_states = n_blocks * size
    n_rows = n_half * LANES
    n_source = pattern_ref.shape[1]
    first = padded - size
    n_segments = place_ref[0]
    row_start = place_ref[1]

    def store(now, j, h, new):
        cur_ref[h, j, first:, :] = new
        cur_ref[h, j, first - 1 : first, :] = new[size - 1 :, :]
        low_ref[now, j * size : (j + 1) * size, h * LANES : (h + 1) * LANES] = new.astype(jnp.bfloat16)

    state = lax.broadcasted_iota(jnp.int32, (size, LANES), 0)
    row = lax.broadcasted_iota(jnp.int32, (size, LANES), 1)
    for j in range(n_blocks):
        for h in range(n_half):
            start = state + j * size == row + (row_start + h * LANES)
            store(0, j, h, start.astype(jnp.float32))
    emit_ref[...] = jnp.zeros_like(emit_ref)

    def segment(g, carried):
        scale, log_scale = carried
        for s in range(steps):
            symbol = observed_ref[g * steps + s]
            emission = symbol_ref[pl.ds(symbol, 1), :]
            emission = emission * cluster_emit_ref[pl.ds(cluster_ref[symbol], 1), :]
            emit_ref[s : s + 1, :] = emission
        emit_col_ref[...] = emit_ref[...].T
        sums = [jnp.zeros((SUBLANES, LANES), jnp.float32) for _ in range(n_half)]
        for s in range(steps):
            turn = s if steps % 2 == 0 else g * steps + s
            now, later = turn % 2, (turn + 1) % 2
            for j in range(n_blocks):
                states = slice(j * size, (j + 1) * size)
                picked = [
                    low_ref[now, pl.ds(pl.multiple_of(pattern_ref[j, k] * size, size), size), :]
                    for k in range(n_source)
                ]
                moved = jnp.dot(
                    weight_ref[j],
                    jnp.concatenate(picked, axis=0),
                    preferred_element_type=jnp.float32,
                )
                emission = jnp.broadcast_to(emit_col_ref[states, s : s + 1], (size, LANES))
                stay = stay_ref[states, :]
                for h in range(n_half):
                    part = slice(h * LANES, (h + 1) * LANES)
                    kept = cur_ref[h, j, first - 1 : padded - 1, :] * stay
                    new = (kept + moved[:, part]) * emission
                    if s == 0:
                        new = new * scale[:, part]
                    store(later, j, h, new)
                    if s == steps - 1:
                        sums[h] = sums[h] + jnp.sum(new.reshape(-1, SUBLANES, LANES), axis=0)
        row_sum = jnp.concatenate([jnp.sum(t, axis=0, keepdims=True) for t in sums], axis=1)
        return 1.0 / row_sum, log_scale + jnp.log(row_sum)

    ones = jnp.ones((1, n_rows), jnp.float32)
    scale, log_scale = lax.fori_loop(0, n_segments, segment, (ones, jnp.zeros_like(ones)))
    scale = scale * n_states
    for j in range(n_blocks * size // LANES):
        per = LANES // size
        for h in range(n_half):
            part = slice(h * LANES, (h + 1) * LANES)
            block = [cur_ref[h, j * per + i, first:, :] for i in range(per)]
            block = jnp.concatenate(block, axis=0) * scale[:, part]
            rows_ref[0, part, j * LANES : (j + 1) * LANES] = block.T
    divisor = (n_segments * steps).astype(jnp.float32)
    rate_ref[...] = (log_scale - jnp.log(jnp.full_like(ones, n_states))) / divisor


def body(observed, pattern, trans_blocks, leave_rate, symbol_emit, cluster_emit, symbol_cluster):
    n_blocks, n_source, size, _ = trans_blocks.shape
    n_states = leave_rate.shape[0]
    steps = observed.shape[0]
    n_rows = n_states // lax.axis_size("rows")
    all_observed = lax.all_gather(observed, "tm", axis=0, tiled=True)
    leave_row = leave_rate.reshape(1, n_states)
    vmem = pl.BlockSpec(memory_space=pltpu.VMEM)
    smem = pl.BlockSpec(memory_space=pltpu.SMEM)
    weight, stay = pl.pallas_call(
        build_kernel,
        out_shape=[
            jax.ShapeDtypeStruct((n_blocks, size, n_source * size), jnp.bfloat16),
            jax.ShapeDtypeStruct((n_states, LANES), jnp.float32),
        ],
        in_specs=[smem, vmem, vmem],
        out_specs=[vmem, vmem],
        scratch_shapes=[pltpu.VMEM((n_states, LANES), jnp.float32)],
        compiler_params=pltpu.CompilerParams(vmem_limit_bytes=32 << 20),
        cost_estimate=pl.CostEstimate(flops=1 << 30, bytes_accessed=4 << 20, transcendentals=0),
        name="build",
    )(pattern, trans_blocks, leave_row)
    place = jnp.stack([lax.axis_index("tm") + 1, lax.axis_index("rows") * n_rows]).astype(jnp.int32)
    return pl.pallas_call(
        functools.partial(chain_kernel, steps, size),
        out_shape=[
            jax.ShapeDtypeStruct((1, n_rows, n_states), jnp.float32),
            jax.ShapeDtypeStruct((1, n_rows), jnp.float32),
        ],
        in_specs=[smem, smem, smem, smem, vmem, vmem, vmem, vmem],
        out_specs=[vmem, vmem],
        scratch_shapes=[
            pltpu.VMEM((n_rows // LANES, n_blocks, size + SUBLANES, LANES), jnp.float32),
            pltpu.VMEM((2, n_states, n_rows), jnp.bfloat16),
            pltpu.VMEM((LANES, n_states), jnp.float32),
            pltpu.VMEM((n_states, LANES), jnp.float32),
        ],
        compiler_params=pltpu.CompilerParams(vmem_limit_bytes=32 << 20),
        cost_estimate=pl.CostEstimate(flops=1 << 34, bytes_accessed=4 << 20, transcendentals=0),
        name="chain",
    )(place, all_observed, symbol_cluster, pattern, symbol_emit, cluster_emit, weight, stay)


def solution(mesh):
    in_specs = (P("tm"), P(), P(), P(), P(), P(), P())
    out_specs = (P("tm", "rows", None), P("tm", "rows"))
    return jax.shard_map(body, mesh=mesh, in_specs=in_specs, out_specs=out_specs, check_vma=False)
```

```python
import functools

import jax
import jax.numpy as jnp
from jax import lax
from jax.experimental import pallas as pl
from jax.experimental.pallas import tpu as pltpu
from jax.sharding import PartitionSpec as P

LANES = 128
SUBLANES = 8


def column(row):
    return jnp.broadcast_to(row, (LANES, row.shape[1])).T


def build_kernel(pattern_ref, blocks_ref, leave_ref, weight_ref, stay_ref, leave_col_ref):
    n_blocks, n_source, size, _ = blocks_ref.shape
    n_states = leave_ref.shape[1]
    leave_col = column(leave_ref[...])
    leave_col_ref[...] = leave_col
    for j in range(n_blocks):
        own = leave_col[j * size : (j + 1) * size]
        stay_ref[j * size : (j + 1) * size, :] = 1.0 - pltpu.roll(own, 1, 0)
    for j in range(n_blocks):
        parts = []
        for k in range(n_source):
            rows = pl.ds(pl.multiple_of(pattern_ref[j, k] * size, size), size)
            parts.append(blocks_ref[j, k].astype(jnp.float32) * leave_col_ref[rows, :size])
        moved = jnp.concatenate(parts, axis=0)
        weight_ref[j] = moved.T.astype(jnp.bfloat16)


def chain_kernel(
    steps,
    size,
    place_ref,
    observed_ref,
    cluster_ref,
    pattern_ref,
    symbol_ref,
    cluster_emit_ref,
    weight_ref,
    stay_ref,
    rows_ref,
    rate_ref,
    cur_ref,
    low_a_ref,
    low_b_ref,
    emit_ref,
    emit_col_ref,
):
    n_half, n_blocks, padded, _ = cur_ref.shape
    n_states = n_blocks * size
    n_rows = n_half * LANES
    n_source = pattern_ref.shape[1]
    first = padded - size
    n_segments = place_ref[0]
    row_start = place_ref[1]

    lows = (low_a_ref, low_b_ref)

    def store(low_ref, j, h, new):
        cur_ref[h, j, first:, :] = new
        cur_ref[h, j, first - 1 : first, :] = new[size - 1 :, :]
        low_ref[j * size : (j + 1) * size, h * LANES : (h + 1) * LANES] = new.astype(jnp.bfloat16)

    state = lax.broadcasted_iota(jnp.int32, (size, LANES), 0)
    row = lax.broadcasted_iota(jnp.int32, (size, LANES), 1)
    for j in range(n_blocks):
        for h in range(n_half):
            start = state + j * size == row + (row_start + h * LANES)
            store(low_a_ref, j, h, start.astype(jnp.float32))
    emit_ref[...] = jnp.zeros_like(emit_ref)

    def segment(g, carried):
        scale, log_scale = carried
        for s in range(steps):
            symbol = observed_ref[g * steps + s]
            emission = symbol_ref[pl.ds(symbol, 1), :]
            emission = emission * cluster_emit_ref[pl.ds(cluster_ref[symbol], 1), :]
            emit_ref[s : s + 1, :] = emission
        emit_col_ref[...] = emit_ref[...].T
        sums = [jnp.zeros((SUBLANES, LANES), jnp.float32) for _ in range(n_half)]
        for s in range(steps):
            now, later = lows[s % 2], lows[(s + 1) % 2]
            for j in range(n_blocks):
                states = slice(j * size, (j + 1) * size)
                picked = [
                    now[pl.ds(pl.multiple_of(pattern_ref[j, k] * size, size), size), :]
                    for k in range(n_source)
                ]
                moved = jnp.dot(
                    weight_ref[j],
                    jnp.concatenate(picked, axis=0),
                    preferred_element_type=jnp.float32,
                )
                emission = jnp.broadcast_to(emit_col_ref[states, s : s + 1], (size, LANES))
                stay = stay_ref[states, :]
                for h in range(n_half):
                    part = slice(h * LANES, (h + 1) * LANES)
                    kept = cur_ref[h, j, first - 1 : padded - 1, :] * stay
                    new = (kept + moved[:, part]) * emission
                    if s == 0:
                        new = new * scale[:, part]
                    store(later, j, h, new)
                    if s == steps - 1:
                        sums[h] = sums[h] + jnp.sum(new.reshape(-1, SUBLANES, LANES), axis=0)
        if steps % 2:
            low_a_ref[...] = low_b_ref[...]
        row_sum = jnp.concatenate([jnp.sum(t, axis=0, keepdims=True) for t in sums], axis=1)
        return 1.0 / row_sum, log_scale + jnp.log(row_sum)

    ones = jnp.ones((1, n_rows), jnp.float32)
    scale, log_scale = lax.fori_loop(0, n_segments, segment, (ones, jnp.zeros_like(ones)))
    scale = scale * n_states
    for j in range(n_blocks * size // LANES):
        per = LANES // size
        for h in range(n_half):
            part = slice(h * LANES, (h + 1) * LANES)
            block = [cur_ref[h, j * per + i, first:, :] for i in range(per)]
            block = jnp.concatenate(block, axis=0) * scale[:, part]
            rows_ref[0, part, j * LANES : (j + 1) * LANES] = block.T
    divisor = (n_segments * steps).astype(jnp.float32)
    rate_ref[...] = (log_scale - jnp.log(jnp.full_like(ones, n_states))) / divisor


def body(observed, pattern, trans_blocks, leave_rate, symbol_emit, cluster_emit, symbol_cluster):
    n_blocks, n_source, size, _ = trans_blocks.shape
    n_states = leave_rate.shape[0]
    steps = observed.shape[0]
    n_rows = n_states // lax.axis_size("rows")
    all_observed = lax.all_gather(observed, "tm", axis=0, tiled=True)
    leave_row = leave_rate.reshape(1, n_states)
    vmem = pl.BlockSpec(memory_space=pltpu.VMEM)
    smem = pl.BlockSpec(memory_space=pltpu.SMEM)
    weight, stay = pl.pallas_call(
        build_kernel,
        out_shape=[
            jax.ShapeDtypeStruct((n_blocks, size, n_source * size), jnp.bfloat16),
            jax.ShapeDtypeStruct((n_states, LANES), jnp.float32),
        ],
        in_specs=[smem, vmem, vmem],
        out_specs=[vmem, vmem],
        scratch_shapes=[pltpu.VMEM((n_states, LANES), jnp.float32)],
        compiler_params=pltpu.CompilerParams(vmem_limit_bytes=32 << 20),
        cost_estimate=pl.CostEstimate(flops=1 << 30, bytes_accessed=4 << 20, transcendentals=0),
        name="build",
    )(pattern, trans_blocks, leave_row)
    place = jnp.stack([lax.axis_index("tm") + 1, lax.axis_index("rows") * n_rows]).astype(jnp.int32)
    return pl.pallas_call(
        functools.partial(chain_kernel, steps, size),
        out_shape=[
            jax.ShapeDtypeStruct((1, n_rows, n_states), jnp.float32),
            jax.ShapeDtypeStruct((1, n_rows), jnp.float32),
        ],
        in_specs=[smem, smem, smem, smem, vmem, vmem, vmem, vmem],
        out_specs=[vmem, vmem],
        scratch_shapes=[
            pltpu.VMEM((n_rows // LANES, n_blocks, size + SUBLANES, LANES), jnp.float32),
            pltpu.VMEM((n_states, n_rows), jnp.bfloat16),
            pltpu.VMEM((n_states, n_rows), jnp.bfloat16),
            pltpu.VMEM((LANES, n_states), jnp.float32),
            pltpu.VMEM((n_states, LANES), jnp.float32),
        ],
        compiler_params=pltpu.CompilerParams(vmem_limit_bytes=32 << 20),
        cost_estimate=pl.CostEstimate(flops=1 << 34, bytes_accessed=4 << 20, transcendentals=0),
        name="chain",
    )(place, all_observed, symbol_cluster, pattern, symbol_emit, cluster_emit, weight, stay)


def solution(mesh):
    in_specs = (P("tm"), P(), P(), P(), P(), P(), P())
    out_specs = (P("tm", "rows", None), P("tm", "rows"))
    return jax.shard_map(body, mesh=mesh, in_specs=in_specs, out_specs=out_specs, check_vma=False)
```

```python
import functools

import jax
import jax.numpy as jnp
from jax import lax
from jax.experimental import pallas as pl
from jax.experimental.pallas import tpu as pltpu
from jax.sharding import PartitionSpec as P

LANES = 128
SUBLANES = 8


def column(row):
    return jnp.broadcast_to(row, (LANES, row.shape[1])).T


def chain_kernel(
    place_ref,
    observed_ref,
    pattern_hbm,
    cluster_hbm,
    leave_hbm,
    blocks_hbm,
    cluster_emit_hbm,
    symbol_hbm,
    rows_hbm,
    rate_ref,
    pattern_ref,
    cluster_ref,
    leave_ref,
    blocks_ref,
    cluster_emit_ref,
    symbol_ref,
    rows_ref,
    leave_col_ref,
    stay_ref,
    weight_ref,
    cur_ref,
    low_a_ref,
    low_b_ref,
    emit_ref,
    emit_col_ref,
    sems,
    block_sems,
    out_sems,
):
    steps = observed_ref.shape[1]
    n_half, n_blocks, padded, _ = cur_ref.shape
    size = blocks_ref.shape[-1]
    n_states = n_blocks * size
    n_rows = n_half * LANES
    n_source = pattern_ref.shape[0]
    first = padded - size
    n_segments = place_ref[0]
    row_start = place_ref[1]
    lows = (low_a_ref, low_b_ref)

    small = [
        pltpu.make_async_copy(source, target, sems.at[i])
        for i, (source, target) in enumerate(
            [
                (leave_hbm, leave_ref),
                (pattern_hbm, pattern_ref),
                (cluster_hbm, cluster_ref),
                (cluster_emit_hbm, cluster_emit_ref),
                (symbol_hbm, symbol_ref),
            ]
        )
    ]
    n_chunks = block_sems.shape[0]
    per_chunk = n_blocks // n_chunks
    chunks = [
        pltpu.make_async_copy(
            blocks_hbm.at[pl.ds(i * per_chunk, per_chunk)],
            blocks_ref.at[pl.ds(i * per_chunk, per_chunk)],
            block_sems.at[i],
        )
        for i in range(n_chunks)
    ]
    for copy in small[:2] + chunks + small[2:]:
        copy.start()

    def store(low_ref, j, h, new):
        cur_ref[h, j, first:, :] = new
        cur_ref[h, j, first - 1 : first, :] = new[size - 1 :, :]
        low_ref[j * size : (j + 1) * size, h * LANES : (h + 1) * LANES] = new.astype(jnp.bfloat16)

    state = lax.broadcasted_iota(jnp.int32, (size, LANES), 0)
    row = lax.broadcasted_iota(jnp.int32, (size, LANES), 1)
    for j in range(n_blocks):
        for h in range(n_half):
            start = state + j * size == row + (row_start + h * LANES)
            store(low_a_ref, j, h, start.astype(jnp.float32))
    emit_ref[...] = jnp.zeros_like(emit_ref)

    small[0].wait()
    leave_col = column(leave_ref[...])
    leave_col_ref[...] = leave_col
    for j in range(n_blocks):
        own = leave_col[j * size : (j + 1) * size]
        stay_ref[j * size : (j + 1) * size, :] = 1.0 - pltpu.roll(own, 1, 0)
    small[1].wait()
    for j in range(n_blocks):
        if j % per_chunk == 0:
            chunks[j // per_chunk].wait()
        parts = []
        for k in range(n_source):
            rows = pl.ds(pl.multiple_of(pattern_ref[k, j] * size, size), size)
            parts.append(blocks_ref[j, k].astype(jnp.float32) * leave_col_ref[rows, :size])
        moved = jnp.concatenate(parts, axis=0)
        weight_ref[j] = moved.T.astype(jnp.bfloat16)
    for copy in small[2:]:
        copy.wait()

    def segment(g, carried):
        scale, log_scale = carried
        for s in range(steps):
            symbol = observed_ref[g, s]
            emission = symbol_ref[pl.ds(symbol, 1), :]
            emission = emission * cluster_emit_ref[pl.ds(cluster_ref[symbol], 1), :]
            emit_ref[s : s + 1, :] = emission
        emit_col_ref[...] = emit_ref[...].T
        sums = [jnp.zeros((SUBLANES, LANES), jnp.float32) for _ in range(n_half)]
        for s in range(steps):
            now, later = lows[s % 2], lows[(s + 1) % 2]
            for j in range(n_blocks):
                states = slice(j * size, (j + 1) * size)
                picked = [
                    now[pl.ds(pl.multiple_of(pattern_ref[k, j] * size, size), size), :]
                    for k in range(n_source)
                ]
                moved = jnp.dot(
                    weight_ref[j],
                    jnp.concatenate(picked, axis=0),
                    preferred_element_type=jnp.float32,
                )
                emission = jnp.broadcast_to(emit_col_ref[states, s : s + 1], (size, LANES))
                stay = stay_ref[states, :]
                for h in range(n_half):
                    part = slice(h * LANES, (h + 1) * LANES)
                    kept = cur_ref[h, j, first - 1 : padded - 1, :] * stay
                    new = (kept + moved[:, part]) * emission
                    if s == 0:
                        new = new * scale[:, part]
                    store(later, j, h, new)
                    if s == steps - 1:
                        sums[h] = sums[h] + jnp.sum(new.reshape(-1, SUBLANES, LANES), axis=0)
        if steps % 2:
            low_a_ref[...] = low_b_ref[...]
        row_sum = jnp.concatenate([jnp.sum(t, axis=0, keepdims=True) for t in sums], axis=1)
        return 1.0 / row_sum, log_scale + jnp.log(row_sum)

    ones = jnp.ones((1, n_rows), jnp.float32)
    scale, log_scale = lax.fori_loop(0, n_segments, segment, (ones, jnp.zeros_like(ones)))
    scale = scale * n_states
    per = LANES // size
    out = []
    for h in range(n_half):
        part = slice(h * LANES, (h + 1) * LANES)
        for j in range(n_states // LANES):
            block = [cur_ref[h, j * per + i, first:, :] for i in range(per)]
            block = jnp.concatenate(block, axis=0) * scale[:, part]
            rows_ref[part, j * LANES : (j + 1) * LANES] = block.T
        rows = pl.ds(h * LANES, LANES)
        out.append(
            pltpu.make_async_copy(rows_ref.at[rows], rows_hbm.at[0, rows], out_sems.at[h])
        )
        out[-1].start()
    divisor = (n_segments * steps).astype(jnp.float32)
    rate_ref[...] = (log_scale - jnp.log(jnp.full_like(ones, n_states))) / divisor
    for copy in out:
        copy.wait()


def body(observed, pattern, trans_blocks, leave_rate, symbol_emit, cluster_emit, symbol_cluster):
    n_blocks, n_source, size, _ = trans_blocks.shape
    n_states = leave_rate.shape[0]
    steps = observed.shape[0]
    n_rows = n_states // lax.axis_size("rows")
    tm = lax.axis_index("tm")
    segments = jnp.arange(lax.axis_size("tm"))
    own = jnp.where(segments[:, None] == tm, observed[None, :], 0)
    all_observed = lax.psum(own, "tm")
    place = jnp.stack([tm + 1, lax.axis_index("rows") * n_rows]).astype(jnp.int32)
    vmem = pl.BlockSpec(memory_space=pltpu.VMEM)
    smem = pl.BlockSpec(memory_space=pltpu.SMEM)
    hbm = pl.BlockSpec(memory_space=pltpu.HBM)
    f32, bf16 = jnp.float32, jnp.bfloat16
    return pl.pallas_call(
        chain_kernel,
        out_shape=[
            jax.ShapeDtypeStruct((1, n_rows, n_states), f32),
            jax.ShapeDtypeStruct((1, n_rows), f32),
        ],
        in_specs=[smem, smem] + [hbm] * 6,
        out_specs=[hbm, vmem],
        scratch_shapes=[
            pltpu.SMEM((n_source, n_blocks), jnp.int32),
            pltpu.SMEM(symbol_cluster.shape, jnp.int32),
            pltpu.VMEM((1, n_states), f32),
            pltpu.VMEM(trans_blocks.shape, bf16),
            pltpu.VMEM(cluster_emit.shape, f32),
            pltpu.VMEM(symbol_emit.shape, f32),
            pltpu.VMEM((n_rows, n_states), f32),
            pltpu.VMEM((n_states, LANES), f32),
            pltpu.VMEM((n_states, LANES), f32),
            pltpu.VMEM((n_blocks, size, n_source * size), bf16),
            pltpu.VMEM((n_rows // LANES, n_blocks, size + SUBLANES, LANES), f32),
            pltpu.VMEM((n_states, n_rows), bf16),
            pltpu.VMEM((n_states, n_rows), bf16),
            pltpu.VMEM((LANES, n_states), f32),
            pltpu.VMEM((n_states, LANES), f32),
            pltpu.SemaphoreType.DMA((5,)),
            pltpu.SemaphoreType.DMA((4,)),
            pltpu.SemaphoreType.DMA((n_rows // LANES,)),
        ],
        compiler_params=pltpu.CompilerParams(vmem_limit_bytes=60 << 20),
        cost_estimate=pl.CostEstimate(flops=1 << 34, bytes_accessed=4 << 20, transcendentals=0),
        name="chain",
    )(
        place,
        all_observed,
        pattern.T,
        symbol_cluster,
        leave_rate.reshape(1, n_states),
        trans_blocks,
        cluster_emit,
        symbol_emit,
    )


def solution(mesh):
    in_specs = (P("tm"), P(), P(), P(), P(), P(), P())
    out_specs = (P("tm", "rows", None), P("tm", "rows"))
    return jax.shard_map(body, mesh=mesh, in_specs=in_specs, out_specs=out_specs, check_vma=False)
```

```python
import functools

import jax
import jax.numpy as jnp
from jax import lax
from jax.experimental import pallas as pl
from jax.experimental.pallas import tpu as pltpu
from jax.sharding import PartitionSpec as P

LANES = 128
SUBLANES = 8


def column(row):
    return jnp.broadcast_to(row, (LANES, row.shape[1])).T


def chain_kernel(
    observed_ref,
    pattern_hbm,
    cluster_hbm,
    leave_hbm,
    blocks_hbm,
    cluster_emit_hbm,
    symbol_hbm,
    rows_hbm,
    rate_ref,
    pattern_ref,
    cluster_ref,
    leave_ref,
    blocks_ref,
    cluster_emit_ref,
    symbol_ref,
    rows_ref,
    leave_col_ref,
    stay_ref,
    weight_ref,
    cur_refs,
    low_refs,
    emit_ref,
    emit_col_ref,
    sems,
    block_sems,
    out_sems,
):
    steps = observed_ref.shape[1]
    n_half = len(cur_refs)
    n_blocks, padded, _ = cur_refs[0].shape
    size = blocks_ref.shape[-1]
    n_states = n_blocks * size
    n_rows = n_half * LANES
    n_source = pattern_ref.shape[0]
    first = padded - size
    n_segments = lax.axis_index("tm") + 1
    row_start = lax.axis_index("rows") * n_rows

    small = [
        pltpu.make_async_copy(source, target, sems.at[i])
        for i, (source, target) in enumerate(
            [
                (leave_hbm, leave_ref),
                (pattern_hbm, pattern_ref),
                (cluster_hbm, cluster_ref),
                (cluster_emit_hbm, cluster_emit_ref),
                (symbol_hbm, symbol_ref),
            ]
        )
    ]
    n_chunks = block_sems.shape[0]
    per_chunk = n_blocks // n_chunks
    chunks = [
        pltpu.make_async_copy(
            blocks_hbm.at[pl.ds(i * per_chunk, per_chunk)],
            blocks_ref.at[pl.ds(i * per_chunk, per_chunk)],
            block_sems.at[i],
        )
        for i in range(n_chunks)
    ]
    for copy in small[:2] + chunks + small[2:]:
        copy.start()

    def store(cur_ref, low_ref, j, new):
        cur_ref[j, first:, :] = new
        cur_ref[j, first - 1 : first, :] = new[size - 1 :, :]
        low_ref[j * size : (j + 1) * size, :] = new.astype(jnp.bfloat16)

    state = lax.broadcasted_iota(jnp.int32, (size, LANES), 0)
    row = lax.broadcasted_iota(jnp.int32, (size, LANES), 1)
    for j in range(n_blocks):
        for h in range(n_half):
            start = state + j * size == row + (row_start + h * LANES)
            store(cur_refs[h], low_refs[h][0], j, start.astype(jnp.float32))
    emit_ref[...] = jnp.zeros_like(emit_ref)

    small[0].wait()
    leave_col = column(leave_ref[...])
    leave_col_ref[...] = leave_col
    for j in range(n_blocks):
        own = leave_col[j * size : (j + 1) * size]
        stay_ref[j * size : (j + 1) * size, :] = 1.0 - pltpu.roll(own, 1, 0)
    small[1].wait()
    for j in range(n_blocks):
        if j % per_chunk == 0:
            chunks[j // per_chunk].wait()
        parts = []
        for k in range(n_source):
            rows = pl.ds(pl.multiple_of(pattern_ref[k, j] * size, size), size)
            parts.append(blocks_ref[j, k].astype(jnp.float32) * leave_col_ref[rows, :size])
        moved = jnp.concatenate(parts, axis=0)
        weight_ref[j] = moved.T.astype(jnp.bfloat16)
    for copy in small[2:]:
        copy.wait()

    def segment(g, carried):
        scale, log_scale = carried
        for s in range(steps):
            symbol = observed_ref[g, s]
            emission = symbol_ref[pl.ds(symbol, 1), :]
            emission = emission * cluster_emit_ref[pl.ds(cluster_ref[symbol], 1), :]
            emit_ref[s : s + 1, :] = emission
        emit_col_ref[...] = emit_ref[...].T
        sums = [jnp.zeros((SUBLANES, LANES), jnp.float32) for _ in range(n_half)]
        for s in range(steps):
            for h in range(n_half):
                now, later = low_refs[h][s % 2], low_refs[h][(s + 1) % 2]
                part = slice(h * LANES, (h + 1) * LANES)
                for j in range(n_blocks):
                    states = slice(j * size, (j + 1) * size)
                    picked = [
                        now[pl.ds(pl.multiple_of(pattern_ref[k, j] * size, size), size), :]
                        for k in range(n_source)
                    ]
                    moved = jnp.dot(
                        weight_ref[j],
                        jnp.concatenate(picked, axis=0),
                        preferred_element_type=jnp.float32,
                    )
                    emission = jnp.broadcast_to(emit_col_ref[states, s : s + 1], (size, LANES))
                    kept = cur_refs[h][j, first - 1 : padded - 1, :] * stay_ref[states, :]
                    new = (kept + moved) * emission
                    if s == 0:
                        new = new * scale[:, part]
                    store(cur_refs[h], later, j, new)
                    if s == steps - 1:
                        sums[h] = sums[h] + jnp.sum(new.reshape(-1, SUBLANES, LANES), axis=0)
        if steps % 2:
            for h in range(n_half):
                low_refs[h][0][...] = low_refs[h][1][...]
        row_sum = jnp.concatenate([jnp.sum(t, axis=0, keepdims=True) for t in sums], axis=1)
        return 1.0 / row_sum, log_scale + jnp.log(row_sum)

    ones = jnp.ones((1, n_rows), jnp.float32)
    scale, log_scale = lax.fori_loop(0, n_segments, segment, (ones, jnp.zeros_like(ones)))
    scale = scale * n_states
    per = LANES // size
    out = []
    for h in range(n_half):
        part = slice(h * LANES, (h + 1) * LANES)
        for j in range(n_states // LANES):
            block = [cur_refs[h][j * per + i, first:, :] for i in range(per)]
            block = jnp.concatenate(block, axis=0) * scale[:, part]
            rows_ref[part, j * LANES : (j + 1) * LANES] = block.T
        rows = pl.ds(h * LANES, LANES)
        out.append(
            pltpu.make_async_copy(rows_ref.at[rows], rows_hbm.at[0, rows], out_sems.at[h])
        )
        out[-1].start()
    divisor = (n_segments * steps).astype(jnp.float32)
    rate_ref[...] = (log_scale - jnp.log(jnp.full_like(ones, n_states))) / divisor
    for copy in out:
        copy.wait()


def body(observed, pattern, trans_blocks, leave_rate, symbol_emit, cluster_emit, symbol_cluster):
    n_blocks, n_source, size, _ = trans_blocks.shape
    n_states = leave_rate.shape[0]
    steps = observed.shape[0]
    n_rows = n_states // lax.axis_size("rows")
    n_half = n_rows // LANES
    tm = lax.axis_index("tm")
    segments = jnp.arange(lax.axis_size("tm"))
    own = jnp.where(segments[:, None] == tm, observed[None, :], 0)
    all_observed = lax.psum(own, "tm")
    vmem = pl.BlockSpec(memory_space=pltpu.VMEM)
    smem = pl.BlockSpec(memory_space=pltpu.SMEM)
    hbm = pl.BlockSpec(memory_space=pltpu.HBM)
    f32, bf16 = jnp.float32, jnp.bfloat16
    return pl.pallas_call(
        chain_kernel,
        out_shape=[
            jax.ShapeDtypeStruct((1, n_rows, n_states), f32),
            jax.ShapeDtypeStruct((1, n_rows), f32),
        ],
        in_specs=[smem] + [hbm] * 6,
        out_specs=[hbm, vmem],
        scratch_shapes=[
            pltpu.SMEM((n_source, n_blocks), jnp.int32),
            pltpu.SMEM(symbol_cluster.shape, jnp.int32),
            pltpu.VMEM((1, n_states), f32),
            pltpu.VMEM(trans_blocks.shape, bf16),
            pltpu.VMEM(cluster_emit.shape, f32),
            pltpu.VMEM(symbol_emit.shape, f32),
            pltpu.VMEM((n_rows, n_states), f32),
            pltpu.VMEM((n_states, LANES), f32),
            pltpu.VMEM((n_states, LANES), f32),
            pltpu.VMEM((n_blocks, size, n_source * size), bf16),
            [pltpu.VMEM((n_blocks, size + SUBLANES, LANES), f32) for _ in range(n_half)],
            [[pltpu.VMEM((n_states, LANES), bf16) for _ in range(2)] for _ in range(n_half)],
            pltpu.VMEM((LANES, n_states), f32),
            pltpu.VMEM((n_states, LANES), f32),
            pltpu.SemaphoreType.DMA((5,)),
            pltpu.SemaphoreType.DMA((4,)),
            pltpu.SemaphoreType.DMA((n_half,)),
        ],
        compiler_params=pltpu.CompilerParams(vmem_limit_bytes=60 << 20),
        cost_estimate=pl.CostEstimate(flops=1 << 34, bytes_accessed=4 << 20, transcendentals=0),
        name="chain",
    )(
        all_observed,
        pattern.T,
        symbol_cluster,
        leave_rate.reshape(1, n_states),
        trans_blocks,
        cluster_emit,
        symbol_emit,
    )


def solution(mesh):
    in_specs = (P("tm"), P(), P(), P(), P(), P(), P())
    out_specs = (P("tm", "rows", None), P("tm", "rows"))
    return jax.shard_map(body, mesh=mesh, in_specs=in_specs, out_specs=out_specs, check_vma=False)
```

```python
import functools

import jax
import jax.numpy as jnp
from jax import lax
from jax.experimental import pallas as pl
from jax.experimental.pallas import tpu as pltpu
from jax.sharding import PartitionSpec as P

LANES = 128
SUBLANES = 8


def column(row):
    return jnp.broadcast_to(row, (LANES, row.shape[1])).T


def chain_kernel(
    observed_ref,
    pattern_hbm,
    cluster_hbm,
    leave_hbm,
    blocks_hbm,
    cluster_emit_hbm,
    symbol_hbm,
    rows_hbm,
    rate_ref,
    pattern_ref,
    cluster_ref,
    leave_ref,
    blocks_ref,
    cluster_emit_ref,
    symbol_ref,
    rows_ref,
    leave_col_ref,
    stay_ref,
    weight_ref,
    back_ref,
    cur_ref,
    base_ref,
    low_a_ref,
    low_b_ref,
    emit_ref,
    emit_col_ref,
    stay_slab_ref,
    emit_slab_ref,
    sum_refs,
    part_refs,
    change_ref,
    sems,
    block_sems,
    out_sems,
):
    steps = observed_ref.shape[1]
    n_half, n_blocks, padded, _ = cur_ref.shape
    size = blocks_ref.shape[-1]
    n_states = n_blocks * size
    n_rows = n_half * LANES
    n_source = pattern_ref.shape[0]
    first = padded - size
    n_segments = lax.axis_index("tm") + 1
    row_start = lax.axis_index("rows") * n_rows
    lows = (low_a_ref, low_b_ref)

    small = [
        pltpu.make_async_copy(source, target, sems.at[i])
        for i, (source, target) in enumerate(
            [
                (leave_hbm, leave_ref),
                (pattern_hbm, pattern_ref),
                (cluster_hbm, cluster_ref),
                (cluster_emit_hbm, cluster_emit_ref),
                (symbol_hbm, symbol_ref),
            ]
        )
    ]
    n_chunks = block_sems.shape[0]
    per_chunk = n_blocks // n_chunks
    chunks = [
        pltpu.make_async_copy(
            blocks_hbm.at[pl.ds(i * per_chunk, per_chunk)],
            blocks_ref.at[pl.ds(i * per_chunk, per_chunk)],
            block_sems.at[i],
        )
        for i in range(n_chunks)
    ]
    for copy in small[:2] + chunks + small[2:]:
        copy.start()

    def store(target_ref, low_ref, j, h, new):
        target_ref[h, j, first:, :] = new
        target_ref[h, j, :first, :] = new[size - first :, :]
        low_ref[j * size : (j + 1) * size, h * LANES : (h + 1) * LANES] = new.astype(jnp.bfloat16)

    state = lax.broadcasted_iota(jnp.int32, (size, LANES), 0)
    row = lax.broadcasted_iota(jnp.int32, (size, LANES), 1)
    for j in range(n_blocks):
        for h in range(n_half):
            start = state + j * size == row + (row_start + h * LANES)
            store(base_ref, low_a_ref, j, h, start.astype(jnp.float32))
    emit_ref[...] = jnp.zeros_like(emit_ref)

    per = LANES // size
    low_half = lax.broadcasted_iota(jnp.int32, (1, LANES), 1) < size

    def twice(tile, at):
        other = pltpu.roll(tile, size, 1)
        return jnp.where(low_half, tile, other) if at == 0 else jnp.where(low_half, other, tile)

    small[0].wait()
    for j in range(n_blocks):
        tile = leave_ref[:, j // per * LANES : (j // per + 1) * LANES]
        tile = jnp.broadcast_to(1.0 - tile, (SUBLANES, LANES))
        stay_slab_ref[j] = twice(tile, j % per)
    leave_col = column(leave_ref[...])
    leave_col_ref[...] = leave_col
    for j in range(n_blocks):
        own = leave_col[j * size : (j + 1) * size]
        stay_ref[j * size : (j + 1) * size, :] = 1.0 - pltpu.roll(own, 1, 0)
    small[1].wait()
    for j in range(n_blocks):
        if j % per_chunk == 0:
            chunks[j // per_chunk].wait()
        parts = []
        for k in range(n_source):
            rows = pl.ds(pl.multiple_of(pattern_ref[k, j] * size, size), size)
            parts.append(blocks_ref[j, k].astype(jnp.float32) * leave_col_ref[rows, :size])
        moved = jnp.concatenate(parts, axis=0).T
        weight_ref[j] = moved.astype(jnp.bfloat16)
        for k in range(n_source):
            tile = moved[:, k // per * LANES : (k // per + 1) * LANES]
            back_ref[j, :, k * LANES : (k + 1) * LANES] = twice(tile, k % per).astype(jnp.bfloat16)
    for copy in small[2:]:
        copy.wait()

    n_tm = observed_ref.shape[0]

    def emission_of(g, s):
        symbol = observed_ref[g, s]
        row = symbol_ref[pl.ds(symbol, 1), :]
        return row * cluster_emit_ref[pl.ds(cluster_ref[symbol], 1), :]

    for s in range(steps):
        emission = jnp.concatenate([emission_of(g, s) for g in range(n_tm)], axis=0)
        for j in range(n_blocks):
            tile = emission[:, j // per * LANES : (j // per + 1) * LANES]
            emit_slab_ref[s, j] = twice(tile, j % per)
    stays = [jnp.broadcast_to(stay_slab_ref[j][:1], (n_tm, LANES)) for j in range(n_blocks)]

    for l in range(steps):
        n_pos = steps - l
        for ref in part_refs:
            ref[...] = jnp.zeros_like(ref)
        for j in range(n_blocks):
            images = []
            for p in range(n_pos):
                image = emit_slab_ref[p, j]
                if l:
                    image = image * sum_refs[l - 1][p + 1, j]
                images.append(image)
                sum_refs[l][p, j] = stays[j] * pltpu.roll(image, LANES - 1, 1)
            images = jnp.concatenate(images, axis=0)[:, :size].astype(jnp.bfloat16)
            moved = jnp.dot(images, back_ref[j], preferred_element_type=jnp.float32)
            for k in range(n_source):
                part = moved[:, k * LANES : (k + 1) * LANES].reshape(n_pos, n_tm, LANES)
                source = pattern_ref[k, j]
                for p in range(n_pos):
                    part_refs[k][p, source] = part_refs[k][p, source] + part[p]
        for j in range(n_blocks):
            for p in range(n_pos):
                total = sum_refs[l][p, j]
                for ref in part_refs:
                    total = total + ref[p, j]
                sum_refs[l][p, j] = total

    changes = []
    for j in range(n_blocks):
        exact = jnp.ones((n_tm, LANES), jnp.float32)
        weight = exact
        deviation = []
        for s in range(steps):
            row_sum = pltpu.roll(sum_refs[s][0, j], 1, 1)
            for q in range(s):
                row_sum = row_sum + deviation[q] * sum_refs[s - q - 1][q + 1, j]
                row_sum = pltpu.roll(row_sum, 1, 1)
            emission = emit_slab_ref[s, j]
            exact = pltpu.roll(exact * stays[j], 1, 1) * emission
            weight = pltpu.roll(weight * stays[j], 1, 1) * emission
            rounded = (weight * (n_states / row_sum)).astype(jnp.bfloat16).astype(jnp.float32)
            rounded = rounded * (row_sum * (1.0 / n_states))
            deviation.append(rounded - weight)
            weight = rounded
        changes.append(weight - exact)
    for m in range(n_states // LANES):
        tile = changes[m * per + per - 1]
        for i in range(per - 1):
            tile = jnp.where(low_half, changes[m * per + i], tile)
        change_ref[:, m * LANES : (m + 1) * LANES] = tile

    def segment(g, carried):
        scale, log_scale = carried
        for s in range(steps):
            emit_ref[s : s + 1, :] = emission_of(g, s)
        emit_ref[steps : steps + 1, :] = change_ref[pl.ds(g, 1), :]
        emit_col_ref[...] = emit_ref[...].T
        sums = [jnp.zeros((SUBLANES, LANES), jnp.float32) for _ in range(n_half)]
        for s in range(steps):
            now, later = lows[s % 2], lows[(s + 1) % 2]
            for j in range(n_blocks):
                states = slice(j * size, (j + 1) * size)
                picked = [
                    now[pl.ds(pl.multiple_of(pattern_ref[k, j] * size, size), size), :]
                    for k in range(n_source)
                ]
                moved = jnp.dot(
                    weight_ref[j],
                    jnp.concatenate(picked, axis=0),
                    preferred_element_type=jnp.float32,
                )
                emission = jnp.broadcast_to(emit_col_ref[states, s : s + 1], (size, LANES))
                stay = stay_ref[states, :]
                from_ref = base_ref if s == 0 else cur_ref
                to_ref = base_ref if s == steps - 1 else cur_ref
                if s == steps - 1:
                    change = jnp.broadcast_to(emit_col_ref[states, steps : steps + 1], (size, LANES))
                for h in range(n_half):
                    part = slice(h * LANES, (h + 1) * LANES)
                    kept = from_ref[h, j, first - 1 : padded - 1, :] * stay
                    new = (kept + moved[:, part]) * emission
                    if s == 0:
                        new = new * scale[:, part]
                    if s == steps - 1:
                        start = base_ref[h, j, first - steps : padded - steps, :]
                        new = new + start * change * scale[:, part]
                        sums[h] = sums[h] + jnp.sum(new.reshape(-1, SUBLANES, LANES), axis=0)
                    store(to_ref, later, j, h, new)
        if steps % 2:
            low_a_ref[...] = low_b_ref[...]
        row_sum = jnp.concatenate([jnp.sum(t, axis=0, keepdims=True) for t in sums], axis=1)
        return 1.0 / row_sum, log_scale + jnp.log(row_sum)

    ones = jnp.ones((1, n_rows), jnp.float32)
    scale, log_scale = lax.fori_loop(0, n_segments, segment, (ones, jnp.zeros_like(ones)))
    scale = scale * n_states
    out = []
    for h in range(n_half):
        part = slice(h * LANES, (h + 1) * LANES)
        for j in range(n_states // LANES):
            block = [base_ref[h, j * per + i, first:, :] for i in range(per)]
            block = jnp.concatenate(block, axis=0) * scale[:, part]
            rows_ref[part, j * LANES : (j + 1) * LANES] = block.T
        rows = pl.ds(h * LANES, LANES)
        out.append(
            pltpu.make_async_copy(rows_ref.at[rows], rows_hbm.at[0, rows], out_sems.at[h])
        )
        out[-1].start()
    divisor = (n_segments * steps).astype(jnp.float32)
    rate_ref[...] = (log_scale - jnp.log(jnp.full_like(ones, n_states))) / divisor
    for copy in out:
        copy.wait()


def body(observed, pattern, trans_blocks, leave_rate, symbol_emit, cluster_emit, symbol_cluster):
    n_blocks, n_source, size, _ = trans_blocks.shape
    n_states = leave_rate.shape[0]
    steps = observed.shape[0]
    n_rows = n_states // lax.axis_size("rows")
    n_tm = lax.axis_size("tm")
    own = jnp.broadcast_to(observed[None, :], (n_tm, steps))
    all_observed = lax.all_to_all(own, "tm", 0, 0, tiled=True)
    vmem = pl.BlockSpec(memory_space=pltpu.VMEM)
    smem = pl.BlockSpec(memory_space=pltpu.SMEM)
    hbm = pl.BlockSpec(memory_space=pltpu.HBM)
    f32, bf16 = jnp.float32, jnp.bfloat16
    return pl.pallas_call(
        chain_kernel,
        out_shape=[
            jax.ShapeDtypeStruct((1, n_rows, n_states), f32),
            jax.ShapeDtypeStruct((1, n_rows), f32),
        ],
        in_specs=[smem] + [hbm] * 6,
        out_specs=[hbm, vmem],
        scratch_shapes=[
            pltpu.SMEM((n_source, n_blocks), jnp.int32),
            pltpu.SMEM(symbol_cluster.shape, jnp.int32),
            pltpu.VMEM((1, n_states), f32),
            pltpu.VMEM(trans_blocks.shape, bf16),
            pltpu.VMEM(cluster_emit.shape, f32),
            pltpu.VMEM(symbol_emit.shape, f32),
            pltpu.VMEM((n_rows, n_states), f32),
            pltpu.VMEM((n_states, LANES), f32),
            pltpu.VMEM((n_states, LANES), f32),
            pltpu.VMEM((n_blocks, size, n_source * size), bf16),
            pltpu.VMEM((n_blocks, size, n_source * LANES), bf16),
            pltpu.VMEM((n_rows // LANES, n_blocks, size + SUBLANES, LANES), f32),
            pltpu.VMEM((n_rows // LANES, n_blocks, size + SUBLANES, LANES), f32),
            pltpu.VMEM((n_states, n_rows), bf16),
            pltpu.VMEM((n_states, n_rows), bf16),
            pltpu.VMEM((LANES, n_states), f32),
            pltpu.VMEM((n_states, LANES), f32),
            pltpu.VMEM((n_blocks, SUBLANES, LANES), f32),
            pltpu.VMEM((steps, n_blocks, n_tm, LANES), f32),
            [pltpu.VMEM((steps - l, n_blocks, n_tm, LANES), f32) for l in range(steps)],
            [pltpu.VMEM((steps, n_blocks, n_tm, LANES), f32) for _ in range(n_source)],
            pltpu.VMEM((n_tm, n_states), f32),
            pltpu.SemaphoreType.DMA((5,)),
            pltpu.SemaphoreType.DMA((4,)),
            pltpu.SemaphoreType.DMA((n_rows // LANES,)),
        ],
        compiler_params=pltpu.CompilerParams(vmem_limit_bytes=60 << 20),
        cost_estimate=pl.CostEstimate(flops=1 << 34, bytes_accessed=4 << 20, transcendentals=0),
        name="chain",
    )(
        all_observed,
        pattern.T,
        symbol_cluster,
        leave_rate.reshape(1, n_states),
        trans_blocks,
        cluster_emit,
        symbol_emit,
    )


def solution(mesh):
    in_specs = (P("tm"), P(), P(), P(), P(), P(), P())
    out_specs = (P("tm", "rows", None), P("tm", "rows"))
    return jax.shard_map(body, mesh=mesh, in_specs=in_specs, out_specs=out_specs, check_vma=False)
```

```python
import functools

import jax
import jax.numpy as jnp
from jax import lax
from jax.experimental import pallas as pl
from jax.experimental.pallas import tpu as pltpu
from jax.sharding import PartitionSpec as P

LANES = 128
SUBLANES = 8


def column(row):
    return jnp.broadcast_to(row, (LANES, row.shape[1])).T


def twice(tile, at, size):
    other = pltpu.roll(tile, size, 1)
    low_half = lax.broadcasted_iota(jnp.int32, (1, LANES), 1) < size
    return jnp.where(low_half, tile, other) if at == 0 else jnp.where(low_half, other, tile)


def build_kernel(
    pattern_ref, leave_ref, blocks_ref, weight_ref, stay_ref, stay_slab_ref, leave_col_ref
):
    n_blocks, n_source, size, _ = blocks_ref.shape
    per = LANES // size
    for j in range(n_blocks):
        tile = leave_ref[:, j // per * LANES : (j // per + 1) * LANES]
        tile = jnp.broadcast_to(1.0 - tile, (SUBLANES, LANES))
        stay_slab_ref[j] = twice(tile, j % per, size)
    leave_col = column(leave_ref[...])
    leave_col_ref[...] = leave_col
    for j in range(n_blocks):
        own = leave_col[j * size : (j + 1) * size]
        stay_ref[j * size : (j + 1) * size, :] = 1.0 - pltpu.roll(own, 1, 0)
    for j in range(n_blocks):
        parts = []
        for k in range(n_source):
            rows = pl.ds(pl.multiple_of(pattern_ref[k, j] * size, size), size)
            parts.append(blocks_ref[j, k].astype(jnp.float32) * leave_col_ref[rows, :size])
        weight_ref[j] = jnp.concatenate(parts, axis=0).T.astype(jnp.bfloat16)


def chain_kernel(
    observed_ref,
    pattern_ref,
    cluster_ref,
    cluster_emit_ref,
    symbol_ref,
    weight_ref,
    stay_ref,
    stay_slab_ref,
    rows_hbm,
    rate_ref,
    rows_ref,
    cur_ref,
    base_ref,
    low_a_ref,
    low_b_ref,
    emit_ref,
    emit_col_ref,
    emit_slab_ref,
    sum_refs,
    part_refs,
    change_ref,
    out_sems,
):
    steps = observed_ref.shape[1]
    n_half, n_blocks, padded, _ = cur_ref.shape
    size = weight_ref.shape[1]
    per = LANES // size
    low_half = lax.broadcasted_iota(jnp.int32, (1, LANES), 1) < size
    n_states = n_blocks * size
    n_rows = n_half * LANES
    n_source = pattern_ref.shape[0]
    first = padded - size
    n_segments = lax.axis_index("tm") + 1
    row_start = lax.axis_index("rows") * n_rows
    lows = (low_a_ref, low_b_ref)

    def store(target_ref, low_ref, j, h, new):
        target_ref[h, j, first:, :] = new
        target_ref[h, j, :first, :] = new[size - first :, :]
        low_ref[j * size : (j + 1) * size, h * LANES : (h + 1) * LANES] = new.astype(jnp.bfloat16)

    state = lax.broadcasted_iota(jnp.int32, (size, LANES), 0)
    row = lax.broadcasted_iota(jnp.int32, (size, LANES), 1)
    for j in range(n_blocks):
        for h in range(n_half):
            start = state + j * size == row + (row_start + h * LANES)
            store(base_ref, low_a_ref, j, h, start.astype(jnp.float32))
    emit_ref[...] = jnp.zeros_like(emit_ref)

    n_tm = observed_ref.shape[0]

    def emission_of(g, s):
        symbol = observed_ref[g, s]
        row = symbol_ref[pl.ds(symbol, 1), :]
        return row * cluster_emit_ref[pl.ds(cluster_ref[symbol], 1), :]

    for s in range(steps):
        emission = jnp.concatenate([emission_of(g, s) for g in range(n_tm)], axis=0)
        for j in range(n_blocks):
            tile = emission[:, j // per * LANES : (j // per + 1) * LANES]
            emit_slab_ref[s, j] = twice(tile, j % per, size)
    stays = [jnp.broadcast_to(stay_slab_ref[j][:1], (n_tm, LANES)) for j in range(n_blocks)]

    for l in range(steps):
        n_pos = steps - l
        for ref in part_refs:
            ref[...] = jnp.zeros_like(ref)
        for j in range(n_blocks):
            images = []
            for p in range(n_pos):
                image = emit_slab_ref[p, j]
                if l:
                    image = image * sum_refs[l - 1][p + 1, j]
                images.append(image)
                sum_refs[l][p, j] = stays[j] * pltpu.roll(image, LANES - 1, 1)
            images = jnp.concatenate(images, axis=0)[:, :size].astype(jnp.bfloat16)
            moved = jnp.dot(images, weight_ref[j], preferred_element_type=jnp.float32)
            for k in range(n_source):
                tile = moved[:, k // per * LANES : (k // per + 1) * LANES]
                tile = tile.reshape(n_pos, n_tm, LANES)
                source = pattern_ref[k, j]
                for p in range(n_pos):
                    part_refs[k][p, source] = part_refs[k][p, source] + tile[p]
        for j in range(n_blocks):
            for p in range(n_pos):
                sides = []
                for i in range(per):
                    sides.append(sum(ref[p, j] for ref in part_refs[i + per :: per]))
                    sides[i] = sides[i] + part_refs[i][p, j]
                total = jnp.where(low_half, sides[0], sides[1])
                total = total + pltpu.roll(total, size, 1)
                sum_refs[l][p, j] = sum_refs[l][p, j] + total

    changes = []
    for j in range(n_blocks):
        exact = jnp.ones((n_tm, LANES), jnp.float32)
        weight = exact
        deviation = []
        for s in range(steps):
            row_sum = pltpu.roll(sum_refs[s][0, j], 1, 1)
            for q in range(s):
                row_sum = row_sum + deviation[q] * sum_refs[s - q - 1][q + 1, j]
                row_sum = pltpu.roll(row_sum, 1, 1)
            emission = emit_slab_ref[s, j]
            exact = pltpu.roll(exact * stays[j], 1, 1) * emission
            weight = pltpu.roll(weight * stays[j], 1, 1) * emission
            rounded = (weight * (n_states / row_sum)).astype(jnp.bfloat16).astype(jnp.float32)
            rounded = rounded * (row_sum * (1.0 / n_states))
            deviation.append(rounded - weight)
            weight = rounded
        changes.append(weight - exact)
    for m in range(n_states // LANES):
        tile = changes[m * per + per - 1]
        for i in range(per - 1):
            tile = jnp.where(low_half, changes[m * per + i], tile)
        change_ref[:, m * LANES : (m + 1) * LANES] = tile

    def segment(g, carried):
        scale, log_scale = carried
        for s in range(steps):
            emit_ref[s : s + 1, :] = emission_of(g, s)
        emit_ref[steps : steps + 1, :] = change_ref[pl.ds(g, 1), :]
        emit_col_ref[...] = emit_ref[...].T
        sums = [jnp.zeros((SUBLANES, LANES), jnp.float32) for _ in range(n_half)]
        for s in range(steps):
            now, later = lows[s % 2], lows[(s + 1) % 2]
            for j in range(n_blocks):
                states = slice(j * size, (j + 1) * size)
                picked = [
                    now[pl.ds(pl.multiple_of(pattern_ref[k, j] * size, size), size), :]
                    for k in range(n_source)
                ]
                moved = jnp.dot(
                    weight_ref[j],
                    jnp.concatenate(picked, axis=0),
                    preferred_element_type=jnp.float32,
                )
                emission = jnp.broadcast_to(emit_col_ref[states, s : s + 1], (size, LANES))
                stay = stay_ref[states, :]
                from_ref = base_ref if s == 0 else cur_ref
                to_ref = base_ref if s == steps - 1 else cur_ref
                if s == steps - 1:
                    change = jnp.broadcast_to(emit_col_ref[states, steps : steps + 1], (size, LANES))
                for h in range(n_half):
                    part = slice(h * LANES, (h + 1) * LANES)
                    kept = from_ref[h, j, first - 1 : padded - 1, :] * stay
                    new = (kept + moved[:, part]) * emission
                    if s == 0:
                        new = new * scale[:, part]
                    if s == steps - 1:
                        start = base_ref[h, j, first - steps : padded - steps, :]
                        new = new + start * change * scale[:, part]
                        sums[h] = sums[h] + jnp.sum(new.reshape(-1, SUBLANES, LANES), axis=0)
                    store(to_ref, later, j, h, new)
        if steps % 2:
            low_a_ref[...] = low_b_ref[...]
        row_sum = jnp.concatenate([jnp.sum(t, axis=0, keepdims=True) for t in sums], axis=1)
        return 1.0 / row_sum, log_scale + jnp.log(row_sum)

    ones = jnp.ones((1, n_rows), jnp.float32)
    scale, log_scale = lax.fori_loop(0, n_segments, segment, (ones, jnp.zeros_like(ones)))
    scale = scale * n_states
    out = []
    for h in range(n_half):
        part = slice(h * LANES, (h + 1) * LANES)
        for j in range(n_states // LANES):
            block = [base_ref[h, j * per + i, first:, :] for i in range(per)]
            block = jnp.concatenate(block, axis=0) * scale[:, part]
            rows_ref[part, j * LANES : (j + 1) * LANES] = block.T
        rows = pl.ds(h * LANES, LANES)
        out.append(
            pltpu.make_async_copy(rows_ref.at[rows], rows_hbm.at[0, rows], out_sems.at[h])
        )
        out[-1].start()
    divisor = (n_segments * steps).astype(jnp.float32)
    rate_ref[...] = (log_scale - jnp.log(jnp.full_like(ones, n_states))) / divisor
    for copy in out:
        copy.wait()


def body(observed, pattern, trans_blocks, leave_rate, symbol_emit, cluster_emit, symbol_cluster):
    n_blocks, n_source, size, _ = trans_blocks.shape
    n_states = leave_rate.shape[0]
    steps = observed.shape[0]
    n_tm = lax.axis_size("tm")
    n_rows = n_states // lax.axis_size("rows")
    n_half = n_rows // LANES
    own = jnp.pad(observed, (0, LANES - steps)).reshape(1, 1, LANES)
    all_observed = lax.all_gather(own, "tm", axis=0, tiled=True)[:, 0, :steps]
    vmem = pl.BlockSpec(memory_space=pltpu.VMEM)
    smem = pl.BlockSpec(memory_space=pltpu.SMEM)
    hbm = pl.BlockSpec(memory_space=pltpu.HBM)
    f32, bf16 = jnp.float32, jnp.bfloat16
    sources = pattern.T
    weight, stay, stay_slab = pl.pallas_call(
        build_kernel,
        out_shape=[
            jax.ShapeDtypeStruct((n_blocks, size, n_source * size), bf16),
            jax.ShapeDtypeStruct((n_states, LANES), f32),
            jax.ShapeDtypeStruct((n_blocks, SUBLANES, LANES), f32),
        ],
        in_specs=[smem, vmem, vmem],
        out_specs=[vmem] * 3,
        scratch_shapes=[pltpu.VMEM((n_states, LANES), f32)],
        compiler_params=pltpu.CompilerParams(vmem_limit_bytes=16 << 20),
        cost_estimate=pl.CostEstimate(flops=1 << 31, bytes_accessed=4 << 20, transcendentals=0),
        name="build",
    )(sources, leave_rate.reshape(1, n_states), trans_blocks)
    return pl.pallas_call(
        chain_kernel,
        out_shape=[
            jax.ShapeDtypeStruct((1, n_rows, n_states), f32),
            jax.ShapeDtypeStruct((1, n_rows), f32),
        ],
        in_specs=[smem] * 3 + [vmem] * 5,
        out_specs=[hbm, vmem],
        scratch_shapes=[
            pltpu.VMEM((n_rows, n_states), f32),
            pltpu.VMEM((n_half, n_blocks, size + SUBLANES, LANES), f32),
            pltpu.VMEM((n_half, n_blocks, size + SUBLANES, LANES), f32),
            pltpu.VMEM((n_states, n_rows), bf16),
            pltpu.VMEM((n_states, n_rows), bf16),
            pltpu.VMEM((LANES, n_states), f32),
            pltpu.VMEM((n_states, LANES), f32),
            pltpu.VMEM((steps, n_blocks, n_tm, LANES), f32),
            [pltpu.VMEM((steps - l, n_blocks, n_tm, LANES), f32) for l in range(steps)],
            [pltpu.VMEM((steps, n_blocks, n_tm, LANES), f32) for _ in range(n_source)],
            pltpu.VMEM((n_tm, n_states), f32),
            pltpu.SemaphoreType.DMA((n_half,)),
        ],
        compiler_params=pltpu.CompilerParams(vmem_limit_bytes=32 << 20),
        cost_estimate=pl.CostEstimate(flops=1 << 34, bytes_accessed=4 << 20, transcendentals=0),
        name="chain",
    )(
        all_observed,
        sources,
        symbol_cluster,
        cluster_emit,
        symbol_emit,
        weight,
        stay,
        stay_slab,
    )


def solution(mesh):
    in_specs = (P("tm"), P(), P(), P(), P(), P(), P())
    out_specs = (P("tm", "rows", None), P("tm", "rows"))
    return jax.shard_map(body, mesh=mesh, in_specs=in_specs, out_specs=out_specs, check_vma=False)
```

```python
import functools

import jax
import jax.numpy as jnp
from jax import lax
from jax.experimental import pallas as pl
from jax.experimental.pallas import tpu as pltpu
from jax.sharding import PartitionSpec as P

LANES = 128
SUBLANES = 8


def column(row):
    return jnp.broadcast_to(row, (LANES, row.shape[1])).T


def twice(tile, at, size):
    other = pltpu.roll(tile, size, 1)
    low_half = lax.broadcasted_iota(jnp.int32, (1, LANES), 1) < size
    return jnp.where(low_half, tile, other) if at == 0 else jnp.where(low_half, other, tile)


def chain_kernel(
    observed_ref,
    pattern_hbm,
    cluster_hbm,
    leave_hbm,
    blocks_hbm,
    cluster_emit_hbm,
    symbol_hbm,
    rows_hbm,
    rate_ref,
    pattern_ref,
    cluster_ref,
    leave_ref,
    blocks_ref,
    cluster_emit_ref,
    symbol_ref,
    rows_ref,
    leave_col_ref,
    stay_ref,
    weight_ref,
    cur_ref,
    base_ref,
    low_a_ref,
    low_b_ref,
    emit_ref,
    emit_col_ref,
    change_col_ref,
    stay_slab_ref,
    emit_slab_ref,
    sum_refs,
    part_refs,
    change_ref,
    sems,
    block_sems,
    out_sems,
):
    n_tm, steps = observed_ref.shape
    n_half, n_blocks, padded, _ = cur_ref.shape
    size = blocks_ref.shape[-1]
    n_states = n_blocks * size
    n_rows = n_half * LANES
    n_source = pattern_ref.shape[0]
    first = padded - size
    n_segments = lax.axis_index("tm") + 1
    row_start = lax.axis_index("rows") * n_rows
    lows = (low_a_ref, low_b_ref)

    small = [
        pltpu.make_async_copy(source, target, sems.at[i])
        for i, (source, target) in enumerate(
            [
                (leave_hbm, leave_ref),
                (pattern_hbm, pattern_ref),
                (cluster_hbm, cluster_ref),
                (cluster_emit_hbm, cluster_emit_ref),
                (symbol_hbm, symbol_ref),
            ]
        )
    ]
    n_chunks = block_sems.shape[0]
    per_chunk = n_blocks // n_chunks
    chunks = [
        pltpu.make_async_copy(
            blocks_hbm.at[pl.ds(i * per_chunk, per_chunk)],
            blocks_ref.at[pl.ds(i * per_chunk, per_chunk)],
            block_sems.at[i],
        )
        for i in range(n_chunks)
    ]
    for copy in small[:2] + chunks + small[2:]:
        copy.start()

    def store(target_ref, low_ref, j, h, new):
        target_ref[h, j, first:, :] = new
        target_ref[h, j, :first, :] = new[size - first :, :]
        low_ref[j * size : (j + 1) * size, h * LANES : (h + 1) * LANES] = new.astype(jnp.bfloat16)

    state = lax.broadcasted_iota(jnp.int32, (size, LANES), 0)
    row = lax.broadcasted_iota(jnp.int32, (size, LANES), 1)
    for j in range(n_blocks):
        for h in range(n_half):
            start = state + j * size == row + (row_start + h * LANES)
            store(base_ref, low_a_ref, j, h, start.astype(jnp.float32))
    emit_ref[...] = jnp.zeros_like(emit_ref)
    for refs in part_refs:
        for ref in refs:
            ref[...] = jnp.zeros_like(ref)

    per = LANES // size
    low_half = lax.broadcasted_iota(jnp.int32, (1, LANES), 1) < size

    small[0].wait()
    for j in range(n_blocks):
        tile = leave_ref[:, j // per * LANES : (j // per + 1) * LANES]
        tile = jnp.broadcast_to(1.0 - tile, (n_tm, LANES))
        stay_slab_ref[j] = twice(tile, j % per, size)
    leave_col = column(leave_ref[...])
    leave_col_ref[...] = leave_col
    for j in range(n_blocks):
        own = leave_col[j * size : (j + 1) * size]
        stay_ref[j * size : (j + 1) * size, :] = 1.0 - pltpu.roll(own, 1, 0)
    small[1].wait()
    for j in range(n_blocks):
        if j % per_chunk == 0:
            chunks[j // per_chunk].wait()
        parts = []
        for k in range(n_source):
            rows = pl.ds(pl.multiple_of(pattern_ref[k, j] * size, size), size)
            parts.append(blocks_ref[j, k].astype(jnp.float32) * leave_col_ref[rows, :size])
        weight_ref[j] = jnp.concatenate(parts, axis=0).T.astype(jnp.bfloat16)
    for copy in small[2:]:
        copy.wait()

    def emission_of(g, s):
        symbol = observed_ref[g, s]
        row = symbol_ref[pl.ds(symbol, 1), :]
        return row * cluster_emit_ref[pl.ds(cluster_ref[symbol], 1), :]

    def find_changes():
        rows = n_blocks * n_tm
        stays = stay_slab_ref[...].reshape(rows, LANES)
        for s in range(steps):
            emission = jnp.concatenate([emission_of(g, s) for g in range(n_tm)], axis=0)
            for j in range(n_blocks):
                tile = emission[:, j // per * LANES : (j // per + 1) * LANES]
                emit_slab_ref[s, j] = twice(tile, j % per, size)

        def row_sums(l, p):
            return sum_refs[l][p].reshape(rows, LANES)

        for l in range(steps):
            n_pos = steps - l
            images = []
            for p in range(n_pos):
                image = emit_slab_ref[p].reshape(rows, LANES)
                if l:
                    image = image * row_sums(l - 1, p + 1)
                images.append(image)
            for j in range(n_blocks):
                own = [image[j * n_tm : (j + 1) * n_tm] for image in images]
                own = jnp.concatenate(own, axis=0)[:, :size].astype(jnp.bfloat16)
                moved = jnp.dot(own, weight_ref[j], preferred_element_type=jnp.float32)
                for k in range(n_source):
                    tile = moved[:, k // per * LANES : (k // per + 1) * LANES]
                    tile = tile.reshape(n_pos, n_tm, LANES)
                    ref = part_refs[l][k % per]
                    source = pattern_ref[k, j]
                    for p in range(n_pos):
                        ref[p, source] = ref[p, source] + tile[p]
            for p in range(n_pos):
                sides = [ref[p].reshape(rows, LANES) for ref in part_refs[l]]
                total = jnp.where(low_half, sides[0], sides[1])
                total = total + pltpu.roll(total, size, 1)
                total = total + stays * pltpu.roll(images[p], LANES - 1, 1)
                sum_refs[l][p] = total.reshape(n_blocks, n_tm, LANES)

        exact = jnp.ones((rows, LANES), jnp.float32)
        weight = exact
        deviation = []
        for s in range(steps):
            row_sum = pltpu.roll(row_sums(s, 0), 1, 1)
            for q in range(s):
                row_sum = row_sum + deviation[q] * row_sums(s - q - 1, q + 1)
                row_sum = pltpu.roll(row_sum, 1, 1)
            emission = emit_slab_ref[s].reshape(rows, LANES)
            exact = pltpu.roll(exact * stays, 1, 1) * emission
            weight = pltpu.roll(weight * stays, 1, 1) * emission
            rounded = (weight * (n_states / row_sum)).astype(jnp.bfloat16).astype(jnp.float32)
            rounded = rounded * (row_sum * (1.0 / n_states))
            deviation.append(rounded - weight)
            weight = rounded
        change = (weight - exact).reshape(n_blocks, n_tm, LANES)
        for m in range(n_states // LANES):
            tile = change[m * per + per - 1]
            for i in range(per - 1):
                tile = jnp.where(low_half, change[m * per + i], tile)
            change_ref[:, m * LANES : (m + 1) * LANES] = tile

    def segment(g, carried, is_first=False):
        scale, log_scale = carried
        for s in range(steps):
            emit_ref[s : s + 1, :] = emission_of(g, s)
        if not is_first:
            emit_ref[steps : steps + 1, :] = change_ref[pl.ds(g, 1), :]
        emit_col_ref[...] = emit_ref[...].T
        if is_first:
            find_changes()
            change_col_ref[...] = column(change_ref[:1, :])
        sums = [jnp.zeros((SUBLANES, LANES), jnp.float32) for _ in range(n_half)]
        for s in range(steps):
            now, later = lows[s % 2], lows[(s + 1) % 2]
            for j in range(n_blocks):
                states = slice(j * size, (j + 1) * size)
                picked = [
                    now[pl.ds(pl.multiple_of(pattern_ref[k, j] * size, size), size), :]
                    for k in range(n_source)
                ]
                moved = jnp.dot(
                    weight_ref[j],
                    jnp.concatenate(picked, axis=0),
                    preferred_element_type=jnp.float32,
                )
                emission = jnp.broadcast_to(emit_col_ref[states, s : s + 1], (size, LANES))
                stay = stay_ref[states, :]
                from_ref = base_ref if s == 0 else cur_ref
                to_ref = base_ref if s == steps - 1 else cur_ref
                if s == steps - 1:
                    if is_first:
                        change = change_col_ref[states, :]
                    else:
                        change = emit_col_ref[states, steps : steps + 1]
                        change = jnp.broadcast_to(change, (size, LANES))
                for h in range(n_half):
                    part = slice(h * LANES, (h + 1) * LANES)
                    kept = from_ref[h, j, first - 1 : padded - 1, :] * stay
                    new = (kept + moved[:, part]) * emission
                    if s == 0:
                        new = new * scale[:, part]
                    if s == steps - 1:
                        start = base_ref[h, j, first - steps : padded - steps, :]
                        new = new + start * change * scale[:, part]
                        sums[h] = sums[h] + jnp.sum(new.reshape(-1, SUBLANES, LANES), axis=0)
                    store(to_ref, later, j, h, new)
        if steps % 2:
            low_a_ref[...] = low_b_ref[...]
        row_sum = jnp.concatenate([jnp.sum(t, axis=0, keepdims=True) for t in sums], axis=1)
        return 1.0 / row_sum, log_scale + jnp.log(row_sum)

    ones = jnp.ones((1, n_rows), jnp.float32)
    carried = segment(0, (ones, jnp.zeros_like(ones)), is_first=True)
    scale, log_scale = lax.fori_loop(1, n_segments, segment, carried)
    scale = scale * n_states
    out = []
    for h in range(n_half):
        part = slice(h * LANES, (h + 1) * LANES)
        for j in range(n_states // LANES):
            block = [base_ref[h, j * per + i, first:, :] for i in range(per)]
            block = jnp.concatenate(block, axis=0) * scale[:, part]
            rows_ref[part, j * LANES : (j + 1) * LANES] = block.T
        rows = pl.ds(h * LANES, LANES)
        out.append(
            pltpu.make_async_copy(rows_ref.at[rows], rows_hbm.at[0, rows], out_sems.at[h])
        )
        out[-1].start()
    divisor = (n_segments * steps).astype(jnp.float32)
    rate_ref[...] = (log_scale - jnp.log(jnp.full_like(ones, n_states))) / divisor
    for copy in out:
        copy.wait()


def body(observed, pattern, trans_blocks, leave_rate, symbol_emit, cluster_emit, symbol_cluster):
    n_blocks, n_source, size, _ = trans_blocks.shape
    n_states = leave_rate.shape[0]
    steps = observed.shape[0]
    n_rows = n_states // lax.axis_size("rows")
    n_tm = lax.axis_size("tm")
    own = jnp.broadcast_to(observed[None, :], (n_tm, steps))
    all_observed = lax.all_to_all(own, "tm", 0, 0, tiled=True)
    vmem = pl.BlockSpec(memory_space=pltpu.VMEM)
    smem = pl.BlockSpec(memory_space=pltpu.SMEM)
    hbm = pl.BlockSpec(memory_space=pltpu.HBM)
    f32, bf16 = jnp.float32, jnp.bfloat16
    return pl.pallas_call(
        chain_kernel,
        out_shape=[
            jax.ShapeDtypeStruct((1, n_rows, n_states), f32),
            jax.ShapeDtypeStruct((1, n_rows), f32),
        ],
        in_specs=[smem] + [hbm] * 6,
        out_specs=[hbm, vmem],
        scratch_shapes=[
            pltpu.SMEM((n_source, n_blocks), jnp.int32),
            pltpu.SMEM(symbol_cluster.shape, jnp.int32),
            pltpu.VMEM((1, n_states), f32),
            pltpu.VMEM(trans_blocks.shape, bf16),
            pltpu.VMEM(cluster_emit.shape, f32),
            pltpu.VMEM(symbol_emit.shape, f32),
            pltpu.VMEM((n_rows, n_states), f32),
            pltpu.VMEM((n_states, LANES), f32),
            pltpu.VMEM((n_states, LANES), f32),
            pltpu.VMEM((n_blocks, size, n_source * size), bf16),
            pltpu.VMEM((n_rows // LANES, n_blocks, size + SUBLANES, LANES), f32),
            pltpu.VMEM((n_rows // LANES, n_blocks, size + SUBLANES, LANES), f32),
            pltpu.VMEM((n_states, n_rows), bf16),
            pltpu.VMEM((n_states, n_rows), bf16),
            pltpu.VMEM((LANES, n_states), f32),
            pltpu.VMEM((n_states, LANES), f32),
            pltpu.VMEM((n_states, LANES), f32),
            pltpu.VMEM((n_blocks, n_tm, LANES), f32),
            pltpu.VMEM((steps, n_blocks, n_tm, LANES), f32),
            [pltpu.VMEM((steps - l, n_blocks, n_tm, LANES), f32) for l in range(steps)],
            [
                [pltpu.VMEM((steps - l, n_blocks, n_tm, LANES), f32) for _ in range(LANES // size)]
                for l in range(steps)
            ],
            pltpu.VMEM((n_tm, n_states), f32),
            pltpu.SemaphoreType.DMA((5,)),
            pltpu.SemaphoreType.DMA((4,)),
            pltpu.SemaphoreType.DMA((n_rows // LANES,)),
        ],
        compiler_params=pltpu.CompilerParams(vmem_limit_bytes=60 << 20),
        cost_estimate=pl.CostEstimate(flops=1 << 34, bytes_accessed=4 << 20, transcendentals=0),
        name="chain",
    )(
        all_observed,
        pattern.T,
        symbol_cluster,
        leave_rate.reshape(1, n_states),
        trans_blocks,
        cluster_emit,
        symbol_emit,
    )


def solution(mesh):
    in_specs = (P("tm"), P(), P(), P(), P(), P(), P())
    out_specs = (P("tm", "rows", None), P("tm", "rows"))
    return jax.shard_map(body, mesh=mesh, in_specs=in_specs, out_specs=out_specs, check_vma=False)
```

```python
import functools

import jax
import jax.numpy as jnp
from jax import lax
from jax.experimental import pallas as pl
from jax.experimental.pallas import tpu as pltpu
from jax.sharding import PartitionSpec as P

LANES = 128
SUBLANES = 8


def column(row):
    return jnp.broadcast_to(row, (LANES, row.shape[1])).T


def twice(tile, at, size):
    other = pltpu.roll(tile, size, 1)
    low_half = lax.broadcasted_iota(jnp.int32, (1, LANES), 1) < size
    return jnp.where(low_half, tile, other) if at == 0 else jnp.where(low_half, other, tile)


def chain_kernel(
    observed_ref,
    pattern_hbm,
    cluster_hbm,
    leave_hbm,
    blocks_hbm,
    cluster_emit_hbm,
    symbol_hbm,
    rows_hbm,
    rate_ref,
    pattern_ref,
    cluster_ref,
    leave_ref,
    blocks_ref,
    cluster_emit_ref,
    symbol_ref,
    rows_ref,
    leave_col_ref,
    stay_ref,
    weight_ref,
    dense_ref,
    cur_ref,
    base_ref,
    low_a_ref,
    low_b_ref,
    emit_ref,
    emit_col_ref,
    change_col_ref,
    stay_slab_ref,
    emit_slab_ref,
    sum_refs,
    part_refs,
    change_ref,
    sems,
    block_sems,
    out_sems,
):
    n_tm, steps = observed_ref.shape
    n_half, n_blocks, padded, _ = cur_ref.shape
    size = blocks_ref.shape[-1]
    n_states = n_blocks * size
    n_rows = n_half * LANES
    n_source = pattern_ref.shape[0]
    first = padded - size
    n_segments = lax.axis_index("tm") + 1
    row_start = lax.axis_index("rows") * n_rows
    lows = (low_a_ref, low_b_ref)

    small = [
        pltpu.make_async_copy(source, target, sems.at[i])
        for i, (source, target) in enumerate(
            [
                (leave_hbm, leave_ref),
                (pattern_hbm, pattern_ref),
                (cluster_hbm, cluster_ref),
                (cluster_emit_hbm, cluster_emit_ref),
                (symbol_hbm, symbol_ref),
            ]
        )
    ]
    n_chunks = block_sems.shape[0]
    per_chunk = n_blocks // n_chunks
    chunks = [
        pltpu.make_async_copy(
            blocks_hbm.at[pl.ds(i * per_chunk, per_chunk)],
            blocks_ref.at[pl.ds(i * per_chunk, per_chunk)],
            block_sems.at[i],
        )
        for i in range(n_chunks)
    ]
    for copy in small[:2] + chunks + small[2:]:
        copy.start()

    def store(target_ref, low_ref, j, h, new):
        target_ref[h, j, first:, :] = new
        target_ref[h, j, :first, :] = new[size - first :, :]
        low_ref[j * size : (j + 1) * size, h * LANES : (h + 1) * LANES] = new.astype(jnp.bfloat16)

    state = lax.broadcasted_iota(jnp.int32, (size, LANES), 0)
    row = lax.broadcasted_iota(jnp.int32, (size, LANES), 1)
    for j in range(n_blocks):
        for h in range(n_half):
            start = state + j * size == row + (row_start + h * LANES)
            store(base_ref, low_a_ref, j, h, start.astype(jnp.float32))
    emit_ref[...] = jnp.zeros_like(emit_ref)
    dense_ref[...] = jnp.zeros_like(dense_ref)
    for refs in part_refs:
        for ref in refs:
            ref[...] = jnp.zeros_like(ref)

    per = LANES // size
    low_half = lax.broadcasted_iota(jnp.int32, (1, LANES), 1) < size

    small[0].wait()
    for j in range(n_blocks):
        tile = leave_ref[:, j // per * LANES : (j // per + 1) * LANES]
        tile = jnp.broadcast_to(1.0 - tile, (n_tm, LANES))
        stay_slab_ref[j] = twice(tile, j % per, size)
    leave_col = column(leave_ref[...])
    leave_col_ref[...] = leave_col
    for j in range(n_blocks):
        own = leave_col[j * size : (j + 1) * size]
        stay_ref[j * size : (j + 1) * size, :] = 1.0 - pltpu.roll(own, 1, 0)
    small[1].wait()
    for j in range(n_blocks):
        if j % per_chunk == 0:
            chunks[j // per_chunk].wait()
        parts = []
        for k in range(n_source):
            rows = pl.ds(pl.multiple_of(pattern_ref[k, j] * size, size), size)
            parts.append(blocks_ref[j, k].astype(jnp.float32) * leave_col_ref[rows, :size])
        moved = jnp.concatenate(parts, axis=0).T.astype(jnp.bfloat16)
        weight_ref[j] = moved
        states = slice(j * size, (j + 1) * size)
        moved = moved.astype(jnp.float32)
        for k in range(n_source):
            source = pattern_ref[k, j]
            tile = twice(moved[:, k // per * LANES : (k // per + 1) * LANES], k % per, size)
            tile = jnp.where(low_half == (source % per == 0), tile, 0.0).astype(jnp.bfloat16)
            dense_ref[source // per, states, :] = dense_ref[source // per, states, :] + tile
    for copy in small[2:]:
        copy.wait()

    def emission_of(g, s):
        symbol = observed_ref[g, s]
        row = symbol_ref[pl.ds(symbol, 1), :]
        return row * cluster_emit_ref[pl.ds(cluster_ref[symbol], 1), :]

    def find_changes():
        rows = n_blocks * n_tm
        stays = stay_slab_ref[...].reshape(rows, LANES)
        for s in range(steps):
            emission = jnp.concatenate([emission_of(g, s) for g in range(n_tm)], axis=0)
            for j in range(n_blocks):
                tile = emission[:, j // per * LANES : (j // per + 1) * LANES]
                emit_slab_ref[s, j] = twice(tile, j % per, size)

        def row_sums(l, p):
            return sum_refs[l][p].reshape(rows, LANES)

        for l in range(steps):
            n_pos = steps - l
            images = []
            for p in range(n_pos):
                image = emit_slab_ref[p].reshape(rows, LANES)
                if l:
                    image = image * row_sums(l - 1, p + 1)
                images.append(image)
            for j in range(n_blocks):
                own = [image[j * n_tm : (j + 1) * n_tm] for image in images]
                own = jnp.concatenate(own, axis=0)[:, :size].astype(jnp.bfloat16)
                moved = jnp.dot(own, weight_ref[j], preferred_element_type=jnp.float32)
                for k in range(n_source):
                    tile = moved[:, k // per * LANES : (k // per + 1) * LANES]
                    tile = tile.reshape(n_pos, n_tm, LANES)
                    ref = part_refs[l][k % per]
                    source = pattern_ref[k, j]
                    for p in range(n_pos):
                        ref[p, source] = ref[p, source] + tile[p]
            for p in range(n_pos):
                sides = [ref[p].reshape(rows, LANES) for ref in part_refs[l]]
                total = jnp.where(low_half, sides[0], sides[1])
                total = total + pltpu.roll(total, size, 1)
                total = total + stays * pltpu.roll(images[p], LANES - 1, 1)
                sum_refs[l][p] = total.reshape(n_blocks, n_tm, LANES)

        exact = jnp.ones((rows, LANES), jnp.float32)
        weight = exact
        deviation = []
        for s in range(steps):
            row_sum = pltpu.roll(row_sums(s, 0), 1, 1)
            for q in range(s):
                row_sum = row_sum + deviation[q] * row_sums(s - q - 1, q + 1)
                row_sum = pltpu.roll(row_sum, 1, 1)
            emission = emit_slab_ref[s].reshape(rows, LANES)
            exact = pltpu.roll(exact * stays, 1, 1) * emission
            weight = pltpu.roll(weight * stays, 1, 1) * emission
            rounded = (weight * (n_states / row_sum)).astype(jnp.bfloat16).astype(jnp.float32)
            rounded = rounded * (row_sum * (1.0 / n_states))
            deviation.append(rounded - weight)
            weight = rounded
        change = (weight - exact).reshape(n_blocks, n_tm, LANES)
        for m in range(n_states // LANES):
            tile = change[m * per + per - 1]
            for i in range(per - 1):
                tile = jnp.where(low_half, change[m * per + i], tile)
            change_ref[:, m * LANES : (m + 1) * LANES] = tile

    def segment(g, carried, is_first=False):
        scale, log_scale = carried
        for s in range(steps):
            emit_ref[s : s + 1, :] = emission_of(g, s)
        if not is_first:
            emit_ref[steps : steps + 1, :] = change_ref[pl.ds(g, 1), :]
        emit_col_ref[...] = emit_ref[...].T
        if is_first:
            find_changes()
            change_col_ref[...] = column(change_ref[:1, :])
        sums = [jnp.zeros((SUBLANES, LANES), jnp.float32) for _ in range(n_half)]
        for s in range(steps):
            now, later = lows[s % 2], lows[(s + 1) % 2]
            dense = jnp.concatenate([dense_ref[m] for m in range(n_states // LANES)], axis=1)
            all_moved = jnp.dot(dense, now[...], preferred_element_type=jnp.float32)
            for j in range(n_blocks):
                states = slice(j * size, (j + 1) * size)
                moved = all_moved[states, :]
                emission = jnp.broadcast_to(emit_col_ref[states, s : s + 1], (size, LANES))
                stay = stay_ref[states, :]
                from_ref = base_ref if s == 0 else cur_ref
                to_ref = base_ref if s == steps - 1 else cur_ref
                if s == steps - 1:
                    if is_first:
                        change = change_col_ref[states, :]
                    else:
                        change = emit_col_ref[states, steps : steps + 1]
                        change = jnp.broadcast_to(change, (size, LANES))
                for h in range(n_half):
                    part = slice(h * LANES, (h + 1) * LANES)
                    kept = from_ref[h, j, first - 1 : padded - 1, :] * stay
                    new = (kept + moved[:, part]) * emission
                    if s == 0:
                        new = new * scale[:, part]
                    if s == steps - 1:
                        start = base_ref[h, j, first - steps : padded - steps, :]
                        new = new + start * change * scale[:, part]
                        sums[h] = sums[h] + jnp.sum(new.reshape(-1, SUBLANES, LANES), axis=0)
                    store(to_ref, later, j, h, new)
        if steps % 2:
            low_a_ref[...] = low_b_ref[...]
        row_sum = jnp.concatenate([jnp.sum(t, axis=0, keepdims=True) for t in sums], axis=1)
        return 1.0 / row_sum, log_scale + jnp.log(row_sum)

    ones = jnp.ones((1, n_rows), jnp.float32)
    carried = segment(0, (ones, jnp.zeros_like(ones)), is_first=True)
    scale, log_scale = lax.fori_loop(1, n_segments, segment, carried)
    scale = scale * n_states
    out = []
    for h in range(n_half):
        part = slice(h * LANES, (h + 1) * LANES)
        for j in range(n_states // LANES):
            block = [base_ref[h, j * per + i, first:, :] for i in range(per)]
            block = jnp.concatenate(block, axis=0) * scale[:, part]
            rows_ref[part, j * LANES : (j + 1) * LANES] = block.T
        rows = pl.ds(h * LANES, LANES)
        out.append(
            pltpu.make_async_copy(rows_ref.at[rows], rows_hbm.at[0, rows], out_sems.at[h])
        )
        out[-1].start()
    divisor = (n_segments * steps).astype(jnp.float32)
    rate_ref[...] = (log_scale - jnp.log(jnp.full_like(ones, n_states))) / divisor
    for copy in out:
        copy.wait()


def body(observed, pattern, trans_blocks, leave_rate, symbol_emit, cluster_emit, symbol_cluster):
    n_blocks, n_source, size, _ = trans_blocks.shape
    n_states = leave_rate.shape[0]
    steps = observed.shape[0]
    n_rows = n_states // lax.axis_size("rows")
    n_tm = lax.axis_size("tm")
    own = jnp.broadcast_to(observed[None, :], (n_tm, steps))
    all_observed = lax.all_to_all(own, "tm", 0, 0, tiled=True)
    vmem = pl.BlockSpec(memory_space=pltpu.VMEM)
    smem = pl.BlockSpec(memory_space=pltpu.SMEM)
    hbm = pl.BlockSpec(memory_space=pltpu.HBM)
    f32, bf16 = jnp.float32, jnp.bfloat16
    return pl.pallas_call(
        chain_kernel,
        out_shape=[
            jax.ShapeDtypeStruct((1, n_rows, n_states), f32),
            jax.ShapeDtypeStruct((1, n_rows), f32),
        ],
        in_specs=[smem] + [hbm] * 6,
        out_specs=[hbm, vmem],
        scratch_shapes=[
            pltpu.SMEM((n_source, n_blocks), jnp.int32),
            pltpu.SMEM(symbol_cluster.shape, jnp.int32),
            pltpu.VMEM((1, n_states), f32),
            pltpu.VMEM(trans_blocks.shape, bf16),
            pltpu.VMEM(cluster_emit.shape, f32),
            pltpu.VMEM(symbol_emit.shape, f32),
            pltpu.VMEM((n_rows, n_states), f32),
            pltpu.VMEM((n_states, LANES), f32),
            pltpu.VMEM((n_states, LANES), f32),
            pltpu.VMEM((n_blocks, size, n_source * size), bf16),
            pltpu.VMEM((n_states // LANES, n_states, LANES), bf16),
            pltpu.VMEM((n_rows // LANES, n_blocks, size + SUBLANES, LANES), f32),
            pltpu.VMEM((n_rows // LANES, n_blocks, size + SUBLANES, LANES), f32),
            pltpu.VMEM((n_states, n_rows), bf16),
            pltpu.VMEM((n_states, n_rows), bf16),
            pltpu.VMEM((LANES, n_states), f32),
            pltpu.VMEM((n_states, LANES), f32),
            pltpu.VMEM((n_states, LANES), f32),
            pltpu.VMEM((n_blocks, n_tm, LANES), f32),
            pltpu.VMEM((steps, n_blocks, n_tm, LANES), f32),
            [pltpu.VMEM((steps - l, n_blocks, n_tm, LANES), f32) for l in range(steps)],
            [
                [pltpu.VMEM((steps - l, n_blocks, n_tm, LANES), f32) for _ in range(LANES // size)]
                for l in range(steps)
            ],
            pltpu.VMEM((n_tm, n_states), f32),
            pltpu.SemaphoreType.DMA((5,)),
            pltpu.SemaphoreType.DMA((4,)),
            pltpu.SemaphoreType.DMA((n_rows // LANES,)),
        ],
        compiler_params=pltpu.CompilerParams(vmem_limit_bytes=60 << 20),
        cost_estimate=pl.CostEstimate(flops=1 << 34, bytes_accessed=4 << 20, transcendentals=0),
        name="chain",
    )(
        all_observed,
        pattern.T,
        symbol_cluster,
        leave_rate.reshape(1, n_states),
        trans_blocks,
        cluster_emit,
        symbol_emit,
    )


def solution(mesh):
    in_specs = (P("tm"), P(), P(), P(), P(), P(), P())
    out_specs = (P("tm", "rows", None), P("tm", "rows"))
    return jax.shard_map(body, mesh=mesh, in_specs=in_specs, out_specs=out_specs, check_vma=False)
```

```python
import functools

import jax
import jax.numpy as jnp
from jax import lax
from jax.experimental import pallas as pl
from jax.experimental.pallas import tpu as pltpu
from jax.sharding import PartitionSpec as P

LANES = 128
SUBLANES = 8


def column(row):
    return jnp.broadcast_to(row, (LANES, row.shape[1])).T


def twice(tile, at, size):
    other = pltpu.roll(tile, size, 1)
    low_half = lax.broadcasted_iota(jnp.int32, (1, LANES), 1) < size
    return jnp.where(low_half, tile, other) if at == 0 else jnp.where(low_half, other, tile)


def chain_kernel(
    observed_ref,
    pattern_hbm,
    cluster_hbm,
    leave_hbm,
    blocks_hbm,
    cluster_emit_hbm,
    symbol_hbm,
    rows_hbm,
    rate_ref,
    pattern_ref,
    cluster_ref,
    leave_ref,
    blocks_ref,
    cluster_emit_ref,
    symbol_ref,
    rows_ref,
    leave_col_ref,
    stay_ref,
    weight_ref,
    stored_ref,
    half_ref,
    cur_ref,
    base_ref,
    low_a_ref,
    low_b_ref,
    emit_ref,
    emit_col_ref,
    change_col_ref,
    stay_slab_ref,
    emit_slab_ref,
    sum_refs,
    part_refs,
    change_ref,
    sems,
    block_sems,
    out_sems,
):
    n_tm, steps = observed_ref.shape
    n_half, n_blocks, padded, _ = cur_ref.shape
    size = blocks_ref.shape[-1]
    n_states = n_blocks * size
    n_rows = n_half * LANES
    n_source = pattern_ref.shape[0]
    first = padded - size
    groups = size // SUBLANES
    n_segments = lax.axis_index("tm") + 1
    row_start = lax.axis_index("rows") * n_rows
    lows = (low_a_ref, low_b_ref)

    small = [
        pltpu.make_async_copy(source, target, sems.at[i])
        for i, (source, target) in enumerate(
            [
                (leave_hbm, leave_ref),
                (pattern_hbm, pattern_ref),
                (cluster_hbm, cluster_ref),
                (cluster_emit_hbm, cluster_emit_ref),
                (symbol_hbm, symbol_ref),
            ]
        )
    ]
    n_chunks = block_sems.shape[0]
    per_chunk = n_blocks // n_chunks
    chunks = [
        pltpu.make_async_copy(
            blocks_hbm.at[pl.ds(i * per_chunk, per_chunk)],
            blocks_ref.at[pl.ds(i * per_chunk, per_chunk)],
            block_sems.at[i],
        )
        for i in range(n_chunks)
    ]
    for copy in small[:2] + chunks + small[2:]:
        copy.start()

    def store(target_ref, low_ref, j, h, new, ahead):
        target_ref[h, j, first:, :] = new
        for m in range(1, ahead + 1):
            group = new[size - m * SUBLANES : size - (m - 1) * SUBLANES, :]
            at = first - m * SUBLANES
            target_ref[h, j, at : at + SUBLANES, :] = pltpu.roll(group, 1, 0)
        low_ref[j * size : (j + 1) * size, h * LANES : (h + 1) * LANES] = new.astype(jnp.bfloat16)

    def stored_order(ref, j):
        rows = [ref[pl.ds(j * size + m, SUBLANES, stride=groups), :] for m in range(groups)]
        return jnp.concatenate(rows, axis=0)

    state = lax.broadcasted_iota(jnp.int32, (size, LANES), 0)
    state = state % SUBLANES * groups + state // SUBLANES
    row = lax.broadcasted_iota(jnp.int32, (size, LANES), 1)
    for j in range(n_blocks):
        for h in range(n_half):
            start = state + j * size == row + (row_start + h * LANES)
            store(base_ref, low_a_ref, j, h, start.astype(jnp.float32), steps)
    emit_ref[...] = jnp.zeros_like(emit_ref)
    for refs in part_refs:
        for ref in refs:
            ref[...] = jnp.zeros_like(ref)

    per = LANES // size
    low_half = lax.broadcasted_iota(jnp.int32, (1, LANES), 1) < size

    small[0].wait()
    for j in range(n_blocks):
        tile = leave_ref[:, j // per * LANES : (j // per + 1) * LANES]
        tile = jnp.broadcast_to(1.0 - tile, (n_tm, LANES))
        stay_slab_ref[j] = twice(tile, j % per, size)
    leave_col = column(leave_ref[...])
    leave_col_ref[...] = leave_col
    for j in range(n_blocks):
        own = leave_col[j * size : (j + 1) * size]
        emit_col_ref[j * size : (j + 1) * size, :] = 1.0 - pltpu.roll(own, 1, 0)
    for j in range(n_blocks):
        stay_ref[j * size : (j + 1) * size, :] = stored_order(emit_col_ref, j)
    row = lax.broadcasted_iota(jnp.int32, (size, size), 0)
    col = lax.broadcasted_iota(jnp.int32, (size, size), 1)
    to_stored = (col == row % SUBLANES * groups + row // SUBLANES).astype(jnp.float32)
    to_stored = to_stored.astype(jnp.bfloat16)
    small[1].wait()
    for j in range(n_blocks):
        if j % per_chunk == 0:
            chunks[j // per_chunk].wait()
        parts = []
        for k in range(n_source):
            rows = pl.ds(pl.multiple_of(pattern_ref[k, j] * size, size), size)
            parts.append(blocks_ref[j, k].astype(jnp.float32) * leave_col_ref[rows, :size])
        weight = jnp.concatenate(parts, axis=0).T.astype(jnp.bfloat16)
        weight_ref[j] = weight
        weight = jnp.dot(to_stored, weight, preferred_element_type=jnp.float32)
        half_ref[j * size : (j + 1) * size, :] = weight.astype(jnp.bfloat16)
    width = n_source * size
    row = lax.broadcasted_iota(jnp.int32, (width, width), 0)
    col = lax.broadcasted_iota(jnp.int32, (width, width), 1)
    source = col // size * size + col % SUBLANES * groups + col % size // SUBLANES
    from_stored = (row == source).astype(jnp.float32).astype(jnp.bfloat16)
    stored = jnp.dot(half_ref[...], from_stored, preferred_element_type=jnp.float32)
    stored_ref[...] = stored.astype(jnp.bfloat16)
    for copy in small[2:]:
        copy.wait()

    def emission_of(g, s):
        symbol = observed_ref[g, s]
        row = symbol_ref[pl.ds(symbol, 1), :]
        return row * cluster_emit_ref[pl.ds(cluster_ref[symbol], 1), :]

    def find_changes():
        rows = n_blocks * n_tm
        stays = stay_slab_ref[...].reshape(rows, LANES)
        for s in range(steps):
            emission = jnp.concatenate([emission_of(g, s) for g in range(n_tm)], axis=0)
            for j in range(n_blocks):
                tile = emission[:, j // per * LANES : (j // per + 1) * LANES]
                emit_slab_ref[s, j] = twice(tile, j % per, size)

        def row_sums(l, p):
            return sum_refs[l][p].reshape(rows, LANES)

        for l in range(steps):
            n_pos = steps - l
            images = []
            for p in range(n_pos):
                image = emit_slab_ref[p].reshape(rows, LANES)
                if l:
                    image = image * row_sums(l - 1, p + 1)
                images.append(image)
            for j in range(n_blocks):
                own = [image[j * n_tm : (j + 1) * n_tm] for image in images]
                own = jnp.concatenate(own, axis=0)[:, :size].astype(jnp.bfloat16)
                moved = jnp.dot(own, weight_ref[j], preferred_element_type=jnp.float32)
                for k in range(n_source):
                    tile = moved[:, k // per * LANES : (k // per + 1) * LANES]
                    tile = tile.reshape(n_pos, n_tm, LANES)
                    ref = part_refs[l][k % per]
                    source = pattern_ref[k, j]
                    for p in range(n_pos):
                        ref[p, source] = ref[p, source] + tile[p]
            for p in range(n_pos):
                sides = [ref[p].reshape(rows, LANES) for ref in part_refs[l]]
                total = jnp.where(low_half, sides[0], sides[1])
                total = total + pltpu.roll(total, size, 1)
                total = total + stays * pltpu.roll(images[p], LANES - 1, 1)
                sum_refs[l][p] = total.reshape(n_blocks, n_tm, LANES)

        exact = jnp.ones((rows, LANES), jnp.float32)
        weight = exact
        deviation = []
        for s in range(steps):
            row_sum = pltpu.roll(row_sums(s, 0), 1, 1)
            for q in range(s):
                row_sum = row_sum + deviation[q] * row_sums(s - q - 1, q + 1)
                row_sum = pltpu.roll(row_sum, 1, 1)
            emission = emit_slab_ref[s].reshape(rows, LANES)
            exact = pltpu.roll(exact * stays, 1, 1) * emission
            weight = pltpu.roll(weight * stays, 1, 1) * emission
            rounded = (weight * (n_states / row_sum)).astype(jnp.bfloat16).astype(jnp.float32)
            rounded = rounded * (row_sum * (1.0 / n_states))
            deviation.append(rounded - weight)
            weight = rounded
        change = (weight - exact).reshape(n_blocks, n_tm, LANES)
        for m in range(n_states // LANES):
            tile = change[m * per + per - 1]
            for i in range(per - 1):
                tile = jnp.where(low_half, change[m * per + i], tile)
            change_ref[:, m * LANES : (m + 1) * LANES] = tile

    def segment(g, carried, is_first=False):
        scale, log_scale = carried
        for s in range(steps):
            emit_ref[s : s + 1, :] = emission_of(g, s)
        if not is_first:
            emit_ref[steps : steps + 1, :] = change_ref[pl.ds(g, 1), :]
        emit_col_ref[...] = emit_ref[...].T
        if is_first:
            find_changes()
            change_col_ref[...] = column(change_ref[:1, :])
        sums = [jnp.zeros((SUBLANES, LANES), jnp.float32) for _ in range(n_half)]
        for s in range(steps):
            now, later = lows[s % 2], lows[(s + 1) % 2]
            for j in range(n_blocks):
                states = slice(j * size, (j + 1) * size)
                picked = [
                    now[pl.ds(pl.multiple_of(pattern_ref[k, j] * size, size), size), :]
                    for k in range(n_source)
                ]
                moved = jnp.dot(
                    stored_ref[states, :],
                    jnp.concatenate(picked, axis=0),
                    preferred_element_type=jnp.float32,
                )
                columns = stored_order(emit_col_ref, j)
                emission = jnp.broadcast_to(columns[:, s : s + 1], (size, LANES))
                stay = stay_ref[states, :]
                from_ref = base_ref if s == 0 else cur_ref
                to_ref = base_ref if s == steps - 1 else cur_ref
                if s == steps - 1:
                    if is_first:
                        change = stored_order(change_col_ref, j)
                    else:
                        change = jnp.broadcast_to(columns[:, steps : steps + 1], (size, LANES))
                for h in range(n_half):
                    part = slice(h * LANES, (h + 1) * LANES)
                    kept = from_ref[h, j, first - SUBLANES : padded - SUBLANES, :] * stay
                    new = (kept + moved[:, part]) * emission
                    if s == 0:
                        new = new * scale[:, part]
                    if s == steps - 1:
                        start = base_ref[h, j, first - steps * SUBLANES : padded - steps * SUBLANES, :]
                        new = new + start * change * scale[:, part]
                        sums[h] = sums[h] + jnp.sum(new.reshape(-1, SUBLANES, LANES), axis=0)
                    store(to_ref, later, j, h, new, steps if to_ref is base_ref else 1)
        if steps % 2:
            low_a_ref[...] = low_b_ref[...]
        row_sum = jnp.concatenate([jnp.sum(t, axis=0, keepdims=True) for t in sums], axis=1)
        return 1.0 / row_sum, log_scale + jnp.log(row_sum)

    ones = jnp.ones((1, n_rows), jnp.float32)
    carried = segment(0, (ones, jnp.zeros_like(ones)), is_first=True)
    scale, log_scale = lax.fori_loop(1, n_segments, segment, carried)
    scale = scale * n_states
    out = []
    for h in range(n_half):
        part = slice(h * LANES, (h + 1) * LANES)
        for j in range(n_states // LANES):
            block = [
                base_ref[h, j * per + i, pl.ds(first + q, groups, stride=SUBLANES), :]
                for i in range(per)
                for q in range(SUBLANES)
            ]
            block = jnp.concatenate(block, axis=0) * scale[:, part]
            rows_ref[part, j * LANES : (j + 1) * LANES] = block.T
        rows = pl.ds(h * LANES, LANES)
        out.append(
            pltpu.make_async_copy(rows_ref.at[rows], rows_hbm.at[0, rows], out_sems.at[h])
        )
        out[-1].start()
    divisor = (n_segments * steps).astype(jnp.float32)
    rate_ref[...] = (log_scale - jnp.log(jnp.full_like(ones, n_states))) / divisor
    for copy in out:
        copy.wait()


def body(observed, pattern, trans_blocks, leave_rate, symbol_emit, cluster_emit, symbol_cluster):
    n_blocks, n_source, size, _ = trans_blocks.shape
    n_states = leave_rate.shape[0]
    steps = observed.shape[0]
    n_rows = n_states // lax.axis_size("rows")
    n_tm = lax.axis_size("tm")
    own = jnp.broadcast_to(observed[None, :], (n_tm, steps))
    all_observed = lax.all_to_all(own, "tm", 0, 0, tiled=True)
    vmem = pl.BlockSpec(memory_space=pltpu.VMEM)
    smem = pl.BlockSpec(memory_space=pltpu.SMEM)
    hbm = pl.BlockSpec(memory_space=pltpu.HBM)
    f32, bf16 = jnp.float32, jnp.bfloat16
    return pl.pallas_call(
        chain_kernel,
        out_shape=[
            jax.ShapeDtypeStruct((1, n_rows, n_states), f32),
            jax.ShapeDtypeStruct((1, n_rows), f32),
        ],
        in_specs=[smem] + [hbm] * 6,
        out_specs=[hbm, vmem],
        scratch_shapes=[
            pltpu.SMEM((n_source, n_blocks), jnp.int32),
            pltpu.SMEM(symbol_cluster.shape, jnp.int32),
            pltpu.VMEM((1, n_states), f32),
            pltpu.VMEM(trans_blocks.shape, bf16),
            pltpu.VMEM(cluster_emit.shape, f32),
            pltpu.VMEM(symbol_emit.shape, f32),
            pltpu.VMEM((n_rows, n_states), f32),
            pltpu.VMEM((n_states, LANES), f32),
            pltpu.VMEM((n_states, LANES), f32),
            pltpu.VMEM((n_blocks, size, n_source * size), bf16),
            pltpu.VMEM((n_states, n_source * size), bf16),
            pltpu.VMEM((n_states, n_source * size), bf16),
            pltpu.VMEM((n_rows // LANES, n_blocks, size + steps * SUBLANES, LANES), f32),
            pltpu.VMEM((n_rows // LANES, n_blocks, size + steps * SUBLANES, LANES), f32),
            pltpu.VMEM((n_states, n_rows), bf16),
            pltpu.VMEM((n_states, n_rows), bf16),
            pltpu.VMEM((LANES, n_states), f32),
            pltpu.VMEM((n_states, LANES), f32),
            pltpu.VMEM((n_states, LANES), f32),
            pltpu.VMEM((n_blocks, n_tm, LANES), f32),
            pltpu.VMEM((steps, n_blocks, n_tm, LANES), f32),
            [pltpu.VMEM((steps - l, n_blocks, n_tm, LANES), f32) for l in range(steps)],
            [
                [pltpu.VMEM((steps - l, n_blocks, n_tm, LANES), f32) for _ in range(LANES // size)]
                for l in range(steps)
            ],
            pltpu.VMEM((n_tm, n_states), f32),
            pltpu.SemaphoreType.DMA((5,)),
            pltpu.SemaphoreType.DMA((4,)),
            pltpu.SemaphoreType.DMA((n_rows // LANES,)),
        ],
        compiler_params=pltpu.CompilerParams(vmem_limit_bytes=60 << 20),
        cost_estimate=pl.CostEstimate(flops=1 << 34, bytes_accessed=4 << 20, transcendentals=0),
        name="chain",
    )(
        all_observed,
        pattern.T,
        symbol_cluster,
        leave_rate.reshape(1, n_states),
        trans_blocks,
        cluster_emit,
        symbol_emit,
    )


def solution(mesh):
    in_specs = (P("tm"), P(), P(), P(), P(), P(), P())
    out_specs = (P("tm", "rows", None), P("tm", "rows"))
    return jax.shard_map(body, mesh=mesh, in_specs=in_specs, out_specs=out_specs, check_vma=False)
```

```python
import functools

import jax
import jax.numpy as jnp
from jax import lax
from jax.experimental import pallas as pl
from jax.experimental.pallas import tpu as pltpu
from jax.sharding import PartitionSpec as P

LANES = 128
SUBLANES = 8


def column(row):
    return jnp.broadcast_to(row, (LANES, row.shape[1])).T


def twice(tile, at, size):
    other = pltpu.roll(tile, size, 1)
    low_half = lax.broadcasted_iota(jnp.int32, (1, LANES), 1) < size
    return jnp.where(low_half, tile, other) if at == 0 else jnp.where(low_half, other, tile)


def build_kernel(
    pattern_ref, leave_ref, blocks_ref, weight_ref, stay_ref, stay_slab_ref, leave_col_ref
):
    n_blocks, n_source, size, _ = blocks_ref.shape
    per = LANES // size
    for j in range(n_blocks):
        tile = leave_ref[:, j // per * LANES : (j // per + 1) * LANES]
        tile = jnp.broadcast_to(1.0 - tile, stay_slab_ref.shape[1:])
        stay_slab_ref[j] = twice(tile, j % per, size)
    leave_col = column(leave_ref[...])
    leave_col_ref[...] = leave_col
    for j in range(n_blocks):
        own = leave_col[j * size : (j + 1) * size]
        stay_ref[j * size : (j + 1) * size, :] = 1.0 - pltpu.roll(own, 1, 0)
    for j in range(n_blocks):
        parts = []
        for k in range(n_source):
            rows = pl.ds(pl.multiple_of(pattern_ref[k, j] * size, size), size)
            parts.append(blocks_ref[j, k].astype(jnp.float32) * leave_col_ref[rows, :size])
        weight_ref[j] = jnp.concatenate(parts, axis=0).T.astype(jnp.bfloat16)


def chain_kernel(
    observed_ref,
    pattern_ref,
    cluster_ref,
    cluster_emit_ref,
    symbol_ref,
    weight_ref,
    stay_ref,
    stay_slab_ref,
    rows_hbm,
    rate_ref,
    rows_ref,
    cur_ref,
    base_ref,
    low_a_ref,
    low_b_ref,
    emit_ref,
    emit_col_ref,
    change_col_ref,
    emit_slab_ref,
    sum_refs,
    part_refs,
    change_ref,
    out_sems,
):
    n_tm, steps = observed_ref.shape
    n_half, n_blocks, padded, _ = cur_ref.shape
    size = weight_ref.shape[1]
    n_states = n_blocks * size
    n_rows = n_half * LANES
    n_source = pattern_ref.shape[0]
    first = padded - size
    n_segments = lax.axis_index("tm") + 1
    row_start = lax.axis_index("rows") * n_rows
    lows = (low_a_ref, low_b_ref)

    def store(target_ref, low_ref, j, h, new):
        target_ref[h, j, first:, :] = new
        target_ref[h, j, :first, :] = new[size - first :, :]
        low_ref[j * size : (j + 1) * size, h * LANES : (h + 1) * LANES] = new.astype(jnp.bfloat16)

    state = lax.broadcasted_iota(jnp.int32, (size, LANES), 0)
    row = lax.broadcasted_iota(jnp.int32, (size, LANES), 1)
    for j in range(n_blocks):
        for h in range(n_half):
            start = state + j * size == row + (row_start + h * LANES)
            store(base_ref, low_a_ref, j, h, start.astype(jnp.float32))
    emit_ref[...] = jnp.zeros_like(emit_ref)
    for refs in part_refs:
        for ref in refs:
            ref[...] = jnp.zeros_like(ref)

    per = LANES // size
    low_half = lax.broadcasted_iota(jnp.int32, (1, LANES), 1) < size

    def emission_of(g, s):
        symbol = observed_ref[(n_segments - 1 - g + n_tm) % n_tm, s]
        row = symbol_ref[pl.ds(symbol, 1), :]
        return row * cluster_emit_ref[pl.ds(cluster_ref[symbol], 1), :]

    def find_changes():
        rows = n_blocks * n_tm
        stays = stay_slab_ref[...].reshape(rows, LANES)
        for s in range(steps):
            emission = jnp.concatenate([emission_of(g, s) for g in range(n_tm)], axis=0)
            for j in range(n_blocks):
                tile = emission[:, j // per * LANES : (j // per + 1) * LANES]
                emit_slab_ref[s, j] = twice(tile, j % per, size)

        def row_sums(l, p):
            return sum_refs[l][p].reshape(rows, LANES)

        for l in range(steps):
            n_pos = steps - l
            images = []
            for p in range(n_pos):
                image = emit_slab_ref[p].reshape(rows, LANES)
                if l:
                    image = image * row_sums(l - 1, p + 1)
                images.append(image)
            for j in range(n_blocks):
                own = [image[j * n_tm : (j + 1) * n_tm] for image in images]
                own = jnp.concatenate(own, axis=0)[:, :size].astype(jnp.bfloat16)
                moved = jnp.dot(own, weight_ref[j], preferred_element_type=jnp.float32)
                for k in range(n_source):
                    tile = moved[:, k // per * LANES : (k // per + 1) * LANES]
                    tile = tile.reshape(n_pos, n_tm, LANES)
                    ref = part_refs[l][k % per]
                    source = pattern_ref[k, j]
                    for p in range(n_pos):
                        ref[p, source] = ref[p, source] + tile[p]
            for p in range(n_pos):
                sides = [ref[p].reshape(rows, LANES) for ref in part_refs[l]]
                total = jnp.where(low_half, sides[0], sides[1])
                total = total + pltpu.roll(total, size, 1)
                total = total + stays * pltpu.roll(images[p], LANES - 1, 1)
                sum_refs[l][p] = total.reshape(n_blocks, n_tm, LANES)

        exact = jnp.ones((rows, LANES), jnp.float32)
        weight = exact
        deviation = []
        for s in range(steps):
            row_sum = pltpu.roll(row_sums(s, 0), 1, 1)
            for q in range(s):
                row_sum = row_sum + deviation[q] * row_sums(s - q - 1, q + 1)
                row_sum = pltpu.roll(row_sum, 1, 1)
            emission = emit_slab_ref[s].reshape(rows, LANES)
            exact = pltpu.roll(exact * stays, 1, 1) * emission
            weight = pltpu.roll(weight * stays, 1, 1) * emission
            rounded = (weight * (n_states / row_sum)).astype(jnp.bfloat16).astype(jnp.float32)
            rounded = rounded * (row_sum * (1.0 / n_states))
            deviation.append(rounded - weight)
            weight = rounded
        change = (weight - exact).reshape(n_blocks, n_tm, LANES)
        for m in range(n_states // LANES):
            tile = change[m * per + per - 1]
            for i in range(per - 1):
                tile = jnp.where(low_half, change[m * per + i], tile)
            change_ref[:, m * LANES : (m + 1) * LANES] = tile

    def segment(g, carried, is_first=False):
        scale, log_scale = carried
        for s in range(steps):
            emit_ref[s : s + 1, :] = emission_of(g, s)
        if not is_first:
            emit_ref[steps : steps + 1, :] = change_ref[pl.ds(g, 1), :]
        emit_col_ref[...] = emit_ref[...].T
        if is_first:
            find_changes()
            change_col_ref[...] = column(change_ref[:1, :])
        sums = [jnp.zeros((SUBLANES, LANES), jnp.float32) for _ in range(n_half)]
        for s in range(steps):
            now, later = lows[s % 2], lows[(s + 1) % 2]
            for j in range(n_blocks):
                states = slice(j * size, (j + 1) * size)
                picked = [
                    now[pl.ds(pl.multiple_of(pattern_ref[k, j] * size, size), size), :]
                    for k in range(n_source)
                ]
                moved = jnp.dot(
                    weight_ref[j],
                    jnp.concatenate(picked, axis=0),
                    preferred_element_type=jnp.float32,
                )
                emission = jnp.broadcast_to(emit_col_ref[states, s : s + 1], (size, LANES))
                stay = stay_ref[states, :]
                from_ref = base_ref if s == 0 else cur_ref
                to_ref = base_ref if s == steps - 1 else cur_ref
                if s == steps - 1:
                    if is_first:
                        change = change_col_ref[states, :]
                    else:
                        change = emit_col_ref[states, steps : steps + 1]
                        change = jnp.broadcast_to(change, (size, LANES))
                for h in range(n_half):
                    part = slice(h * LANES, (h + 1) * LANES)
                    kept = from_ref[h, j, first - 1 : padded - 1, :] * stay
                    new = (kept + moved[:, part]) * emission
                    if s == 0:
                        new = new * scale[:, part]
                    if s == steps - 1:
                        start = base_ref[h, j, first - steps : padded - steps, :]
                        new = new + start * change * scale[:, part]
                        sums[h] = sums[h] + jnp.sum(new.reshape(-1, SUBLANES, LANES), axis=0)
                    store(to_ref, later, j, h, new)
        if steps % 2:
            low_a_ref[...] = low_b_ref[...]
        row_sum = jnp.concatenate([jnp.sum(t, axis=0, keepdims=True) for t in sums], axis=1)
        return 1.0 / row_sum, log_scale + jnp.log(row_sum)

    ones = jnp.ones((1, n_rows), jnp.float32)
    carried = segment(0, (ones, jnp.zeros_like(ones)), is_first=True)
    scale, log_scale = lax.fori_loop(1, n_segments, segment, carried)
    scale = scale * n_states
    out = []
    for h in range(n_half):
        part = slice(h * LANES, (h + 1) * LANES)
        for j in range(n_states // LANES):
            block = [base_ref[h, j * per + i, first:, :] for i in range(per)]
            block = jnp.concatenate(block, axis=0) * scale[:, part]
            rows_ref[part, j * LANES : (j + 1) * LANES] = block.T
        rows = pl.ds(h * LANES, LANES)
        out.append(
            pltpu.make_async_copy(rows_ref.at[rows], rows_hbm.at[0, rows], out_sems.at[h])
        )
        out[-1].start()
    divisor = (n_segments * steps).astype(jnp.float32)
    rate_ref[...] = (log_scale - jnp.log(jnp.full_like(ones, n_states))) / divisor
    for copy in out:
        copy.wait()


def body(observed, pattern, trans_blocks, leave_rate, symbol_emit, cluster_emit, symbol_cluster):
    n_blocks, n_source, size, _ = trans_blocks.shape
    n_states = leave_rate.shape[0]
    steps = observed.shape[0]
    n_tm = lax.axis_size("tm")
    n_rows = n_states // lax.axis_size("rows")
    n_half = n_rows // LANES
    all_observed = observed.reshape(1, steps)
    while all_observed.shape[0] < n_tm:
        distance = all_observed.shape[0]
        route = [(i, i + distance) for i in range(n_tm - distance)]
        earlier = lax.ppermute(all_observed, "tm", route)
        all_observed = jnp.concatenate([all_observed, earlier], axis=0)
    all_observed = all_observed[:n_tm]
    vmem = pl.BlockSpec(memory_space=pltpu.VMEM)
    smem = pl.BlockSpec(memory_space=pltpu.SMEM)
    hbm = pl.BlockSpec(memory_space=pltpu.HBM)
    f32, bf16 = jnp.float32, jnp.bfloat16
    sources = pattern.T
    weight, stay, stay_slab = pl.pallas_call(
        build_kernel,
        out_shape=[
            jax.ShapeDtypeStruct((n_blocks, size, n_source * size), bf16),
            jax.ShapeDtypeStruct((n_states, LANES), f32),
            jax.ShapeDtypeStruct((n_blocks, n_tm, LANES), f32),
        ],
        in_specs=[smem, vmem, vmem],
        out_specs=[vmem] * 3,
        scratch_shapes=[pltpu.VMEM((n_states, LANES), f32)],
        compiler_params=pltpu.CompilerParams(vmem_limit_bytes=16 << 20),
        cost_estimate=pl.CostEstimate(flops=1 << 31, bytes_accessed=4 << 20, transcendentals=0),
        name="build",
    )(sources, leave_rate.reshape(1, n_states), trans_blocks)
    return pl.pallas_call(
        chain_kernel,
        out_shape=[
            jax.ShapeDtypeStruct((1, n_rows, n_states), f32),
            jax.ShapeDtypeStruct((1, n_rows), f32),
        ],
        in_specs=[smem] * 3 + [vmem] * 5,
        out_specs=[hbm, vmem],
        scratch_shapes=[
            pltpu.VMEM((n_rows, n_states), f32),
            pltpu.VMEM((n_half, n_blocks, size + SUBLANES, LANES), f32),
            pltpu.VMEM((n_half, n_blocks, size + SUBLANES, LANES), f32),
            pltpu.VMEM((n_states, n_rows), bf16),
            pltpu.VMEM((n_states, n_rows), bf16),
            pltpu.VMEM((LANES, n_states), f32),
            pltpu.VMEM((n_states, LANES), f32),
            pltpu.VMEM((n_states, LANES), f32),
            pltpu.VMEM((steps, n_blocks, n_tm, LANES), f32),
            [pltpu.VMEM((steps - l, n_blocks, n_tm, LANES), f32) for l in range(steps)],
            [
                [pltpu.VMEM((steps - l, n_blocks, n_tm, LANES), f32) for _ in range(LANES // size)]
                for l in range(steps)
            ],
            pltpu.VMEM((n_tm, n_states), f32),
            pltpu.SemaphoreType.DMA((n_half,)),
        ],
        compiler_params=pltpu.CompilerParams(vmem_limit_bytes=32 << 20),
        cost_estimate=pl.CostEstimate(flops=1 << 34, bytes_accessed=4 << 20, transcendentals=0),
        name="chain",
    )(
        all_observed,
        sources,
        symbol_cluster,
        cluster_emit,
        symbol_emit,
        weight,
        stay,
        stay_slab,
    )


def solution(mesh):
    in_specs = (P("tm"), P(), P(), P(), P(), P(), P())
    out_specs = (P("tm", "rows", None), P("tm", "rows"))
    return jax.shard_map(body, mesh=mesh, in_specs=in_specs, out_specs=out_specs, check_vma=False)
```

```python
import functools

import jax
import jax.numpy as jnp
from jax import lax
from jax.experimental import pallas as pl
from jax.experimental.pallas import tpu as pltpu
from jax.sharding import PartitionSpec as P

LANES = 128
SUBLANES = 8


def column(row):
    return jnp.broadcast_to(row, (LANES, row.shape[1])).T


def twice(tile, at, size):
    other = pltpu.roll(tile, size, 1)
    low_half = lax.broadcasted_iota(jnp.int32, (1, LANES), 1) < size
    return jnp.where(low_half, tile, other) if at == 0 else jnp.where(low_half, other, tile)


def chain_kernel(
    observed_ref,
    pattern_hbm,
    cluster_hbm,
    leave_hbm,
    blocks_hbm,
    cluster_emit_hbm,
    symbol_hbm,
    rows_hbm,
    rate_ref,
    pattern_ref,
    cluster_ref,
    leave_ref,
    blocks_ref,
    cluster_emit_ref,
    symbol_ref,
    rows_ref,
    leave_col_ref,
    stay_ref,
    weight_ref,
    cur_ref,
    base_ref,
    low_a_ref,
    low_b_ref,
    emit_ref,
    emit_col_ref,
    change_col_ref,
    stay_slab_ref,
    emit_slab_ref,
    sum_refs,
    part_refs,
    change_ref,
    sems,
    block_sems,
    out_sems,
):
    n_tm, steps = observed_ref.shape
    n_half, n_blocks, padded, _ = cur_ref.shape
    size = blocks_ref.shape[-1]
    n_states = n_blocks * size
    n_rows = n_half * LANES
    n_source = pattern_ref.shape[0]
    first = padded - size
    n_segments = lax.axis_index("tm") + 1
    row_start = lax.axis_index("rows") * n_rows
    lows = (low_a_ref, low_b_ref)

    small = [
        pltpu.make_async_copy(source, target, sems.at[i])
        for i, (source, target) in enumerate(
            [
                (leave_hbm, leave_ref),
                (pattern_hbm, pattern_ref),
                (cluster_hbm, cluster_ref),
                (cluster_emit_hbm, cluster_emit_ref),
                (symbol_hbm, symbol_ref),
            ]
        )
    ]
    n_chunks = block_sems.shape[0]
    per_chunk = n_blocks // n_chunks
    chunks = [
        pltpu.make_async_copy(
            blocks_hbm.at[pl.ds(i * per_chunk, per_chunk)],
            blocks_ref.at[pl.ds(i * per_chunk, per_chunk)],
            block_sems.at[i],
        )
        for i in range(n_chunks)
    ]
    for copy in small[:2] + chunks + small[2:]:
        copy.start()

    def store(target_ref, low_ref, j, h, new):
        target_ref[h, j, first:, :] = new
        target_ref[h, j, :first, :] = new[size - first :, :]
        if low_ref is not None:
            rows, part = slice(j * size, (j + 1) * size), slice(h * LANES, (h + 1) * LANES)
            low_ref[rows, part] = new.astype(jnp.bfloat16)

    state = lax.broadcasted_iota(jnp.int32, (size, LANES), 0)
    row = lax.broadcasted_iota(jnp.int32, (size, LANES), 1)
    for j in range(n_blocks):
        for h in range(n_half):
            start = state + j * size == row + (row_start + h * LANES)
            store(base_ref, None, j, h, start.astype(jnp.float32))

    def moved_from_identity(j):
        own = [jnp.zeros((size, LANES), jnp.float32) for _ in range(n_half)]
        lane_block = lax.broadcasted_iota(jnp.int32, (size, LANES), 1) // size + row_start // size
        for k in range(n_source):
            tile = weight_ref[j, :, k // per * LANES : (k // per + 1) * LANES]
            tile = twice(tile.astype(jnp.float32), k % per, size)
            for h in range(n_half):
                here = lane_block + h * per == pattern_ref[k, j]
                own[h] = own[h] + jnp.where(here, tile, 0.0)
        return jnp.concatenate(own, axis=1)
    emit_ref[...] = jnp.zeros_like(emit_ref)
    for refs in part_refs:
        for ref in refs:
            ref[...] = jnp.zeros_like(ref)

    per = LANES // size
    low_half = lax.broadcasted_iota(jnp.int32, (1, LANES), 1) < size

    small[0].wait()
    for j in range(n_blocks):
        tile = leave_ref[:, j // per * LANES : (j // per + 1) * LANES]
        tile = jnp.broadcast_to(1.0 - tile, (n_tm, LANES))
        stay_slab_ref[j] = twice(tile, j % per, size)
    leave_col = column(leave_ref[...])
    leave_col_ref[...] = leave_col
    for j in range(n_blocks):
        own = leave_col[j * size : (j + 1) * size]
        stay_ref[j * size : (j + 1) * size, :] = 1.0 - pltpu.roll(own, 1, 0)
    small[1].wait()
    for j in range(n_blocks):
        if j % per_chunk == 0:
            chunks[j // per_chunk].wait()
        parts = []
        for k in range(n_source):
            rows = pl.ds(pl.multiple_of(pattern_ref[k, j] * size, size), size)
            parts.append(blocks_ref[j, k].astype(jnp.float32) * leave_col_ref[rows, :size])
        weight_ref[j] = jnp.concatenate(parts, axis=0).T.astype(jnp.bfloat16)
    for copy in small[2:]:
        copy.wait()

    def emission_of(g, s):
        symbol = observed_ref[g, s]
        row = symbol_ref[pl.ds(symbol, 1), :]
        return row * cluster_emit_ref[pl.ds(cluster_ref[symbol], 1), :]

    def find_changes():
        rows = n_blocks * n_tm
        stays = stay_slab_ref[...].reshape(rows, LANES)
        for s in range(steps):
            emission = jnp.concatenate([emission_of(g, s) for g in range(n_tm)], axis=0)
            for j in range(n_blocks):
                tile = emission[:, j // per * LANES : (j // per + 1) * LANES]
                emit_slab_ref[s, j] = twice(tile, j % per, size)

        def row_sums(l, p):
            return sum_refs[l][p].reshape(rows, LANES)

        for l in range(steps):
            n_pos = steps - l
            images = []
            for p in range(n_pos):
                image = emit_slab_ref[p].reshape(rows, LANES)
                if l:
                    image = image * row_sums(l - 1, p + 1)
                images.append(image)
            for j in range(n_blocks):
                own = [image[j * n_tm : (j + 1) * n_tm] for image in images]
                own = jnp.concatenate(own, axis=0)[:, :size].astype(jnp.bfloat16)
                moved = jnp.dot(own, weight_ref[j], preferred_element_type=jnp.float32)
                for k in range(n_source):
                    tile = moved[:, k // per * LANES : (k // per + 1) * LANES]
                    tile = tile.reshape(n_pos, n_tm, LANES)
                    ref = part_refs[l][k % per]
                    source = pattern_ref[k, j]
                    for p in range(n_pos):
                        ref[p, source] = ref[p, source] + tile[p]
            for p in range(n_pos):
                sides = [ref[p].reshape(rows, LANES) for ref in part_refs[l]]
                total = jnp.where(low_half, sides[0], sides[1])
                total = total + pltpu.roll(total, size, 1)
                total = total + stays * pltpu.roll(images[p], LANES - 1, 1)
                sum_refs[l][p] = total.reshape(n_blocks, n_tm, LANES)

        exact = jnp.ones((rows, LANES), jnp.float32)
        weight = exact
        deviation = []
        for s in range(steps):
            row_sum = pltpu.roll(row_sums(s, 0), 1, 1)
            for q in range(s):
                row_sum = row_sum + deviation[q] * row_sums(s - q - 1, q + 1)
                row_sum = pltpu.roll(row_sum, 1, 1)
            emission = emit_slab_ref[s].reshape(rows, LANES)
            exact = pltpu.roll(exact * stays, 1, 1) * emission
            weight = pltpu.roll(weight * stays, 1, 1) * emission
            rounded = (weight * (n_states / row_sum)).astype(jnp.bfloat16).astype(jnp.float32)
            rounded = rounded * (row_sum * (1.0 / n_states))
            deviation.append(rounded - weight)
            weight = rounded
        change = (weight - exact).reshape(n_blocks, n_tm, LANES)
        for m in range(n_states // LANES):
            tile = change[m * per + per - 1]
            for i in range(per - 1):
                tile = jnp.where(low_half, change[m * per + i], tile)
            change_ref[:, m * LANES : (m + 1) * LANES] = tile

    def segment(g, carried, is_first=False):
        scale, log_scale = carried
        for s in range(steps):
            emit_ref[s : s + 1, :] = emission_of(g, s)
        if not is_first:
            emit_ref[steps : steps + 1, :] = change_ref[pl.ds(g, 1), :]
        emit_col_ref[...] = emit_ref[...].T
        if is_first:
            find_changes()
            change_col_ref[...] = column(change_ref[:1, :])
        sums = [jnp.zeros((SUBLANES, LANES), jnp.float32) for _ in range(n_half)]
        for s in range(steps):
            now, later = lows[s % 2], lows[(s + 1) % 2]
            for j in range(n_blocks):
                states = slice(j * size, (j + 1) * size)
                if is_first and s == 0:
                    moved = moved_from_identity(j)
                else:
                    picked = [
                        now[pl.ds(pl.multiple_of(pattern_ref[k, j] * size, size), size), :]
                        for k in range(n_source)
                    ]
                    moved = jnp.dot(
                        weight_ref[j],
                        jnp.concatenate(picked, axis=0),
                        preferred_element_type=jnp.float32,
                    )
                emission = jnp.broadcast_to(emit_col_ref[states, s : s + 1], (size, LANES))
                stay = stay_ref[states, :]
                from_ref = base_ref if s == 0 else cur_ref
                to_ref = base_ref if s == steps - 1 else cur_ref
                if s == steps - 1:
                    if is_first:
                        change = change_col_ref[states, :]
                    else:
                        change = emit_col_ref[states, steps : steps + 1]
                        change = jnp.broadcast_to(change, (size, LANES))
                for h in range(n_half):
                    part = slice(h * LANES, (h + 1) * LANES)
                    kept = from_ref[h, j, first - 1 : padded - 1, :] * stay
                    new = (kept + moved[:, part]) * emission
                    if s == steps - 1:
                        start = base_ref[h, j, first - steps : padded - steps, :]
                        new = new + start * change
                        if not is_first:
                            new = new * scale[:, part]
                        sums[h] = sums[h] + jnp.sum(new.reshape(-1, SUBLANES, LANES), axis=0)
                    store(to_ref, later, j, h, new)
        if steps % 2:
            low_a_ref[...] = low_b_ref[...]
        row_sum = jnp.concatenate([jnp.sum(t, axis=0, keepdims=True) for t in sums], axis=1)
        return 1.0 / row_sum, log_scale + jnp.log(row_sum)

    ones = jnp.ones((1, n_rows), jnp.float32)
    carried = segment(0, (ones, jnp.zeros_like(ones)), is_first=True)
    scale, log_scale = lax.fori_loop(1, n_segments, segment, carried)
    scale = scale * n_states
    out = []
    n_tiles = n_states // LANES
    per_out = n_half * n_tiles // out_sems.shape[0]
    for h in range(n_half):
        part = slice(h * LANES, (h + 1) * LANES)
        for j in range(n_tiles):
            block = [base_ref[h, j * per + i, first:, :] for i in range(per)]
            block = jnp.concatenate(block, axis=0) * scale[:, part]
            rows_ref[part, j * LANES : (j + 1) * LANES] = block.T
            if (j + 1) % per_out == 0:
                rows = pl.ds(h * LANES, LANES)
                cols = pl.ds((j + 1 - per_out) * LANES, per_out * LANES)
                sem = out_sems.at[len(out)]
                out.append(
                    pltpu.make_async_copy(rows_ref.at[rows, cols], rows_hbm.at[0, rows, cols], sem)
                )
                out[-1].start()
    divisor = (n_segments * steps).astype(jnp.float32)
    rate_ref[...] = (log_scale - jnp.log(jnp.full_like(ones, n_states))) / divisor
    for copy in out:
        copy.wait()


def body(observed, pattern, trans_blocks, leave_rate, symbol_emit, cluster_emit, symbol_cluster):
    n_blocks, n_source, size, _ = trans_blocks.shape
    n_states = leave_rate.shape[0]
    steps = observed.shape[0]
    n_rows = n_states // lax.axis_size("rows")
    n_tm = lax.axis_size("tm")
    own = jnp.broadcast_to(observed[None, :], (n_tm, steps))
    all_observed = lax.all_to_all(own, "tm", 0, 0, tiled=True)
    vmem = pl.BlockSpec(memory_space=pltpu.VMEM)
    smem = pl.BlockSpec(memory_space=pltpu.SMEM)
    hbm = pl.BlockSpec(memory_space=pltpu.HBM)
    f32, bf16 = jnp.float32, jnp.bfloat16
    return pl.pallas_call(
        chain_kernel,
        out_shape=[
            jax.ShapeDtypeStruct((1, n_rows, n_states), f32),
            jax.ShapeDtypeStruct((1, n_rows), f32),
        ],
        in_specs=[smem] + [hbm] * 6,
        out_specs=[hbm, vmem],
        scratch_shapes=[
            pltpu.SMEM((n_source, n_blocks), jnp.int32),
            pltpu.SMEM(symbol_cluster.shape, jnp.int32),
            pltpu.VMEM((1, n_states), f32),
            pltpu.VMEM(trans_blocks.shape, bf16),
            pltpu.VMEM(cluster_emit.shape, f32),
            pltpu.VMEM(symbol_emit.shape, f32),
            pltpu.VMEM((n_rows, n_states), f32),
            pltpu.VMEM((n_states, LANES), f32),
            pltpu.VMEM((n_states, LANES), f32),
            pltpu.VMEM((n_blocks, size, n_source * size), bf16),
            pltpu.VMEM((n_rows // LANES, n_blocks, size + SUBLANES, LANES), f32),
            pltpu.VMEM((n_rows // LANES, n_blocks, size + SUBLANES, LANES), f32),
            pltpu.VMEM((n_states, n_rows), bf16),
            pltpu.VMEM((n_states, n_rows), bf16),
            pltpu.VMEM((LANES, n_states), f32),
            pltpu.VMEM((n_states, LANES), f32),
            pltpu.VMEM((n_states, LANES), f32),
            pltpu.VMEM((n_blocks, n_tm, LANES), f32),
            pltpu.VMEM((steps, n_blocks, n_tm, LANES), f32),
            [pltpu.VMEM((steps - l, n_blocks, n_tm, LANES), f32) for l in range(steps)],
            [
                [pltpu.VMEM((steps - l, n_blocks, n_tm, LANES), f32) for _ in range(LANES // size)]
                for l in range(steps)
            ],
            pltpu.VMEM((n_tm, n_states), f32),
            pltpu.SemaphoreType.DMA((5,)),
            pltpu.SemaphoreType.DMA((4,)),
            pltpu.SemaphoreType.DMA((2 * n_rows // LANES,)),
        ],
        compiler_params=pltpu.CompilerParams(vmem_limit_bytes=60 << 20),
        cost_estimate=pl.CostEstimate(flops=1 << 34, bytes_accessed=4 << 20, transcendentals=0),
        name="chain",
    )(
        all_observed,
        pattern.T,
        symbol_cluster,
        leave_rate.reshape(1, n_states),
        trans_blocks,
        cluster_emit,
        symbol_emit,
    )


def solution(mesh):
    in_specs = (P("tm"), P(), P(), P(), P(), P(), P())
    out_specs = (P("tm", "rows", None), P("tm", "rows"))
    return jax.shard_map(body, mesh=mesh, in_specs=in_specs, out_specs=out_specs, check_vma=False)
```

```python
import functools

import jax
import jax.numpy as jnp
from jax import lax
from jax.experimental import pallas as pl
from jax.experimental.pallas import tpu as pltpu
from jax.sharding import PartitionSpec as P

LANES = 128
SUBLANES = 8


def column(row):
    return jnp.broadcast_to(row, (LANES, row.shape[1])).T


def twice(tile, at, size):
    other = pltpu.roll(tile, size, 1)
    low_half = lax.broadcasted_iota(jnp.int32, (1, LANES), 1) < size
    return jnp.where(low_half, tile, other) if at == 0 else jnp.where(low_half, other, tile)


def chain_kernel(
    observed_ref,
    pattern_hbm,
    cluster_hbm,
    leave_hbm,
    blocks_hbm,
    cluster_emit_hbm,
    symbol_hbm,
    rows_hbm,
    rate_ref,
    pattern_ref,
    cluster_ref,
    leave_ref,
    blocks_ref,
    cluster_emit_ref,
    symbol_ref,
    rows_ref,
    leave_col_ref,
    stay_ref,
    weight_ref,
    cur_ref,
    base_ref,
    low_a_ref,
    low_b_ref,
    emit_ref,
    emit_col_ref,
    change_col_ref,
    stay_slab_ref,
    emit_slab_ref,
    sum_refs,
    part_refs,
    change_ref,
    sems,
    block_sems,
    out_sems,
):
    n_tm, steps = observed_ref.shape
    n_half, n_blocks, padded, _ = cur_ref.shape
    size = blocks_ref.shape[-1]
    n_states = n_blocks * size
    n_rows = n_half * LANES
    n_source = pattern_ref.shape[0]
    first = padded - size
    n_segments = lax.axis_index("tm") + 1
    row_start = lax.axis_index("rows") * n_rows
    lows = (low_a_ref, low_b_ref)

    small = [
        pltpu.make_async_copy(source, target, sems.at[i])
        for i, (source, target) in enumerate(
            [
                (leave_hbm, leave_ref),
                (pattern_hbm, pattern_ref),
                (cluster_hbm, cluster_ref),
                (cluster_emit_hbm, cluster_emit_ref),
                (symbol_hbm, symbol_ref),
            ]
        )
    ]
    n_chunks = block_sems.shape[0]
    per_chunk = n_blocks // n_chunks
    chunks = [
        pltpu.make_async_copy(
            blocks_hbm.at[pl.ds(i * per_chunk, per_chunk)],
            blocks_ref.at[pl.ds(i * per_chunk, per_chunk)],
            block_sems.at[i],
        )
        for i in range(n_chunks)
    ]
    for copy in small + chunks:
        copy.start()

    def store(target_ref, low_ref, j, h, new):
        target_ref[h, j, first:, :] = new
        target_ref[h, j, :first, :] = new[size - first :, :]
        if low_ref is not None:
            rows, part = slice(j * size, (j + 1) * size), slice(h * LANES, (h + 1) * LANES)
            low_ref[rows, part] = new.astype(jnp.bfloat16)

    state = lax.broadcasted_iota(jnp.int32, (size, LANES), 0)
    row = lax.broadcasted_iota(jnp.int32, (size, LANES), 1)
    for j in range(n_blocks):
        for h in range(n_half):
            start = state + j * size == row + (row_start + h * LANES)
            store(base_ref, None, j, h, start.astype(jnp.float32))

    def moved_from_identity(j):
        own = [jnp.zeros((size, LANES), jnp.float32) for _ in range(n_half)]
        lane_block = lax.broadcasted_iota(jnp.int32, (size, LANES), 1) // size + row_start // size
        for k in range(n_source):
            tile = weight_ref[j, :, k // per * LANES : (k // per + 1) * LANES]
            tile = twice(tile.astype(jnp.float32), k % per, size)
            for h in range(n_half):
                here = lane_block + h * per == pattern_ref[k, j]
                own[h] = own[h] + jnp.where(here, tile, 0.0)
        return jnp.concatenate(own, axis=1)
    emit_ref[...] = jnp.zeros_like(emit_ref)
    for refs in part_refs:
        for ref in refs:
            ref[...] = jnp.zeros_like(ref)

    per = LANES // size
    low_half = lax.broadcasted_iota(jnp.int32, (1, LANES), 1) < size

    small[0].wait()
    for j in range(n_blocks):
        tile = leave_ref[:, j // per * LANES : (j // per + 1) * LANES]
        tile = jnp.broadcast_to(1.0 - tile, (n_tm, LANES))
        stay_slab_ref[j] = twice(tile, j % per, size)
    leave_col = column(leave_ref[...])
    leave_col_ref[...] = leave_col
    for j in range(n_blocks):
        own = leave_col[j * size : (j + 1) * size]
        stay_ref[j * size : (j + 1) * size, :] = 1.0 - pltpu.roll(own, 1, 0)
    for copy in small[1:]:
        copy.wait()

    def build(j):
        if j % per_chunk == 0:
            chunks[j // per_chunk].wait()
        parts = []
        for k in range(n_source):
            rows = pl.ds(pl.multiple_of(pattern_ref[k, j] * size, size), size)
            parts.append(blocks_ref[j, k].astype(jnp.float32) * leave_col_ref[rows, :size])
        weight_ref[j] = jnp.concatenate(parts, axis=0).T.astype(jnp.bfloat16)

    def emission_of(g, s):
        symbol = observed_ref[g, s]
        row = symbol_ref[pl.ds(symbol, 1), :]
        return row * cluster_emit_ref[pl.ds(cluster_ref[symbol], 1), :]

    def find_changes():
        rows = n_blocks * n_tm
        stays = stay_slab_ref[...].reshape(rows, LANES)
        for s in range(steps):
            emission = jnp.concatenate([emission_of(g, s) for g in range(n_tm)], axis=0)
            for j in range(n_blocks):
                tile = emission[:, j // per * LANES : (j // per + 1) * LANES]
                emit_slab_ref[s, j] = twice(tile, j % per, size)
        yield

        def row_sums(l, p):
            return sum_refs[l][p].reshape(rows, LANES)

        for l in range(steps):
            n_pos = steps - l
            images = []
            for p in range(n_pos):
                image = emit_slab_ref[p].reshape(rows, LANES)
                if l:
                    image = image * row_sums(l - 1, p + 1)
                images.append(image)
            for j in range(n_blocks):
                own = [image[j * n_tm : (j + 1) * n_tm] for image in images]
                own = jnp.concatenate(own, axis=0)[:, :size].astype(jnp.bfloat16)
                moved = jnp.dot(own, weight_ref[j], preferred_element_type=jnp.float32)
                for k in range(n_source):
                    tile = moved[:, k // per * LANES : (k // per + 1) * LANES]
                    tile = tile.reshape(n_pos, n_tm, LANES)
                    ref = part_refs[l][k % per]
                    source = pattern_ref[k, j]
                    for p in range(n_pos):
                        ref[p, source] = ref[p, source] + tile[p]
                yield
            for p in range(n_pos):
                sides = [ref[p].reshape(rows, LANES) for ref in part_refs[l]]
                total = jnp.where(low_half, sides[0], sides[1])
                total = total + pltpu.roll(total, size, 1)
                total = total + stays * pltpu.roll(images[p], LANES - 1, 1)
                sum_refs[l][p] = total.reshape(n_blocks, n_tm, LANES)
            yield

        exact = jnp.ones((rows, LANES), jnp.float32)
        weight = exact
        deviation = []
        for s in range(steps):
            row_sum = pltpu.roll(row_sums(s, 0), 1, 1)
            for q in range(s):
                row_sum = row_sum + deviation[q] * row_sums(s - q - 1, q + 1)
                row_sum = pltpu.roll(row_sum, 1, 1)
            emission = emit_slab_ref[s].reshape(rows, LANES)
            exact = pltpu.roll(exact * stays, 1, 1) * emission
            weight = pltpu.roll(weight * stays, 1, 1) * emission
            rounded = (weight * (n_states / row_sum)).astype(jnp.bfloat16).astype(jnp.float32)
            rounded = rounded * (row_sum * (1.0 / n_states))
            deviation.append(rounded - weight)
            weight = rounded
            yield
        change = (weight - exact).reshape(n_blocks, n_tm, LANES)
        for m in range(n_states // LANES):
            tile = change[m * per + per - 1]
            for i in range(per - 1):
                tile = jnp.where(low_half, change[m * per + i], tile)
            change_ref[:, m * LANES : (m + 1) * LANES] = tile

    def segment(g, carried, is_first=False):
        scale, log_scale = carried
        for s in range(steps):
            emit_ref[s : s + 1, :] = emission_of(g, s)
        if not is_first:
            emit_ref[steps : steps + 1, :] = change_ref[pl.ds(g, 1), :]
        emit_col_ref[...] = emit_ref[...].T
        beside = iter(())
        if is_first:
            beside = find_changes()
            next(beside)
        sums = [jnp.zeros((SUBLANES, LANES), jnp.float32) for _ in range(n_half)]
        for s in range(steps):
            now, later = lows[s % 2], lows[(s + 1) % 2]
            if is_first and s == steps - 1:
                for _ in beside:
                    pass
                change_col_ref[...] = column(change_ref[:1, :])
            for j in range(n_blocks):
                if is_first and s == 0:
                    build(j)
                for _ in range(2 if s else 1):
                    next(beside, None)
                states = slice(j * size, (j + 1) * size)
                if is_first and s == 0:
                    moved = moved_from_identity(j)
                else:
                    picked = [
                        now[pl.ds(pl.multiple_of(pattern_ref[k, j] * size, size), size), :]
                        for k in range(n_source)
                    ]
                    moved = jnp.dot(
                        weight_ref[j],
                        jnp.concatenate(picked, axis=0),
                        preferred_element_type=jnp.float32,
                    )
                emission = jnp.broadcast_to(emit_col_ref[states, s : s + 1], (size, LANES))
                stay = stay_ref[states, :]
                from_ref = base_ref if s == 0 else cur_ref
                to_ref = base_ref if s == steps - 1 else cur_ref
                if s == steps - 1:
                    if is_first:
                        change = change_col_ref[states, :]
                    else:
                        change = emit_col_ref[states, steps : steps + 1]
                        change = jnp.broadcast_to(change, (size, LANES))
                for h in range(n_half):
                    part = slice(h * LANES, (h + 1) * LANES)
                    kept = from_ref[h, j, first - 1 : padded - 1, :] * stay
                    new = (kept + moved[:, part]) * emission
                    if s == steps - 1:
                        start = base_ref[h, j, first - steps : padded - steps, :]
                        new = new + start * change
                        if not is_first:
                            new = new * scale[:, part]
                        sums[h] = sums[h] + jnp.sum(new.reshape(-1, SUBLANES, LANES), axis=0)
                    store(to_ref, later, j, h, new)
        if steps % 2:
            low_a_ref[...] = low_b_ref[...]
        row_sum = jnp.concatenate([jnp.sum(t, axis=0, keepdims=True) for t in sums], axis=1)
        return 1.0 / row_sum, log_scale + jnp.log(row_sum)

    ones = jnp.ones((1, n_rows), jnp.float32)
    carried = segment(0, (ones, jnp.zeros_like(ones)), is_first=True)
    scale, log_scale = lax.fori_loop(1, n_segments, segment, carried)
    scale = scale * n_states
    out = []
    n_tiles = n_states // LANES
    per_out = n_half * n_tiles // out_sems.shape[0]
    for h in range(n_half):
        part = slice(h * LANES, (h + 1) * LANES)
        for j in range(n_tiles):
            block = [base_ref[h, j * per + i, first:, :] for i in range(per)]
            block = jnp.concatenate(block, axis=0) * scale[:, part]
            rows_ref[part, j * LANES : (j + 1) * LANES] = block.T
            if (j + 1) % per_out == 0:
                rows = pl.ds(h * LANES, LANES)
                cols = pl.ds((j + 1 - per_out) * LANES, per_out * LANES)
                sem = out_sems.at[len(out)]
                out.append(
                    pltpu.make_async_copy(rows_ref.at[rows, cols], rows_hbm.at[0, rows, cols], sem)
                )
                out[-1].start()
    divisor = (n_segments * steps).astype(jnp.float32)
    rate_ref[...] = (log_scale - jnp.log(jnp.full_like(ones, n_states))) / divisor
    for copy in out:
        copy.wait()


def body(observed, pattern, trans_blocks, leave_rate, symbol_emit, cluster_emit, symbol_cluster):
    n_blocks, n_source, size, _ = trans_blocks.shape
    n_states = leave_rate.shape[0]
    steps = observed.shape[0]
    n_rows = n_states // lax.axis_size("rows")
    n_tm = lax.axis_size("tm")
    own = jnp.broadcast_to(observed[None, :], (n_tm, steps))
    all_observed = lax.all_to_all(own, "tm", 0, 0, tiled=True)
    vmem = pl.BlockSpec(memory_space=pltpu.VMEM)
    smem = pl.BlockSpec(memory_space=pltpu.SMEM)
    hbm = pl.BlockSpec(memory_space=pltpu.HBM)
    f32, bf16 = jnp.float32, jnp.bfloat16
    return pl.pallas_call(
        chain_kernel,
        out_shape=[
            jax.ShapeDtypeStruct((1, n_rows, n_states), f32),
            jax.ShapeDtypeStruct((1, n_rows), f32),
        ],
        in_specs=[smem] + [hbm] * 6,
        out_specs=[hbm, vmem],
        scratch_shapes=[
            pltpu.SMEM((n_source, n_blocks), jnp.int32),
            pltpu.SMEM(symbol_cluster.shape, jnp.int32),
            pltpu.VMEM((1, n_states), f32),
            pltpu.VMEM(trans_blocks.shape, bf16),
            pltpu.VMEM(cluster_emit.shape, f32),
            pltpu.VMEM(symbol_emit.shape, f32),
            pltpu.VMEM((n_rows, n_states), f32),
            pltpu.VMEM((n_states, LANES), f32),
            pltpu.VMEM((n_states, LANES), f32),
            pltpu.VMEM((n_blocks, size, n_source * size), bf16),
            pltpu.VMEM((n_rows // LANES, n_blocks, size + SUBLANES, LANES), f32),
            pltpu.VMEM((n_rows // LANES, n_blocks, size + SUBLANES, LANES), f32),
            pltpu.VMEM((n_states, n_rows), bf16),
            pltpu.VMEM((n_states, n_rows), bf16),
            pltpu.VMEM((LANES, n_states), f32),
            pltpu.VMEM((n_states, LANES), f32),
            pltpu.VMEM((n_states, LANES), f32),
            pltpu.VMEM((n_blocks, n_tm, LANES), f32),
            pltpu.VMEM((steps, n_blocks, n_tm, LANES), f32),
            [pltpu.VMEM((steps - l, n_blocks, n_tm, LANES), f32) for l in range(steps)],
            [
                [pltpu.VMEM((steps - l, n_blocks, n_tm, LANES), f32) for _ in range(LANES // size)]
                for l in range(steps)
            ],
            pltpu.VMEM((n_tm, n_states), f32),
            pltpu.SemaphoreType.DMA((5,)),
            pltpu.SemaphoreType.DMA((4,)),
            pltpu.SemaphoreType.DMA((2 * n_rows // LANES,)),
        ],
        compiler_params=pltpu.CompilerParams(vmem_limit_bytes=60 << 20),
        cost_estimate=pl.CostEstimate(flops=1 << 34, bytes_accessed=4 << 20, transcendentals=0),
        name="chain",
    )(
        all_observed,
        pattern.T,
        symbol_cluster,
        leave_rate.reshape(1, n_states),
        trans_blocks,
        cluster_emit,
        symbol_emit,
    )


def solution(mesh):
    in_specs = (P("tm"), P(), P(), P(), P(), P(), P())
    out_specs = (P("tm", "rows", None), P("tm", "rows"))
    return jax.shard_map(body, mesh=mesh, in_specs=in_specs, out_specs=out_specs, check_vma=False)
```

```python
import functools

import jax
import jax.numpy as jnp
from jax import lax
from jax.experimental import pallas as pl
from jax.experimental.pallas import tpu as pltpu
from jax.sharding import PartitionSpec as P

LANES = 128
SUBLANES = 8


def column(row):
    return jnp.broadcast_to(row, (LANES, row.shape[1])).T


def twice(tile, at, size):
    other = pltpu.roll(tile, size, 1)
    low_half = lax.broadcasted_iota(jnp.int32, (1, LANES), 1) < size
    return jnp.where(low_half, tile, other) if at == 0 else jnp.where(low_half, other, tile)


def chain_kernel(
    observed_ref,
    pattern_hbm,
    cluster_hbm,
    leave_hbm,
    blocks_hbm,
    cluster_emit_hbm,
    symbol_hbm,
    rows_hbm,
    rate_ref,
    pattern_ref,
    cluster_ref,
    leave_ref,
    blocks_ref,
    cluster_rows_ref,
    emit_ref,
    rows_ref,
    leave_col_ref,
    stay_ref,
    weight_ref,
    cur_ref,
    base_ref,
    low_a_ref,
    low_b_ref,
    emit_col_ref,
    all_col_ref,
    stay_slab_ref,
    emit_slab_ref,
    sum_refs,
    part_refs,
    sems,
    row_sems,
    block_sems,
    out_sems,
):
    n_tm, steps = observed_ref.shape
    n_half, n_blocks, padded, _ = cur_ref.shape
    size = blocks_ref.shape[-1]
    n_states = n_blocks * size
    n_rows = n_half * LANES
    n_source = pattern_ref.shape[0]
    first = padded - size
    n_segments = lax.axis_index("tm") + 1
    row_start = lax.axis_index("rows") * n_rows
    lows = (low_a_ref, low_b_ref)

    small = [
        pltpu.make_async_copy(source, target, sems.at[i])
        for i, (source, target) in enumerate(
            [
                (leave_hbm, leave_ref),
                (pattern_hbm, pattern_ref),
                (cluster_hbm, cluster_ref),
            ]
        )
    ]
    n_chunks = block_sems.shape[0]
    per_chunk = n_blocks // n_chunks
    chunks = [
        pltpu.make_async_copy(
            blocks_hbm.at[pl.ds(i * per_chunk, per_chunk)],
            blocks_ref.at[pl.ds(i * per_chunk, per_chunk)],
            block_sems.at[i],
        )
        for i in range(n_chunks)
    ]
    emit_ref[...] = jnp.zeros_like(emit_ref)
    small[2].start()
    for copy in small[:2] + chunks:
        copy.start()
    n_all = n_tm * steps
    small[2].wait()
    row_copies = []
    for s in range(steps):
        for g in range(n_tm):
            symbol = observed_ref[g, s]
            row = pl.ds(s * n_tm + g, 1)
            for source, target, index, sem in (
                (symbol_hbm, emit_ref, symbol, row_sems.at[0]),
                (cluster_emit_hbm, cluster_rows_ref, cluster_ref[symbol], row_sems.at[1]),
            ):
                copy = pltpu.make_async_copy(source.at[pl.ds(index, 1)], target.at[row], sem)
                copy.start()

    def store(target_ref, low_ref, j, h, new):
        target_ref[h, j, first:, :] = new
        target_ref[h, j, :first, :] = new[size - first :, :]
        if low_ref is not None:
            rows, part = slice(j * size, (j + 1) * size), slice(h * LANES, (h + 1) * LANES)
            low_ref[rows, part] = new.astype(jnp.bfloat16)

    state = lax.broadcasted_iota(jnp.int32, (size, LANES), 0)
    row = lax.broadcasted_iota(jnp.int32, (size, LANES), 1)
    for j in range(n_blocks):
        for h in range(n_half):
            start = state + j * size == row + (row_start + h * LANES)
            store(base_ref, None, j, h, start.astype(jnp.float32))

    def moved_from_identity(j):
        own = [jnp.zeros((size, LANES), jnp.float32) for _ in range(n_half)]
        lane_block = lax.broadcasted_iota(jnp.int32, (size, LANES), 1) // size + row_start // size
        for k in range(n_source):
            tile = weight_ref[j, :, k // per * LANES : (k // per + 1) * LANES]
            tile = twice(tile.astype(jnp.float32), k % per, size)
            for h in range(n_half):
                here = lane_block + h * per == pattern_ref[k, j]
                own[h] = own[h] + jnp.where(here, tile, 0.0)
        return jnp.concatenate(own, axis=1)
    for refs in part_refs:
        for ref in refs:
            ref[...] = jnp.zeros_like(ref)

    per = LANES // size
    low_half = lax.broadcasted_iota(jnp.int32, (1, LANES), 1) < size

    small[0].wait()
    for j in range(n_blocks):
        tile = leave_ref[:, j // per * LANES : (j // per + 1) * LANES]
        tile = jnp.broadcast_to(1.0 - tile, (n_tm, LANES))
        stay_slab_ref[j] = twice(tile, j % per, size)
    leave_col = column(leave_ref[...])
    leave_col_ref[...] = leave_col
    for j in range(n_blocks):
        own = leave_col[j * size : (j + 1) * size]
        stay_ref[j * size : (j + 1) * size, :] = 1.0 - pltpu.roll(own, 1, 0)
    small[1].wait()
    for j in range(n_blocks):
        if j % per_chunk == 0:
            chunks[j // per_chunk].wait()
        parts = []
        for k in range(n_source):
            rows = pl.ds(pl.multiple_of(pattern_ref[k, j] * size, size), size)
            parts.append(blocks_ref[j, k].astype(jnp.float32) * leave_col_ref[rows, :size])
        weight_ref[j] = jnp.concatenate(parts, axis=0).T.astype(jnp.bfloat16)
    rows = pl.ds(0, n_all)
    pltpu.make_async_copy(symbol_hbm.at[rows], emit_ref.at[rows], row_sems.at[0]).wait()
    rows = pl.ds(0, cluster_rows_ref.shape[0])
    pltpu.make_async_copy(cluster_rows_ref, cluster_rows_ref, row_sems.at[1]).wait()
    emit_ref[:n_all, :] = emit_ref[:n_all, :] * cluster_rows_ref[...]

    def find_changes():
        rows = n_blocks * n_tm
        stays = stay_slab_ref[...].reshape(rows, LANES)
        for s in range(steps):
            for j in range(n_blocks):
                cols = slice(j // per * LANES, (j // per + 1) * LANES)
                tile = emit_ref[s * n_tm : (s + 1) * n_tm, cols]
                emit_slab_ref[s, j] = twice(tile, j % per, size)

        def row_sums(l, p):
            return sum_refs[l][p].reshape(rows, LANES)

        for l in range(steps):
            n_pos = steps - l
            images = []
            for p in range(n_pos):
                image = emit_slab_ref[p].reshape(rows, LANES)
                if l:
                    image = image * row_sums(l - 1, p + 1)
                images.append(image)
            for j in range(n_blocks):
                own = [image[j * n_tm : (j + 1) * n_tm] for image in images]
                own = jnp.concatenate(own, axis=0)[:, :size].astype(jnp.bfloat16)
                moved = jnp.dot(own, weight_ref[j], preferred_element_type=jnp.float32)
                for k in range(n_source):
                    tile = moved[:, k // per * LANES : (k // per + 1) * LANES]
                    tile = tile.reshape(n_pos, n_tm, LANES)
                    ref = part_refs[l][k % per]
                    source = pattern_ref[k, j]
                    for p in range(n_pos):
                        ref[p, source] = ref[p, source] + tile[p]
            for p in range(n_pos):
                sides = [ref[p].reshape(rows, LANES) for ref in part_refs[l]]
                total = jnp.where(low_half, sides[0], sides[1])
                total = total + pltpu.roll(total, size, 1)
                total = total + stays * pltpu.roll(images[p], LANES - 1, 1)
                sum_refs[l][p] = total.reshape(n_blocks, n_tm, LANES)

        exact = jnp.ones((rows, LANES), jnp.float32)
        weight = exact
        deviation = []
        for s in range(steps):
            row_sum = pltpu.roll(row_sums(s, 0), 1, 1)
            for q in range(s):
                row_sum = row_sum + deviation[q] * row_sums(s - q - 1, q + 1)
                row_sum = pltpu.roll(row_sum, 1, 1)
            emission = emit_slab_ref[s].reshape(rows, LANES)
            exact = pltpu.roll(exact * stays, 1, 1) * emission
            weight = pltpu.roll(weight * stays, 1, 1) * emission
            rounded = (weight * (n_states / row_sum)).astype(jnp.bfloat16).astype(jnp.float32)
            rounded = rounded * (row_sum * (1.0 / n_states))
            deviation.append(rounded - weight)
            weight = rounded
        change = (weight - exact).reshape(n_blocks, n_tm, LANES)
        for m in range(n_states // LANES):
            tile = change[m * per + per - 1]
            for i in range(per - 1):
                tile = jnp.where(low_half, change[m * per + i], tile)
            emit_ref[n_all : n_all + n_tm, m * LANES : (m + 1) * LANES] = tile

    def segment(g, carried, is_first=False):
        scale, log_scale = carried
        if is_first:
            emit_col_ref[...] = emit_ref[...].T
            find_changes()
            all_col_ref[...] = emit_ref[...].T
        else:
            emit_col_ref[...] = pltpu.roll(all_col_ref[...], LANES - g, 1)
        sums = [jnp.zeros((SUBLANES, LANES), jnp.float32) for _ in range(n_half)]
        for s in range(steps):
            now, later = lows[s % 2], lows[(s + 1) % 2]
            for j in range(n_blocks):
                states = slice(j * size, (j + 1) * size)
                if is_first and s == 0:
                    moved = moved_from_identity(j)
                else:
                    picked = [
                        now[pl.ds(pl.multiple_of(pattern_ref[k, j] * size, size), size), :]
                        for k in range(n_source)
                    ]
                    moved = jnp.dot(
                        weight_ref[j],
                        jnp.concatenate(picked, axis=0),
                        preferred_element_type=jnp.float32,
                    )
                emission = jnp.broadcast_to(emit_col_ref[states, s * n_tm : s * n_tm + 1], (size, LANES))
                stay = stay_ref[states, :]
                from_ref = base_ref if s == 0 else cur_ref
                to_ref = base_ref if s == steps - 1 else cur_ref
                if s == steps - 1:
                    change_ref = all_col_ref if is_first else emit_col_ref
                    change = change_ref[states, n_all : n_all + 1]
                    change = jnp.broadcast_to(change, (size, LANES))
                for h in range(n_half):
                    part = slice(h * LANES, (h + 1) * LANES)
                    kept = from_ref[h, j, first - 1 : padded - 1, :] * stay
                    new = (kept + moved[:, part]) * emission
                    if s == steps - 1:
                        start = base_ref[h, j, first - steps : padded - steps, :]
                        new = new + start * change
                        if not is_first:
                            new = new * scale[:, part]
                        sums[h] = sums[h] + jnp.sum(new.reshape(-1, SUBLANES, LANES), axis=0)
                    store(to_ref, later, j, h, new)
        if steps % 2:
            low_a_ref[...] = low_b_ref[...]
        row_sum = jnp.concatenate([jnp.sum(t, axis=0, keepdims=True) for t in sums], axis=1)
        return 1.0 / row_sum, log_scale + jnp.log(row_sum)

    ones = jnp.ones((1, n_rows), jnp.float32)
    carried = segment(0, (ones, jnp.zeros_like(ones)), is_first=True)
    scale, log_scale = lax.fori_loop(1, n_segments, segment, carried)
    scale = scale * n_states
    out = []
    n_tiles = n_states // LANES
    per_out = n_half * n_tiles // out_sems.shape[0]
    for h in range(n_half):
        part = slice(h * LANES, (h + 1) * LANES)
        for j in range(n_tiles):
            block = [base_ref[h, j * per + i, first:, :] for i in range(per)]
            block = jnp.concatenate(block, axis=0) * scale[:, part]
            rows_ref[part, j * LANES : (j + 1) * LANES] = block.T
            if (j + 1) % per_out == 0:
                rows = pl.ds(h * LANES, LANES)
                cols = pl.ds((j + 1 - per_out) * LANES, per_out * LANES)
                sem = out_sems.at[len(out)]
                out.append(
                    pltpu.make_async_copy(rows_ref.at[rows, cols], rows_hbm.at[0, rows, cols], sem)
                )
                out[-1].start()
    divisor = (n_segments * steps).astype(jnp.float32)
    rate_ref[...] = (log_scale - jnp.log(jnp.full_like(ones, n_states))) / divisor
    for copy in out:
        copy.wait()


def body(observed, pattern, trans_blocks, leave_rate, symbol_emit, cluster_emit, symbol_cluster):
    n_blocks, n_source, size, _ = trans_blocks.shape
    n_states = leave_rate.shape[0]
    steps = observed.shape[0]
    n_rows = n_states // lax.axis_size("rows")
    n_tm = lax.axis_size("tm")
    own = jnp.broadcast_to(observed[None, :], (n_tm, steps))
    all_observed = lax.all_to_all(own, "tm", 0, 0, tiled=True)
    vmem = pl.BlockSpec(memory_space=pltpu.VMEM)
    smem = pl.BlockSpec(memory_space=pltpu.SMEM)
    hbm = pl.BlockSpec(memory_space=pltpu.HBM)
    f32, bf16 = jnp.float32, jnp.bfloat16
    return pl.pallas_call(
        chain_kernel,
        out_shape=[
            jax.ShapeDtypeStruct((1, n_rows, n_states), f32),
            jax.ShapeDtypeStruct((1, n_rows), f32),
        ],
        in_specs=[smem] + [hbm] * 6,
        out_specs=[hbm, vmem],
        scratch_shapes=[
            pltpu.SMEM((n_source, n_blocks), jnp.int32),
            pltpu.SMEM(symbol_cluster.shape, jnp.int32),
            pltpu.VMEM((1, n_states), f32),
            pltpu.VMEM(trans_blocks.shape, bf16),
            pltpu.VMEM((n_tm * steps, n_states), f32),
            pltpu.VMEM((LANES, n_states), f32),
            pltpu.VMEM((n_rows, n_states), f32),
            pltpu.VMEM((n_states, LANES), f32),
            pltpu.VMEM((n_states, LANES), f32),
            pltpu.VMEM((n_blocks, size, n_source * size), bf16),
            pltpu.VMEM((n_rows // LANES, n_blocks, size + SUBLANES, LANES), f32),
            pltpu.VMEM((n_rows // LANES, n_blocks, size + SUBLANES, LANES), f32),
            pltpu.VMEM((n_states, n_rows), bf16),
            pltpu.VMEM((n_states, n_rows), bf16),
            pltpu.VMEM((n_states, LANES), f32),
            pltpu.VMEM((n_states, LANES), f32),
            pltpu.VMEM((n_blocks, n_tm, LANES), f32),
            pltpu.VMEM((steps, n_blocks, n_tm, LANES), f32),
            [pltpu.VMEM((steps - l, n_blocks, n_tm, LANES), f32) for l in range(steps)],
            [
                [pltpu.VMEM((steps - l, n_blocks, n_tm, LANES), f32) for _ in range(LANES // size)]
                for l in range(steps)
            ],
            pltpu.SemaphoreType.DMA((3,)),
            pltpu.SemaphoreType.DMA((2,)),
            pltpu.SemaphoreType.DMA((4,)),
            pltpu.SemaphoreType.DMA((2 * n_rows // LANES,)),
        ],
        compiler_params=pltpu.CompilerParams(vmem_limit_bytes=60 << 20),
        cost_estimate=pl.CostEstimate(flops=1 << 34, bytes_accessed=4 << 20, transcendentals=0),
        name="chain",
    )(
        all_observed,
        pattern.T,
        symbol_cluster,
        leave_rate.reshape(1, n_states),
        trans_blocks,
        cluster_emit,
        symbol_emit,
    )


def solution(mesh):
    in_specs = (P("tm"), P(), P(), P(), P(), P(), P())
    out_specs = (P("tm", "rows", None), P("tm", "rows"))
    return jax.shard_map(body, mesh=mesh, in_specs=in_specs, out_specs=out_specs, check_vma=False)
```

```python
import functools

import jax
import jax.numpy as jnp
from jax import lax
from jax.experimental import pallas as pl
from jax.experimental.pallas import tpu as pltpu
from jax.sharding import PartitionSpec as P

LANES = 128
SUBLANES = 8


def column(row):
    return jnp.broadcast_to(row, (LANES, row.shape[1])).T


def twice(tile, at, size):
    other = pltpu.roll(tile, size, 1)
    low_half = lax.broadcasted_iota(jnp.int32, (1, LANES), 1) < size
    return jnp.where(low_half, tile, other) if at == 0 else jnp.where(low_half, other, tile)


def chain_kernel(
    observed_hbm,
    pattern_hbm,
    cluster_hbm,
    leave_hbm,
    blocks_hbm,
    cluster_emit_hbm,
    symbol_hbm,
    rows_hbm,
    rate_hbm,
    observed_ref,
    rate_ref,
    pattern_ref,
    cluster_ref,
    leave_ref,
    blocks_ref,
    cluster_emit_ref,
    symbol_ref,
    rows_ref,
    leave_col_ref,
    stay_ref,
    weight_ref,
    cur_ref,
    base_ref,
    low_a_ref,
    low_b_ref,
    emit_ref,
    emit_col_ref,
    change_col_ref,
    stay_slab_ref,
    emit_slab_ref,
    sum_refs,
    part_refs,
    change_ref,
    sems,
    block_sems,
    out_sems,
):
    n_tm, steps = observed_ref.shape
    n_half, n_blocks, padded, _ = cur_ref.shape
    size = blocks_ref.shape[-1]
    n_states = n_blocks * size
    n_rows = n_half * LANES
    n_source = pattern_ref.shape[0]
    first = padded - size
    n_segments = lax.axis_index("tm") + 1
    row_start = lax.axis_index("rows") * n_rows
    lows = (low_a_ref, low_b_ref)

    small = [
        pltpu.make_async_copy(source, target, sems.at[i])
        for i, (source, target) in enumerate(
            [
                (leave_hbm, leave_ref),
                (pattern_hbm, pattern_ref),
                (observed_hbm, observed_ref),
                (cluster_hbm, cluster_ref),
                (cluster_emit_hbm, cluster_emit_ref),
                (symbol_hbm, symbol_ref),
            ]
        )
    ]
    n_chunks = block_sems.shape[0]
    per_chunk = n_blocks // n_chunks
    chunks = [
        pltpu.make_async_copy(
            blocks_hbm.at[pl.ds(i * per_chunk, per_chunk)],
            blocks_ref.at[pl.ds(i * per_chunk, per_chunk)],
            block_sems.at[i],
        )
        for i in range(n_chunks)
    ]
    for copy in small[:2] + chunks + small[2:]:
        copy.start()

    def store(target_ref, low_ref, j, h, new):
        target_ref[h, j, first:, :] = new
        target_ref[h, j, :first, :] = new[size - first :, :]
        if low_ref is not None:
            rows, part = slice(j * size, (j + 1) * size), slice(h * LANES, (h + 1) * LANES)
            low_ref[rows, part] = new.astype(jnp.bfloat16)

    state = lax.broadcasted_iota(jnp.int32, (size, LANES), 0)
    row = lax.broadcasted_iota(jnp.int32, (size, LANES), 1)
    for j in range(n_blocks):
        for h in range(n_half):
            start = state + j * size == row + (row_start + h * LANES)
            store(base_ref, None, j, h, start.astype(jnp.float32))

    def moved_from_identity(j):
        own = [jnp.zeros((size, LANES), jnp.float32) for _ in range(n_half)]
        lane_block = lax.broadcasted_iota(jnp.int32, (size, LANES), 1) // size + row_start // size
        for k in range(n_source):
            tile = weight_ref[j, :, k // per * LANES : (k // per + 1) * LANES]
            tile = twice(tile.astype(jnp.float32), k % per, size)
            for h in range(n_half):
                here = lane_block + h * per == pattern_ref[k, j]
                own[h] = own[h] + jnp.where(here, tile, 0.0)
        return jnp.concatenate(own, axis=1)
    emit_ref[...] = jnp.zeros_like(emit_ref)
    for refs in part_refs:
        for ref in refs:
            ref[...] = jnp.zeros_like(ref)

    per = LANES // size
    low_half = lax.broadcasted_iota(jnp.int32, (1, LANES), 1) < size

    small[0].wait()
    for j in range(n_blocks):
        tile = leave_ref[:, j // per * LANES : (j // per + 1) * LANES]
        tile = jnp.broadcast_to(1.0 - tile, (n_tm, LANES))
        stay_slab_ref[j] = twice(tile, j % per, size)
    leave_col = column(leave_ref[...])
    leave_col_ref[...] = leave_col
    for j in range(n_blocks):
        own = leave_col[j * size : (j + 1) * size]
        stay_ref[j * size : (j + 1) * size, :] = 1.0 - pltpu.roll(own, 1, 0)
    small[1].wait()
    for j in range(n_blocks):
        if j % per_chunk == 0:
            chunks[j // per_chunk].wait()
        parts = []
        for k in range(n_source):
            rows = pl.ds(pl.multiple_of(pattern_ref[k, j] * size, size), size)
            parts.append(blocks_ref[j, k].astype(jnp.float32) * leave_col_ref[rows, :size])
        weight_ref[j] = jnp.concatenate(parts, axis=0).T.astype(jnp.bfloat16)
    for copy in small[2:]:
        copy.wait()

    def emission_of(g, s):
        symbol = observed_ref[g, s]
        row = symbol_ref[pl.ds(symbol, 1), :]
        return row * cluster_emit_ref[pl.ds(cluster_ref[symbol], 1), :]

    def find_changes():
        rows = n_blocks * n_tm
        stays = stay_slab_ref[...].reshape(rows, LANES)
        for s in range(steps):
            emission = jnp.concatenate([emission_of(g, s) for g in range(n_tm)], axis=0)
            for j in range(n_blocks):
                tile = emission[:, j // per * LANES : (j // per + 1) * LANES]
                emit_slab_ref[s, j] = twice(tile, j % per, size)

        def row_sums(l, p):
            return sum_refs[l][p].reshape(rows, LANES)

        for l in range(steps):
            n_pos = steps - l
            images = []
            for p in range(n_pos):
                image = emit_slab_ref[p].reshape(rows, LANES)
                if l:
                    image = image * row_sums(l - 1, p + 1)
                images.append(image)
            for j in range(n_blocks):
                own = [image[j * n_tm : (j + 1) * n_tm] for image in images]
                own = jnp.concatenate(own, axis=0)[:, :size].astype(jnp.bfloat16)
                moved = jnp.dot(own, weight_ref[j], preferred_element_type=jnp.float32)
                for k in range(n_source):
                    tile = moved[:, k // per * LANES : (k // per + 1) * LANES]
                    tile = tile.reshape(n_pos, n_tm, LANES)
                    ref = part_refs[l][k % per]
                    source = pattern_ref[k, j]
                    for p in range(n_pos):
                        ref[p, source] = ref[p, source] + tile[p]
            for p in range(n_pos):
                sides = [ref[p].reshape(rows, LANES) for ref in part_refs[l]]
                total = jnp.where(low_half, sides[0], sides[1])
                total = total + pltpu.roll(total, size, 1)
                total = total + stays * pltpu.roll(images[p], LANES - 1, 1)
                sum_refs[l][p] = total.reshape(n_blocks, n_tm, LANES)

        exact = jnp.ones((rows, LANES), jnp.float32)
        weight = exact
        deviation = []
        for s in range(steps):
            row_sum = pltpu.roll(row_sums(s, 0), 1, 1)
            for q in range(s):
                row_sum = row_sum + deviation[q] * row_sums(s - q - 1, q + 1)
                row_sum = pltpu.roll(row_sum, 1, 1)
            emission = emit_slab_ref[s].reshape(rows, LANES)
            exact = pltpu.roll(exact * stays, 1, 1) * emission
            weight = pltpu.roll(weight * stays, 1, 1) * emission
            rounded = (weight * (n_states / row_sum)).astype(jnp.bfloat16).astype(jnp.float32)
            rounded = rounded * (row_sum * (1.0 / n_states))
            deviation.append(rounded - weight)
            weight = rounded
        change = (weight - exact).reshape(n_blocks, n_tm, LANES)
        for m in range(n_states // LANES):
            tile = change[m * per + per - 1]
            for i in range(per - 1):
                tile = jnp.where(low_half, change[m * per + i], tile)
            change_ref[:, m * LANES : (m + 1) * LANES] = tile

    def segment(g, carried, is_first=False):
        scale, log_scale = carried
        for s in range(steps):
            emit_ref[s : s + 1, :] = emission_of(g, s)
        if not is_first:
            emit_ref[steps : steps + 1, :] = change_ref[pl.ds(g, 1), :]
        emit_col_ref[...] = emit_ref[...].T
        if is_first:
            find_changes()
            change_col_ref[...] = column(change_ref[:1, :])
        sums = [jnp.zeros((SUBLANES, LANES), jnp.float32) for _ in range(n_half)]
        for s in range(steps):
            now, later = lows[s % 2], lows[(s + 1) % 2]
            for j in range(n_blocks):
                states = slice(j * size, (j + 1) * size)
                if is_first and s == 0:
                    moved = moved_from_identity(j)
                else:
                    picked = [
                        now[pl.ds(pl.multiple_of(pattern_ref[k, j] * size, size), size), :]
                        for k in range(n_source)
                    ]
                    moved = jnp.dot(
                        weight_ref[j],
                        jnp.concatenate(picked, axis=0),
                        preferred_element_type=jnp.float32,
                    )
                emission = jnp.broadcast_to(emit_col_ref[states, s : s + 1], (size, LANES))
                stay = stay_ref[states, :]
                from_ref = base_ref if s == 0 else cur_ref
                to_ref = base_ref if s == steps - 1 else cur_ref
                if s == steps - 1:
                    if is_first:
                        change = change_col_ref[states, :]
                    else:
                        change = emit_col_ref[states, steps : steps + 1]
                        change = jnp.broadcast_to(change, (size, LANES))
                for h in range(n_half):
                    part = slice(h * LANES, (h + 1) * LANES)
                    kept = from_ref[h, j, first - 1 : padded - 1, :] * stay
                    new = (kept + moved[:, part]) * emission
                    if s == steps - 1:
                        start = base_ref[h, j, first - steps : padded - steps, :]
                        new = new + start * change
                        if not is_first:
                            new = new * scale[:, part]
                        sums[h] = sums[h] + jnp.sum(new.reshape(-1, SUBLANES, LANES), axis=0)
                    store(to_ref, later, j, h, new)
        if steps % 2:
            low_a_ref[...] = low_b_ref[...]
        row_sum = jnp.concatenate([jnp.sum(t, axis=0, keepdims=True) for t in sums], axis=1)
        return 1.0 / row_sum, log_scale + jnp.log(row_sum)

    ones = jnp.ones((1, n_rows), jnp.float32)
    carried = segment(0, (ones, jnp.zeros_like(ones)), is_first=True)
    scale, log_scale = lax.fori_loop(1, n_segments, segment, carried)
    scale = scale * n_states
    n_out = out_sems.shape[0]
    divisor = (n_segments * steps).astype(jnp.float32)
    rate_ref[...] = (log_scale - jnp.log(jnp.full_like(ones, n_states))) / divisor
    out = [pltpu.make_async_copy(rate_ref, rate_hbm, out_sems.at[0])]
    out[0].start()
    n_tiles = n_states // LANES
    per_out = n_half * n_tiles // (n_out - 1)
    for h in range(n_half):
        part = slice(h * LANES, (h + 1) * LANES)
        for j in range(n_tiles):
            block = [base_ref[h, j * per + i, first:, :] for i in range(per)]
            block = jnp.concatenate(block, axis=0) * scale[:, part]
            rows_ref[part, j * LANES : (j + 1) * LANES] = block.T
            if (j + 1) % per_out == 0:
                rows = pl.ds(h * LANES, LANES)
                cols = pl.ds((j + 1 - per_out) * LANES, per_out * LANES)
                sem = out_sems.at[len(out)]
                out.append(
                    pltpu.make_async_copy(rows_ref.at[rows, cols], rows_hbm.at[0, rows, cols], sem)
                )
                out[-1].start()
    for copy in out:
        copy.wait()


def body(observed, pattern, trans_blocks, leave_rate, symbol_emit, cluster_emit, symbol_cluster):
    n_blocks, n_source, size, _ = trans_blocks.shape
    n_states = leave_rate.shape[0]
    steps = observed.shape[0]
    n_rows = n_states // lax.axis_size("rows")
    n_tm = lax.axis_size("tm")
    own = jnp.broadcast_to(observed[None, :], (n_tm, steps))
    all_observed = lax.all_to_all(own, "tm", 0, 0, tiled=True)
    hbm = pl.BlockSpec(memory_space=pltpu.HBM)
    f32, bf16 = jnp.float32, jnp.bfloat16
    return pl.pallas_call(
        chain_kernel,
        out_shape=[
            jax.ShapeDtypeStruct((1, n_rows, n_states), f32),
            jax.ShapeDtypeStruct((1, n_rows), f32),
        ],
        in_specs=[hbm] * 7,
        out_specs=[hbm, hbm],
        scratch_shapes=[
            pltpu.SMEM((n_tm, steps), jnp.int32),
            pltpu.VMEM((1, n_rows), f32),
            pltpu.SMEM((n_source, n_blocks), jnp.int32),
            pltpu.SMEM(symbol_cluster.shape, jnp.int32),
            pltpu.VMEM((1, n_states), f32),
            pltpu.VMEM(trans_blocks.shape, bf16),
            pltpu.VMEM(cluster_emit.shape, f32),
            pltpu.VMEM(symbol_emit.shape, f32),
            pltpu.VMEM((n_rows, n_states), f32),
            pltpu.VMEM((n_states, LANES), f32),
            pltpu.VMEM((n_states, LANES), f32),
            pltpu.VMEM((n_blocks, size, n_source * size), bf16),
            pltpu.VMEM((n_rows // LANES, n_blocks, size + SUBLANES, LANES), f32),
            pltpu.VMEM((n_rows // LANES, n_blocks, size + SUBLANES, LANES), f32),
            pltpu.VMEM((n_states, n_rows), bf16),
            pltpu.VMEM((n_states, n_rows), bf16),
            pltpu.VMEM((LANES, n_states), f32),
            pltpu.VMEM((n_states, LANES), f32),
            pltpu.VMEM((n_states, LANES), f32),
            pltpu.VMEM((n_blocks, n_tm, LANES), f32),
            pltpu.VMEM((steps, n_blocks, n_tm, LANES), f32),
            [pltpu.VMEM((steps - l, n_blocks, n_tm, LANES), f32) for l in range(steps)],
            [
                [pltpu.VMEM((steps - l, n_blocks, n_tm, LANES), f32) for _ in range(LANES // size)]
                for l in range(steps)
            ],
            pltpu.VMEM((n_tm, n_states), f32),
            pltpu.SemaphoreType.DMA((6,)),
            pltpu.SemaphoreType.DMA((4,)),
            pltpu.SemaphoreType.DMA((1 + 2 * n_rows // LANES,)),
        ],
        compiler_params=pltpu.CompilerParams(vmem_limit_bytes=60 << 20),
        cost_estimate=pl.CostEstimate(flops=1 << 34, bytes_accessed=4 << 20, transcendentals=0),
        name="chain",
    )(
        all_observed,
        pattern.T,
        symbol_cluster,
        leave_rate.reshape(1, n_states),
        trans_blocks,
        cluster_emit,
        symbol_emit,
    )


def solution(mesh):
    in_specs = (P("tm"), P(), P(), P(), P(), P(), P())
    out_specs = (P("tm", "rows", None), P("tm", "rows"))
    return jax.shard_map(body, mesh=mesh, in_specs=in_specs, out_specs=out_specs, check_vma=False)
```

```python
import functools

import jax
import jax.numpy as jnp
from jax import lax
from jax.experimental import pallas as pl
from jax.experimental.pallas import tpu as pltpu
from jax.sharding import PartitionSpec as P

LANES = 128
SUBLANES = 8


def column(row):
    return jnp.broadcast_to(row, (LANES, row.shape[1])).T


def twice(tile, at, size):
    other = pltpu.roll(tile, size, 1)
    low_half = lax.broadcasted_iota(jnp.int32, (1, LANES), 1) < size
    return jnp.where(low_half, tile, other) if at == 0 else jnp.where(low_half, other, tile)


def chain_kernel(
    observed_hbm,
    pattern_hbm,
    cluster_hbm,
    leave_hbm,
    blocks_hbm,
    cluster_emit_hbm,
    symbol_hbm,
    rows_hbm,
    rate_hbm,
    observed_ref,
    rate_ref,
    pattern_ref,
    cluster_ref,
    leave_ref,
    blocks_ref,
    cluster_emit_ref,
    symbol_ref,
    rows_ref,
    leave_col_ref,
    stay_ref,
    weight_ref,
    cur_ref,
    base_ref,
    low_a_ref,
    low_b_ref,
    emit_ref,
    emit_col_ref,
    change_col_ref,
    stay_slab_ref,
    emit_slab_ref,
    sum_refs,
    part_refs,
    change_ref,
    sems,
    block_sems,
    out_sems,
):
    n_tm, steps = observed_ref.shape
    n_half, n_blocks, padded, _ = cur_ref.shape
    size = blocks_ref.shape[-1]
    n_states = n_blocks * size
    n_rows = n_half * LANES
    n_source = pattern_ref.shape[0]
    first = padded - size
    n_segments = lax.axis_index("tm") + 1
    row_start = lax.axis_index("rows") * n_rows
    lows = (low_a_ref, low_b_ref)

    small = [
        pltpu.make_async_copy(source, target, sems.at[i])
        for i, (source, target) in enumerate(
            [
                (leave_hbm, leave_ref),
                (pattern_hbm, pattern_ref),
                (observed_hbm, observed_ref),
                (cluster_hbm, cluster_ref),
                (cluster_emit_hbm, cluster_emit_ref),
                (symbol_hbm, symbol_ref),
            ]
        )
    ]
    n_chunks = block_sems.shape[0]
    per_chunk = n_blocks // n_chunks
    chunks = [
        pltpu.make_async_copy(
            blocks_hbm.at[pl.ds(i * per_chunk, per_chunk)],
            blocks_ref.at[pl.ds(i * per_chunk, per_chunk)],
            block_sems.at[i],
        )
        for i in range(n_chunks)
    ]
    for copy in small[:2] + chunks + small[2:]:
        copy.start()

    def store(target_ref, low_ref, j, h, new):
        target_ref[h, j, first:, :] = new
        target_ref[h, j, :first, :] = new[size - first :, :]
        if low_ref is not None:
            rows, part = slice(j * size, (j + 1) * size), slice(h * LANES, (h + 1) * LANES)
            low_ref[rows, part] = new.astype(jnp.bfloat16)

    state = lax.broadcasted_iota(jnp.int32, (size, LANES), 0)
    row = lax.broadcasted_iota(jnp.int32, (size, LANES), 1)
    for j in range(n_blocks):
        for h in range(n_half):
            start = state + j * size == row + (row_start + h * LANES)
            store(base_ref, None, j, h, start.astype(jnp.float32))

    def moved_from_identity(j):
        own = [jnp.zeros((size, LANES), jnp.float32) for _ in range(n_half)]
        lane_block = lax.broadcasted_iota(jnp.int32, (size, LANES), 1) // size + row_start // size
        for k in range(n_source):
            tile = weight_ref[j, :, k // per * LANES : (k // per + 1) * LANES]
            tile = twice(tile.astype(jnp.float32), k % per, size)
            for h in range(n_half):
                here = lane_block + h * per == pattern_ref[k, j]
                own[h] = own[h] + jnp.where(here, tile, 0.0)
        return jnp.concatenate(own, axis=1)
    emit_ref[...] = jnp.zeros_like(emit_ref)
    for refs in part_refs:
        for ref in refs:
            ref[...] = jnp.zeros_like(ref)

    per = LANES // size
    low_half = lax.broadcasted_iota(jnp.int32, (1, LANES), 1) < size

    small[0].wait()
    for j in range(n_blocks):
        tile = leave_ref[:, j // per * LANES : (j // per + 1) * LANES]
        tile = jnp.broadcast_to(1.0 - tile, (n_tm, LANES))
        stay_slab_ref[j] = twice(tile, j % per, size)
    leave_col = column(leave_ref[...])
    leave_col_ref[...] = leave_col
    for j in range(n_blocks):
        own = leave_col[j * size : (j + 1) * size]
        stay_ref[j * size : (j + 1) * size, :] = 1.0 - pltpu.roll(own, 1, 0)
    small[1].wait()
    for j in range(n_blocks):
        if j % per_chunk == 0:
            chunks[j // per_chunk].wait()
        parts = []
        for k in range(n_source):
            rows = pl.ds(pl.multiple_of(pattern_ref[k, j] * size, size), size)
            parts.append(blocks_ref[j, k].astype(jnp.float32) * leave_col_ref[rows, :size])
        weight_ref[j] = jnp.concatenate(parts, axis=0).T.astype(jnp.bfloat16)
    for copy in small[2:]:
        copy.wait()

    def emission_of(g, s):
        symbol = observed_ref[g, s]
        row = symbol_ref[pl.ds(symbol, 1), :]
        return row * cluster_emit_ref[pl.ds(cluster_ref[symbol], 1), :]

    def find_changes():
        rows = n_blocks * n_tm
        stays = stay_slab_ref[...].reshape(rows, LANES)
        for s in range(steps):
            emission = jnp.concatenate([emission_of(g, s) for g in range(n_tm)], axis=0)
            for j in range(n_blocks):
                tile = emission[:, j // per * LANES : (j // per + 1) * LANES]
                emit_slab_ref[s, j] = twice(tile, j % per, size)
        yield

        def row_sums(l, p):
            return sum_refs[l][p].reshape(rows, LANES)

        for l in range(steps):
            n_pos = steps - l
            images = []
            for p in range(n_pos):
                image = emit_slab_ref[p].reshape(rows, LANES)
                if l:
                    image = image * row_sums(l - 1, p + 1)
                images.append(image)
            for j in range(n_blocks):
                own = [image[j * n_tm : (j + 1) * n_tm] for image in images]
                own = jnp.concatenate(own, axis=0)[:, :size].astype(jnp.bfloat16)
                moved = jnp.dot(own, weight_ref[j], preferred_element_type=jnp.float32)
                for k in range(n_source):
                    tile = moved[:, k // per * LANES : (k // per + 1) * LANES]
                    tile = tile.reshape(n_pos, n_tm, LANES)
                    ref = part_refs[l][k % per]
                    source = pattern_ref[k, j]
                    for p in range(n_pos):
                        ref[p, source] = ref[p, source] + tile[p]
                yield
            for p in range(n_pos):
                sides = [ref[p].reshape(rows, LANES) for ref in part_refs[l]]
                total = jnp.where(low_half, sides[0], sides[1])
                total = total + pltpu.roll(total, size, 1)
                total = total + stays * pltpu.roll(images[p], LANES - 1, 1)
                sum_refs[l][p] = total.reshape(n_blocks, n_tm, LANES)
            yield

        exact = jnp.ones((rows, LANES), jnp.float32)
        weight = exact
        deviation = []
        for s in range(steps):
            row_sum = pltpu.roll(row_sums(s, 0), 1, 1)
            for q in range(s):
                row_sum = row_sum + deviation[q] * row_sums(s - q - 1, q + 1)
                row_sum = pltpu.roll(row_sum, 1, 1)
            emission = emit_slab_ref[s].reshape(rows, LANES)
            exact = pltpu.roll(exact * stays, 1, 1) * emission
            weight = pltpu.roll(weight * stays, 1, 1) * emission
            rounded = (weight * (n_states / row_sum)).astype(jnp.bfloat16).astype(jnp.float32)
            rounded = rounded * (row_sum * (1.0 / n_states))
            deviation.append(rounded - weight)
            weight = rounded
            yield
        change = (weight - exact).reshape(n_blocks, n_tm, LANES)
        for m in range(n_states // LANES):
            tile = change[m * per + per - 1]
            for i in range(per - 1):
                tile = jnp.where(low_half, change[m * per + i], tile)
            change_ref[:, m * LANES : (m + 1) * LANES] = tile

    def segment(g, carried, is_first=False):
        scale, log_scale = carried
        for s in range(steps):
            emit_ref[s : s + 1, :] = emission_of(g, s)
        if not is_first:
            emit_ref[steps : steps + 1, :] = change_ref[pl.ds(g, 1), :]
        emit_col_ref[...] = emit_ref[...].T
        beside = find_changes() if is_first else iter(())
        sums = [jnp.zeros((SUBLANES, LANES), jnp.float32) for _ in range(n_half)]
        for s in range(steps):
            now, later = lows[s % 2], lows[(s + 1) % 2]
            if is_first and s == steps - 1:
                for _ in beside:
                    pass
                change_col_ref[...] = column(change_ref[:1, :])
            for j in range(n_blocks):
                for _ in range(2):
                    next(beside, None)
                states = slice(j * size, (j + 1) * size)
                if is_first and s == 0:
                    moved = moved_from_identity(j)
                else:
                    picked = [
                        now[pl.ds(pl.multiple_of(pattern_ref[k, j] * size, size), size), :]
                        for k in range(n_source)
                    ]
                    moved = jnp.dot(
                        weight_ref[j],
                        jnp.concatenate(picked, axis=0),
                        preferred_element_type=jnp.float32,
                    )
                emission = jnp.broadcast_to(emit_col_ref[states, s : s + 1], (size, LANES))
                stay = stay_ref[states, :]
                from_ref = base_ref if s == 0 else cur_ref
                to_ref = base_ref if s == steps - 1 else cur_ref
                if s == steps - 1:
                    if is_first:
                        change = change_col_ref[states, :]
                    else:
                        change = emit_col_ref[states, steps : steps + 1]
                        change = jnp.broadcast_to(change, (size, LANES))
                for h in range(n_half):
                    part = slice(h * LANES, (h + 1) * LANES)
                    kept = from_ref[h, j, first - 1 : padded - 1, :] * stay
                    new = (kept + moved[:, part]) * emission
                    if s == steps - 1:
                        start = base_ref[h, j, first - steps : padded - steps, :]
                        new = new + start * change
                        if not is_first:
                            new = new * scale[:, part]
                        sums[h] = sums[h] + jnp.sum(new.reshape(-1, SUBLANES, LANES), axis=0)
                    store(to_ref, later, j, h, new)
        if steps % 2:
            low_a_ref[...] = low_b_ref[...]
        row_sum = jnp.concatenate([jnp.sum(t, axis=0, keepdims=True) for t in sums], axis=1)
        return 1.0 / row_sum, log_scale + jnp.log(row_sum)

    ones = jnp.ones((1, n_rows), jnp.float32)
    carried = segment(0, (ones, jnp.zeros_like(ones)), is_first=True)
    scale, log_scale = lax.fori_loop(1, n_segments, segment, carried)
    scale = scale * n_states
    n_out = out_sems.shape[0]
    divisor = (n_segments * steps).astype(jnp.float32)
    rate_ref[...] = (log_scale - jnp.log(jnp.full_like(ones, n_states))) / divisor
    out = [pltpu.make_async_copy(rate_ref, rate_hbm, out_sems.at[0])]
    out[0].start()
    n_tiles = n_states // LANES
    per_out = n_half * n_tiles // (n_out - 1)
    for h in range(n_half):
        part = slice(h * LANES, (h + 1) * LANES)
        for j in range(n_tiles):
            block = [base_ref[h, j * per + i, first:, :] for i in range(per)]
            block = jnp.concatenate(block, axis=0) * scale[:, part]
            rows_ref[part, j * LANES : (j + 1) * LANES] = block.T
            if (j + 1) % per_out == 0:
                rows = pl.ds(h * LANES, LANES)
                cols = pl.ds((j + 1 - per_out) * LANES, per_out * LANES)
                sem = out_sems.at[len(out)]
                out.append(
                    pltpu.make_async_copy(rows_ref.at[rows, cols], rows_hbm.at[0, rows, cols], sem)
                )
                out[-1].start()
    for copy in out:
        copy.wait()


def body(observed, pattern, trans_blocks, leave_rate, symbol_emit, cluster_emit, symbol_cluster):
    n_blocks, n_source, size, _ = trans_blocks.shape
    n_states = leave_rate.shape[0]
    steps = observed.shape[0]
    n_rows = n_states // lax.axis_size("rows")
    n_tm = lax.axis_size("tm")
    own = jnp.broadcast_to(observed[None, :], (n_tm, steps))
    all_observed = lax.all_to_all(own, "tm", 0, 0, tiled=True)
    hbm = pl.BlockSpec(memory_space=pltpu.HBM)
    f32, bf16 = jnp.float32, jnp.bfloat16
    return pl.pallas_call(
        chain_kernel,
        out_shape=[
            jax.ShapeDtypeStruct((1, n_rows, n_states), f32),
            jax.ShapeDtypeStruct((1, n_rows), f32),
        ],
        in_specs=[hbm] * 7,
        out_specs=[hbm, hbm],
        scratch_shapes=[
            pltpu.SMEM((n_tm, steps), jnp.int32),
            pltpu.VMEM((1, n_rows), f32),
            pltpu.SMEM((n_source, n_blocks), jnp.int32),
            pltpu.SMEM(symbol_cluster.shape, jnp.int32),
            pltpu.VMEM((1, n_states), f32),
            pltpu.VMEM(trans_blocks.shape, bf16),
            pltpu.VMEM(cluster_emit.shape, f32),
            pltpu.VMEM(symbol_emit.shape, f32),
            pltpu.VMEM((n_rows, n_states), f32),
            pltpu.VMEM((n_states, LANES), f32),
            pltpu.VMEM((n_states, LANES), f32),
            pltpu.VMEM((n_blocks, size, n_source * size), bf16),
            pltpu.VMEM((n_rows // LANES, n_blocks, size + SUBLANES, LANES), f32),
            pltpu.VMEM((n_rows // LANES, n_blocks, size + SUBLANES, LANES), f32),
            pltpu.VMEM((n_states, n_rows), bf16),
            pltpu.VMEM((n_states, n_rows), bf16),
            pltpu.VMEM((LANES, n_states), f32),
            pltpu.VMEM((n_states, LANES), f32),
            pltpu.VMEM((n_states, LANES), f32),
            pltpu.VMEM((n_blocks, n_tm, LANES), f32),
            pltpu.VMEM((steps, n_blocks, n_tm, LANES), f32),
            [pltpu.VMEM((steps - l, n_blocks, n_tm, LANES), f32) for l in range(steps)],
            [
                [pltpu.VMEM((steps - l, n_blocks, n_tm, LANES), f32) for _ in range(LANES // size)]
                for l in range(steps)
            ],
            pltpu.VMEM((n_tm, n_states), f32),
            pltpu.SemaphoreType.DMA((6,)),
            pltpu.SemaphoreType.DMA((4,)),
            pltpu.SemaphoreType.DMA((1 + 2 * n_rows // LANES,)),
        ],
        compiler_params=pltpu.CompilerParams(vmem_limit_bytes=60 << 20),
        cost_estimate=pl.CostEstimate(flops=1 << 34, bytes_accessed=4 << 20, transcendentals=0),
        name="chain",
    )(
        all_observed,
        pattern.T,
        symbol_cluster,
        leave_rate.reshape(1, n_states),
        trans_blocks,
        cluster_emit,
        symbol_emit,
    )


def solution(mesh):
    in_specs = (P("tm"), P(), P(), P(), P(), P(), P())
    out_specs = (P("tm", "rows", None), P("tm", "rows"))
    return jax.shard_map(body, mesh=mesh, in_specs=in_specs, out_specs=out_specs, check_vma=False)
```

```python
import functools

import jax
import jax.numpy as jnp
from jax import lax
from jax.experimental import pallas as pl
from jax.experimental.pallas import tpu as pltpu
from jax.sharding import PartitionSpec as P

LANES = 128
SUBLANES = 8


def column(row):
    return jnp.broadcast_to(row, (LANES, row.shape[1])).T


def twice(tile, at, size):
    other = pltpu.roll(tile, size, 1)
    low_half = lax.broadcasted_iota(jnp.int32, (1, LANES), 1) < size
    return jnp.where(low_half, tile, other) if at == 0 else jnp.where(low_half, other, tile)


def chain_kernel(
    observed_hbm,
    pattern_hbm,
    cluster_hbm,
    leave_hbm,
    blocks_hbm,
    cluster_emit_hbm,
    symbol_hbm,
    rows_hbm,
    rate_hbm,
    observed_ref,
    rate_ref,
    pattern_ref,
    cluster_ref,
    leave_ref,
    blocks_ref,
    cluster_emit_ref,
    symbol_ref,
    rows_ref,
    leave_col_ref,
    stay_ref,
    weight_ref,
    cur_ref,
    base_ref,
    low_a_ref,
    low_b_ref,
    emit_ref,
    emit_col_ref,
    change_col_ref,
    stay_slab_ref,
    emit_slab_ref,
    sum_refs,
    part_refs,
    change_ref,
    sems,
    block_sems,
    out_sems,
):
    n_tm, steps = observed_ref.shape
    n_half, n_blocks, padded, _ = cur_ref.shape
    size = blocks_ref.shape[-1]
    n_states = n_blocks * size
    n_rows = n_half * LANES
    n_source = pattern_ref.shape[0]
    first = padded - size
    n_segments = lax.axis_index("tm") + 1
    row_start = lax.axis_index("rows") * n_rows
    lows = (low_a_ref, low_b_ref)

    small = [
        pltpu.make_async_copy(source, target, sems.at[i])
        for i, (source, target) in enumerate(
            [
                (leave_hbm, leave_ref),
                (pattern_hbm, pattern_ref),
                (observed_hbm, observed_ref),
                (cluster_hbm, cluster_ref),
                (cluster_emit_hbm, cluster_emit_ref),
                (symbol_hbm, symbol_ref),
            ]
        )
    ]
    n_chunks = block_sems.shape[0]
    per_chunk = n_blocks // n_chunks
    chunks = [
        pltpu.make_async_copy(
            blocks_hbm.at[pl.ds(i * per_chunk, per_chunk)],
            blocks_ref.at[pl.ds(i * per_chunk, per_chunk)],
            block_sems.at[i],
        )
        for i in range(n_chunks)
    ]
    for copy in small[:2] + chunks + small[2:]:
        copy.start()

    def store(target_ref, low_ref, j, h, new):
        target_ref[h, j, first:, :] = new
        target_ref[h, j, :first, :] = new[size - first :, :]
        if low_ref is not None:
            rows, part = slice(j * size, (j + 1) * size), slice(h * LANES, (h + 1) * LANES)
            low_ref[rows, part] = new.astype(jnp.bfloat16)

    state = lax.broadcasted_iota(jnp.int32, (size, LANES), 0)
    row = lax.broadcasted_iota(jnp.int32, (size, LANES), 1)
    for j in range(n_blocks):
        for h in range(n_half):
            start = state + j * size == row + (row_start + h * LANES)
            store(base_ref, None, j, h, start.astype(jnp.float32))

    def moved_from_identity(j):
        own = [jnp.zeros((size, LANES), jnp.float32) for _ in range(n_half)]
        lane_block = lax.broadcasted_iota(jnp.int32, (size, LANES), 1) // size + row_start // size
        for k in range(n_source):
            tile = weight_ref[j, :, k // per * LANES : (k // per + 1) * LANES]
            tile = twice(tile.astype(jnp.float32), k % per, size)
            for h in range(n_half):
                here = lane_block + h * per == pattern_ref[k, j]
                own[h] = own[h] + jnp.where(here, tile, 0.0)
        return jnp.concatenate(own, axis=1)
    emit_ref[...] = jnp.zeros_like(emit_ref)
    for refs in part_refs:
        for ref in refs:
            ref[...] = jnp.zeros_like(ref)

    per = LANES // size
    low_half = lax.broadcasted_iota(jnp.int32, (1, LANES), 1) < size

    small[0].wait()
    for j in range(n_blocks):
        tile = leave_ref[:, j // per * LANES : (j // per + 1) * LANES]
        tile = jnp.broadcast_to(1.0 - tile, (n_tm, LANES))
        stay_slab_ref[j] = twice(tile, j % per, size)
    leave_col = column(leave_ref[...])
    leave_col_ref[...] = leave_col
    for j in range(n_blocks):
        own = leave_col[j * size : (j + 1) * size]
        stay_ref[j * size : (j + 1) * size, :] = 1.0 - pltpu.roll(own, 1, 0)
    small[1].wait()
    for j in range(n_blocks):
        if j % per_chunk == 0:
            chunks[j // per_chunk].wait()
        parts = []
        for k in range(n_source):
            rows = pl.ds(pl.multiple_of(pattern_ref[k, j] * size, size), size)
            parts.append(blocks_ref[j, k].astype(jnp.float32) * leave_col_ref[rows, :size])
        weight_ref[j] = jnp.concatenate(parts, axis=0).T.astype(jnp.bfloat16)
    for copy in small[2:]:
        copy.wait()

    def emission_of(g, s):
        symbol = observed_ref[g, s]
        row = symbol_ref[pl.ds(symbol, 1), :]
        return row * cluster_emit_ref[pl.ds(cluster_ref[symbol], 1), :]

    def find_changes():
        rows = n_blocks * n_tm
        stays = stay_slab_ref[...].reshape(rows, LANES)
        for s in range(steps):
            emission = jnp.concatenate([emission_of(g, s) for g in range(n_tm)], axis=0)
            for j in range(n_blocks):
                tile = emission[:, j // per * LANES : (j // per + 1) * LANES]
                emit_slab_ref[s, j] = twice(tile, j % per, size)

        def row_sums(l, p):
            return sum_refs[l][p].reshape(rows, LANES)

        for l in range(steps):
            n_pos = steps - l
            images = []
            for p in range(n_pos):
                image = emit_slab_ref[p].reshape(rows, LANES)
                if l:
                    image = image * row_sums(l - 1, p + 1)
                images.append(image)
            for j in range(n_blocks):
                own = [image[j * n_tm : (j + 1) * n_tm] for image in images]
                own = jnp.concatenate(own, axis=0)[:, :size].astype(jnp.bfloat16)
                moved = jnp.dot(own, weight_ref[j], preferred_element_type=jnp.float32)
                for k in range(n_source):
                    tile = moved[:, k // per * LANES : (k // per + 1) * LANES]
                    tile = tile.reshape(n_pos, n_tm, LANES)
                    ref = part_refs[l][k % per]
                    source = pattern_ref[k, j]
                    for p in range(n_pos):
                        ref[p, source] = ref[p, source] + tile[p]
            for p in range(n_pos):
                sides = [ref[p].reshape(rows, LANES) for ref in part_refs[l]]
                total = jnp.where(low_half, sides[0], sides[1])
                total = total + pltpu.roll(total, size, 1)
                total = total + stays * pltpu.roll(images[p], LANES - 1, 1)
                sum_refs[l][p] = total.reshape(n_blocks, n_tm, LANES)

        exact = jnp.ones((rows, LANES), jnp.float32)
        weight = exact
        deviation = []
        for s in range(steps):
            row_sum = pltpu.roll(row_sums(s, 0), 1, 1)
            for q in range(s):
                row_sum = row_sum + deviation[q] * row_sums(s - q - 1, q + 1)
                row_sum = pltpu.roll(row_sum, 1, 1)
            emission = emit_slab_ref[s].reshape(rows, LANES)
            exact = pltpu.roll(exact * stays, 1, 1) * emission
            weight = pltpu.roll(weight * stays, 1, 1) * emission
            rounded = (weight * (n_states / row_sum)).astype(jnp.bfloat16).astype(jnp.float32)
            rounded = rounded * (row_sum * (1.0 / n_states))
            deviation.append(rounded - weight)
            weight = rounded
        change = (weight - exact).reshape(n_blocks, n_tm, LANES)
        for m in range(n_states // LANES):
            tile = change[m * per + per - 1]
            for i in range(per - 1):
                tile = jnp.where(low_half, change[m * per + i], tile)
            change_ref[:, m * LANES : (m + 1) * LANES] = tile

    def segment(g, carried, is_first=False):
        scale, log_scale = carried
        for s in range(steps):
            emit_ref[s : s + 1, :] = emission_of(g, s)
        if not is_first:
            emit_ref[steps : steps + 1, :] = change_ref[pl.ds(g, 1), :]
        emit_col_ref[...] = emit_ref[...].T
        if is_first:
            find_changes()
            change_col_ref[...] = column(change_ref[:1, :])
        sums = [jnp.zeros((SUBLANES, LANES), jnp.float32) for _ in range(n_half)]
        for s in range(steps):
            now, later = lows[s % 2], lows[(s + 1) % 2]
            for j in range(n_blocks):
                states = slice(j * size, (j + 1) * size)
                if is_first and s == 0:
                    moved = moved_from_identity(j)
                else:
                    picked = [
                        now[pl.ds(pl.multiple_of(pattern_ref[k, j] * size, size), size), :]
                        for k in range(n_source)
                    ]
                    moved = jnp.dot(
                        weight_ref[j],
                        jnp.concatenate(picked, axis=0),
                        preferred_element_type=jnp.float32,
                    )
                emission = jnp.broadcast_to(emit_col_ref[states, s : s + 1], (size, LANES))
                stay = stay_ref[states, :]
                from_ref = base_ref if s == 0 else cur_ref
                to_ref = base_ref if s == steps - 1 else cur_ref
                if s == steps - 1:
                    if is_first:
                        change = change_col_ref[states, :]
                    else:
                        change = emit_col_ref[states, steps : steps + 1]
                        change = jnp.broadcast_to(change, (size, LANES))
                for h in range(n_half):
                    part = slice(h * LANES, (h + 1) * LANES)
                    kept = from_ref[h, j, first - 1 : padded - 1, :] * stay
                    new = (kept + moved[:, part]) * emission
                    if s == steps - 1:
                        start = base_ref[h, j, first - steps : padded - steps, :]
                        new = new + start * change
                        if not is_first:
                            new = new * scale[:, part]
                        sums[h] = sums[h] + jnp.sum(new.reshape(-1, SUBLANES, LANES), axis=0)
                    store(to_ref, later, j, h, new)
        if steps % 2:
            low_a_ref[...] = low_b_ref[...]
        row_sum = jnp.concatenate([jnp.sum(t, axis=0, keepdims=True) for t in sums], axis=1)
        return 1.0 / row_sum, log_scale + jnp.log(row_sum)

    ones = jnp.ones((1, n_rows), jnp.float32)
    carried = segment(0, (ones, jnp.zeros_like(ones)), is_first=True)
    scale, log_scale = lax.fori_loop(1, n_segments, segment, carried)
    scale = scale * n_states
    n_out = out_sems.shape[0]
    divisor = (n_segments * steps).astype(jnp.float32)
    rate_ref[...] = (log_scale - jnp.log(jnp.full_like(ones, n_states))) / divisor
    out = [pltpu.make_async_copy(rate_ref, rate_hbm, out_sems.at[0])]
    out[0].start()
    n_tiles = n_states // LANES
    per_out = n_half * n_tiles // (n_out - 1)
    for h in range(n_half):
        part = slice(h * LANES, (h + 1) * LANES)
        for j in range(n_tiles):
            block = [base_ref[h, j * per + i, first:, :] for i in range(per)]
            block = jnp.concatenate(block, axis=0) * scale[:, part]
            rows_ref[part, j * LANES : (j + 1) * LANES] = block.T
            if (j + 1) % per_out == 0:
                rows = pl.ds(h * LANES, LANES)
                cols = pl.ds((j + 1 - per_out) * LANES, per_out * LANES)
                sem = out_sems.at[len(out)]
                out.append(
                    pltpu.make_async_copy(rows_ref.at[rows, cols], rows_hbm.at[0, rows, cols], sem)
                )
                out[-1].start()
    for copy in out:
        copy.wait()


def body(observed, pattern, trans_blocks, leave_rate, symbol_emit, cluster_emit, symbol_cluster):
    n_blocks, n_source, size, _ = trans_blocks.shape
    n_states = leave_rate.shape[0]
    steps = observed.shape[0]
    n_rows = n_states // lax.axis_size("rows")
    n_tm = lax.axis_size("tm")
    own = jnp.broadcast_to(observed[None, :], (n_tm, steps))
    all_observed = lax.all_to_all(own, "tm", 0, 0, tiled=True)
    hbm = pl.BlockSpec(memory_space=pltpu.HBM)
    f32, bf16 = jnp.float32, jnp.bfloat16
    return pl.pallas_call(
        chain_kernel,
        out_shape=[
            jax.ShapeDtypeStruct((1, n_rows, n_states), f32),
            jax.ShapeDtypeStruct((1, n_rows), f32),
        ],
        in_specs=[hbm] * 7,
        out_specs=[hbm, hbm],
        scratch_shapes=[
            pltpu.SMEM((n_tm, steps), jnp.int32),
            pltpu.VMEM((1, n_rows), f32),
            pltpu.SMEM((n_source, n_blocks), jnp.int32),
            pltpu.SMEM(symbol_cluster.shape, jnp.int32),
            pltpu.VMEM((1, n_states), f32),
            pltpu.VMEM(trans_blocks.shape, bf16),
            pltpu.VMEM(cluster_emit.shape, f32),
            pltpu.VMEM(symbol_emit.shape, f32),
            pltpu.VMEM((n_rows, n_states), f32),
            pltpu.VMEM((n_states, LANES), f32),
            pltpu.VMEM((n_states, LANES), f32),
            pltpu.VMEM((n_blocks, size, n_source * size), bf16),
            pltpu.VMEM((n_rows // LANES, n_blocks, size + SUBLANES, LANES), f32),
            pltpu.VMEM((n_rows // LANES, n_blocks, size + SUBLANES, LANES), f32),
            pltpu.VMEM((n_states, n_rows), bf16),
            pltpu.VMEM((n_states, n_rows), bf16),
            pltpu.VMEM((LANES, n_states), f32),
            pltpu.VMEM((n_states, LANES), f32),
            pltpu.VMEM((n_states, LANES), f32),
            pltpu.VMEM((n_blocks, n_tm, LANES), f32),
            pltpu.VMEM((steps, n_blocks, n_tm, LANES), f32),
            [pltpu.VMEM((steps - l, n_blocks, n_tm, LANES), f32) for l in range(steps)],
            [
                [pltpu.VMEM((steps - l, n_blocks, n_tm, LANES), f32) for _ in range(LANES // size)]
                for l in range(steps)
            ],
            pltpu.VMEM((n_tm, n_states), f32),
            pltpu.SemaphoreType.DMA((6,)),
            pltpu.SemaphoreType.DMA((n_blocks,)),
            pltpu.SemaphoreType.DMA((1 + 4 * n_rows // LANES,)),
        ],
        compiler_params=pltpu.CompilerParams(vmem_limit_bytes=60 << 20),
        cost_estimate=pl.CostEstimate(flops=1 << 34, bytes_accessed=4 << 20, transcendentals=0),
        name="chain",
    )(
        all_observed,
        pattern.T,
        symbol_cluster,
        leave_rate.reshape(1, n_states),
        trans_blocks,
        cluster_emit,
        symbol_emit,
    )


def solution(mesh):
    in_specs = (P("tm"), P(), P(), P(), P(), P(), P())
    out_specs = (P("tm", "rows", None), P("tm", "rows"))
    return jax.shard_map(body, mesh=mesh, in_specs=in_specs, out_specs=out_specs, check_vma=False)
```
